32 devices in a mesh: clip: 8 (over z, x), frame: 4 (over y, core).
Axes of the slice: x: 2, y: 2, z: 4, core: 2. Of those that a mesh axis runs over, the one named last changes fastest.
Arguments:
- clips_in: bfloat16 [32, 16, 196, 768], P('clip', 'frame'), may hold values from -6 to 6
- teacher: bfloat16 [32, 16, 196, 768], P('clip', 'frame'), may hold values from -6 to 6
- valid: int32 [32, 16, 196], P('clip', 'frame'), may hold values from 0 to 1, as said below
- norm_gain: bfloat16 [768, 3], P(('clip', 'frame')), may hold values from 0.5 to 1.5
- norm_shift: bfloat16 [768, 3], P(('clip', 'frame')), may hold values from -1.796875 to 1.796875
- w_space: bfloat16 [768, 2304], P(('clip', 'frame')), may hold values from -0.21875 to 0.21875
- qv_bias: bfloat16 [768, 4], P(('clip', 'frame')), may hold values from -1.796875 to 1.796875
- w_space_out: bfloat16 [768, 768], P(('clip', 'frame')), may hold values from -1.75 to 1.75
- mix_bias: bfloat16 [768, 3], P(('clip', 'frame')), may hold values from -1.796875 to 1.796875
- w_time: bfloat16 [768, 2304], P(('clip', 'frame')), may hold values from -0.21875 to 0.21875
- w_time_out: bfloat16 [768, 768], P(('clip', 'frame')), may hold values from -0.875 to 0.875
- w_up: bfloat16 [768, 3072], P(('clip', 'frame')), may hold values from -0.21875 to 0.21875
- up_bias: bfloat16 [3072], P(('clip', 'frame')), may hold values from -3 to 3
- w_down: bfloat16 [3072, 768], P(('clip', 'frame')), may hold values from -0.109375 to 0.109375
Outputs:
- layer_out: bfloat16 [32, 16, 196, 768], P('clip', 'frame')
- loss_value: float32 [], replicated
- input_grad: bfloat16 [32, 16, 196, 768], P('clip', 'frame')
- gain_grad: float32 [768, 3], P(('clip', 'frame'))
- shift_grad: float32 [768, 3], P(('clip', 'frame'))
- w_space_grad: float32 [768, 2304], P(('clip', 'frame'))
- qv_bias_grad: float32 [768, 3], P(('clip', 'frame'))
- time_query_bias_grad: float32 [768], P(('clip', 'frame'))
- w_space_out_grad: float32 [768, 768], P(('clip', 'frame'))
- mix_bias_grad: float32 [768, 3], P(('clip', 'frame'))
- w_time_grad: float32 [768, 2304], P(('clip', 'frame'))
- w_time_out_grad: float32 [768, 768], P(('clip', 'frame'))
- w_up_grad: float32 [768, 3072], P(('clip', 'frame'))
- up_bias_grad: float32 [3072], P(('clip', 'frame'))
- w_down_grad: float32 [3072, 768], P(('clip', 'frame'))
The draws below stay inside these ranges and needn't reach their ends.
Inputs may be any that keep to these rules, and one draw needn't show every extreme that they name: The first place of the first frame of every clip is valid.
All inputs are finite; a program needn't handle non-finite values.
Results may differ from the reference program's by a relative error of at most 0.009.
Values may be sent and summed in bfloat16 or wider, within the bound.
A program may use at most 640 MiB of HBM per device.

```python
import jax
import jax.numpy as jnp
from jax import lax

D = 768
HEADS = 12
HEAD = 64
FF = 3072
FRAMES = 16
PLACES = 196
CLIPS = 32


def draw_valid(key, part):
    key = jax.random.fold_in(key, 11)
    shape = (CLIPS, FRAMES, PLACES)
    rolls = jax.random.randint(key, shape, 0, 1000)
    clip_place = lax.broadcasted_iota(jnp.int32, shape, 0)
    frame_place = lax.broadcasted_iota(jnp.int32, shape, 1)
    token_place = lax.broadcasted_iota(jnp.int32, shape, 2)
    level = 250 + 500 * clip_place // max(CLIPS - 1, 1)
    first = (frame_place == 0) & (token_place == 0)
    return jnp.where(first | (rolls < level), 1, 0).astype(jnp.int32)


def levels(rng, shape, shards, low, high):
    def one(position, parts):
        steps = jax.random.uniform(jax.random.fold_in(jax.random.fold_in(rng, 6), position), (parts,), jnp.float32, low / len(shards), high / len(shards))
        return jnp.repeat(jnp.exp(steps), shape[position] // parts).reshape((-1,) + (1,) * (len(shape) - position - 1))

    level = one(*shards[0])
    for cut in shards[1:]:
        level = level * one(*cut)
    return level


def gaussian(rng, extent, spread, reach, pieces=(), kind=jnp.bfloat16):
    entries = jax.random.normal(rng, extent, jnp.float32) * spread
    if len(pieces) > 0:
        entries = levels(rng, extent, pieces, -0.22, 0.18) * entries
    return jnp.clip(entries, min=-reach, max=reach).astype(kind)


def setup_inputs(seed: int = 0) -> dict:
    key_of = jax.random.split(jax.random.key(seed), 15)
    clips_in = gaussian(key_of[0], (CLIPS, FRAMES, PLACES, D), 1.0, 6.0, ((0, 8), (1, 4)))
    teacher = gaussian(key_of[1], (CLIPS, FRAMES, PLACES, D), 1.0, 6.0, ((0, 8), (1, 4)))
    valid = draw_valid(jax.random.fold_in(key_of[14], 71), 0)
    norm_gain = jnp.clip(1.0 + 0.1 * jax.random.normal(key_of[3], (D, 3), jnp.float32), 0.5, 1.5).astype(jnp.bfloat16)
    norm_shift = gaussian(key_of[4], (D, 3), 0.3, 1.796875, ((0, 32),))
    w_space = gaussian(key_of[5], (D, 3 * D), D ** -0.5, 0.21875, ((0, 32),))
    qv_bias = gaussian(key_of[6], (D, 4), 0.3, 1.796875, ((0, 32),))
    w_space_out = gaussian(key_of[7], (D, D), (D // 64) ** -0.5, 1.75, ((0, 32),))
    mix_bias = gaussian(key_of[8], (D, 3), 0.3, 1.796875, ((0, 32),))
    w_time = gaussian(key_of[9], (D, 3 * D), D ** -0.5, 0.21875, ((0, 32),))
    w_time_out = gaussian(key_of[10], (D, D), (D // 16) ** -0.5, 0.875, ((0, 32),))
    w_up = gaussian(key_of[11], (D, FF), D ** -0.5, 0.21875, ((0, 32),))
    up_bias = gaussian(key_of[12], (FF,), 0.5, 3.0, ((0, 32),))
    w_down = gaussian(key_of[13], (FF, D), FF ** -0.5, 0.109375, ((0, 32),))
    return {"clips_in": clips_in, "teacher": teacher, "valid": valid, "norm_gain": norm_gain, "norm_shift": norm_shift, "w_space": w_space, "qv_bias": qv_bias, "w_space_out": w_space_out, "mix_bias": mix_bias, "w_time": w_time, "w_time_out": w_time_out, "w_up": w_up, "up_bias": up_bias, "w_down": w_down}


EPS = 1e-06

@jax.custom_vjp
def low(v):
    return lax.optimization_barrier(v.astype(jnp.bfloat16)).astype(jnp.float32)

@jax.custom_vjp
def low_back(v):
    return v

def low_keep(v):
    return (low(v), None)

def low_pass(kept, grad):
    return (grad,)

def back_keep(v):
    return (v, None)

def back_low(kept, grad):
    return (low(grad),)
low.defvjp(low_keep, low_pass)
low_back.defvjp(back_keep, back_low)

def mm_high(left, right):
    return jnp.dot(left, right, precision=lax.Precision.HIGHEST)

def einsum_high(form, left, right):
    return jnp.einsum(form, left, right, precision=lax.Precision.HIGHEST)

def both_round(value):
    return low(low_back(value))

def norm_rows(inputs, gain, shift):
    center = inputs - lax.optimization_barrier(jnp.mean(inputs, -1, keepdims=True))
    inverse = lax.rsqrt(lax.optimization_barrier(jnp.mean(center * center, -1, keepdims=True)) + EPS)
    return center * inverse * gain + shift

def softmax_last(scores):
    top = lax.optimization_barrier(jnp.max(scores, -1, keepdims=True))
    expo = jnp.exp(scores - top)
    return expo / lax.optimization_barrier(jnp.sum(expo, -1, keepdims=True))

def layer(params, clip):
    gain, shift, w_space, qv_bias, w_space_out, mix_bias, w_time, w_time_out, w_up, up_bias, w_down = params
    frames, places, width = clip.shape
    rows = clip.reshape(-1, width)
    factor = HEAD ** (-0.5)
    heads = (frames, places, HEADS, HEAD)
    in_a = low(norm_rows(rows, gain[:, 0], shift[:, 0]))
    proj_a = mm_high(in_a, w_space)
    q_a = both_round(proj_a[:, :width] + qv_bias[:, 0])
    k_a = both_round(proj_a[:, width:2 * width])
    v_a = both_round(proj_a[:, 2 * width:] + qv_bias[:, 1])
    scores_a = low_back(einsum_high('fphe,fqhe->fhpq', q_a.reshape(heads), k_a.reshape(heads)) * factor)
    probs_a = low(softmax_last(scores_a))
    mix_a = both_round(einsum_high('fhpq,fqhe->fphe', probs_a, v_a.reshape(heads)).reshape(-1, width))
    after_a = rows + low_back(mm_high(mix_a, w_space_out) + mix_bias[:, 0])
    in_b = low(norm_rows(after_a, gain[:, 1], shift[:, 1]))
    proj_b = mm_high(in_b, w_time)
    q_b = both_round(proj_b[:, :width] + qv_bias[:, 2])
    k_b = both_round(proj_b[:, width:2 * width])
    v_b = both_round(proj_b[:, 2 * width:] + qv_bias[:, 3])
    scores_b = low_back(einsum_high('fphe,tphe->phft', q_b.reshape(heads), k_b.reshape(heads)) * factor)
    probs_b = low(softmax_last(scores_b))
    mix_b = both_round(einsum_high('phft,tphe->fphe', probs_b, v_b.reshape(heads)).reshape(-1, width))
    after_b = after_a + low_back(mm_high(mix_b, w_time_out) + mix_bias[:, 1])
    in_c = low(norm_rows(after_b, gain[:, 2], shift[:, 2]))
    pre_act = low_back(mm_high(in_c, w_up) + up_bias)
    hidden = low(jax.nn.gelu(pre_act, approximate=False))
    result = after_b + low_back(mm_high(hidden, w_down) + mix_bias[:, 2])
    return result.reshape(clip.shape)

def reference(clips_in, teacher, valid, norm_gain, norm_shift, w_space, qv_bias, w_space_out, mix_bias, w_time, w_time_out, w_up, up_bias, w_down):
    params = (norm_gain.astype(jnp.float32), norm_shift.astype(jnp.float32), w_space.astype(jnp.float32), qv_bias.astype(jnp.float32), w_space_out.astype(jnp.float32), mix_bias.astype(jnp.float32), w_time.astype(jnp.float32), w_time_out.astype(jnp.float32), w_up.astype(jnp.float32), up_bias.astype(jnp.float32), w_down.astype(jnp.float32))
    count = jnp.sum(valid.astype(jnp.float32))

    def clip_step(carry, item):
        clip, target, keep = item

        def objective(weights, inputs):
            result = layer(weights, inputs)
            diff = result - target
            return (result, jnp.sum(keep[..., None] * diff * diff) / (count * D))
        (result, part_loss), pullback = jax.vjp(objective, params, clip)
        grad_weights, grad_clip = pullback((jnp.zeros_like(result), jnp.ones_like(part_loss)))
        summed, total = carry
        summed = jax.tree.map(jnp.add, summed, grad_weights)
        return ((summed, total + part_loss), (result.astype(jnp.bfloat16), grad_clip.astype(jnp.bfloat16)))
    start = (jax.tree.map(jnp.zeros_like, params), jnp.zeros((), jnp.float32))
    (grads, loss_value), (outputs, grad_in) = lax.scan(clip_step, start, (clips_in.astype(jnp.float32), teacher.astype(jnp.float32), valid.astype(jnp.float32)))
    bias_all = grads[3]
    bias_kept = jnp.stack([bias_all[:, 0], bias_all[:, 1], bias_all[:, 3]], -1)
    return (outputs, loss_value, grad_in, grads[0], grads[1], grads[2], bias_kept, bias_all[:, 2], grads[4], grads[5], grads[6], grads[7], grads[8], grads[9], grads[10])
```

```python
import functools

import jax
import jax.numpy as jnp
from jax import lax
from jax.experimental import pallas as pl
from jax.experimental.pallas import tpu as pltpu
from jax.sharding import PartitionSpec as P

D = 768
HEADS = 12
HEAD = 64
FF = 3072
EPS = 1e-06
F32 = jnp.float32
BF16 = jnp.bfloat16
PARAMS = pltpu.CompilerParams(vmem_limit_bytes=60 << 20)

GAIN, SHIFT, QV, MIX, UP = 0, 3, 6, 10, 13


def dot(left, right):
    return jnp.dot(left, right, preferred_element_type=F32)


def dot_nt(left, right):
    return lax.dot_general(left, right, (((1,), (1,)), ((), ())), preferred_element_type=F32)


def dot_tn(left, right):
    return lax.dot_general(left, right, (((0,), (0,)), ((), ())), preferred_element_type=F32)


def normalize(rows):
    center = rows - jnp.mean(rows, -1, keepdims=True)
    inverse = lax.rsqrt(jnp.mean(center * center, -1, keepdims=True) + EPS)
    return center * inverse, inverse


def normalize_back(grad_out, hat, inverse, gain):
    grad_hat = grad_out * gain
    return inverse * (
        grad_hat
        - jnp.mean(grad_hat, -1, keepdims=True)
        - hat * jnp.mean(grad_hat * hat, -1, keepdims=True)
    )


def column_sum(rows):
    return jnp.sum(rows, 0, keepdims=True)


def first_lanes(shape):
    return lax.broadcasted_iota(jnp.int32, shape, 1) < HEAD


def halves(block):
    low = first_lanes(block.shape)
    zero = jnp.zeros_like(block)
    return jnp.where(low, block, zero), jnp.where(low, zero, block)


def pair(index):
    return slice(2 * HEAD * index, 2 * HEAD * (index + 1))


def attention(query, key, value, keep_probs, mask=None):
    outs = []
    for p in range(HEADS // 2):
        key_pair, value_pair = key[:, pair(p)], value[:, pair(p)]
        mixed = []
        for side, one in enumerate(halves(query[:, pair(p)])):
            scores = dot_nt(one, key_pair)
            if mask is not None:
                scores = jnp.where(mask, scores, -1e30)
            expo = jnp.exp(scores - jnp.max(scores, -1, keepdims=True))
            probs = (expo * (1.0 / jnp.sum(expo, -1, keepdims=True))).astype(BF16)
            keep_probs(2 * p + side, probs)
            mixed.append(dot(probs, value_pair))
        outs.append(jnp.where(first_lanes(mixed[0].shape), mixed[0], mixed[1]).astype(BF16))
    return jnp.concatenate(outs, 1)


def attention_back(query, key, value, grad_mix, probs_of):
    grad_q, grad_k, grad_v = [], [], []
    for p in range(HEADS // 2):
        query_pair, key_pair = query[:, pair(p)], key[:, pair(p)]
        value_pair, grad_pair = value[:, pair(p)], grad_mix[:, pair(p)]
        parts = []
        for side, one in enumerate(halves(grad_pair)):
            probs = probs_of(2 * p + side)
            wide = probs.astype(F32)
            grad_p = dot_nt(one, value_pair)
            term = wide * grad_p
            grad_s = (term - wide * jnp.sum(term, -1, keepdims=True)).astype(BF16)
            parts.append((dot(grad_s, key_pair), dot_tn(grad_s, query_pair), dot_tn(probs, grad_pair)))
        low = first_lanes(parts[0][0].shape)
        grad_q.append((jnp.where(low, parts[0][0], parts[1][0]) * HEAD ** (-0.5)).astype(BF16))
        grad_k.append(jnp.where(low, parts[0][1], parts[1][1]).astype(BF16))
        grad_v.append(jnp.where(low, parts[0][2], parts[1][2]).astype(BF16))
    return jnp.concatenate(grad_q + grad_k + grad_v, 1)


def project(rows, weights, table, query_row):
    proj = dot(rows, weights)
    query = (proj[:, :D] + table[query_row : query_row + 1, :]).astype(BF16)
    key = proj[:, D : 2 * D].astype(BF16)
    value = (proj[:, 2 * D :] + table[query_row + 1 : query_row + 2, :]).astype(BF16)
    return (query.astype(F32) * HEAD ** (-0.5)).astype(BF16), key, value


def fixed(shape):
    return pl.BlockSpec(shape, lambda *_: (0,) * len(shape), pipeline_mode=pl.Buffered(1))


def accumulate(ref, value, first):
    @pl.when(first)
    def _():
        ref[...] = value

    @pl.when(jnp.logical_not(first))
    def _():
        ref[...] += value


def space_kernel(clip, x_ref, table, w_ref, in_ref, q_ref, k_ref, v_ref, mix_ref, p_ref, out_ref):
    rows = x_ref[0, 0].astype(F32)
    hat, _ = normalize(rows)
    normed = (hat * table[GAIN : GAIN + 1, :] + table[SHIFT : SHIFT + 1, :]).astype(BF16)
    in_ref[0] = normed
    query, key, value = project(normed, w_ref[:, : 3 * D], table, QV)
    q_ref[0], k_ref[0], v_ref[0] = query, key, value

    def keep(head, probs):
        p_ref[0, head] = probs

    mixed = attention(query, key, value, keep)
    mix_ref[0] = mixed
    after = rows + dot(mixed, w_ref[:, 3 * D : 4 * D]) + table[MIX : MIX + 1, :]
    out_ref[0] = after.astype(BF16)


def space_forward(clip, inputs, table, weights):
    _, frames, places, _ = inputs.shape

    def frame(*tail):
        return pl.BlockSpec((1,) + tail, lambda i, c: (i,) + (0,) * len(tail))

    def shape(*tail):
        return jax.ShapeDtypeStruct((frames,) + tail, BF16)

    return pl.pallas_call(
        space_kernel,
        grid_spec=pltpu.PrefetchScalarGridSpec(
            num_scalar_prefetch=1,
            grid=(frames,),
            in_specs=[
                pl.BlockSpec((1, 1, places, D), lambda i, c: (c[0], i, 0, 0)),
                fixed(table.shape),
                fixed((D, 4 * D)),
            ],
            out_specs=[frame(places, D)] * 5 + [frame(HEADS, places, places), frame(places, D)],
        ),
        out_shape=[shape(places, D)] * 5 + [shape(HEADS, places, places), shape(places, D)],
        compiler_params=PARAMS,
        name="space_forward",
    )(clip, inputs, table, weights)


def largest_divisor(number, limit):
    return max(n for n in range(1, limit + 1) if number % n == 0)


def time_kernel(frames, group, a_ref, table, w_ref, in_ref, q_ref, k_ref, v_ref, mix_ref, p_ref, out_ref):
    rows = a_ref[...].astype(F32)
    hat, _ = normalize(rows)
    normed = (hat * table[GAIN + 1 : GAIN + 2, :] + table[SHIFT + 1 : SHIFT + 2, :]).astype(BF16)
    in_ref[...] = normed
    query, key, value = project(normed, w_ref[:, : 3 * D], table, QV + 2)
    q_ref[...], k_ref[...], v_ref[...] = query, key, value
    place = lax.broadcasted_iota(jnp.int32, (group, group), 0) // frames
    mask = place == lax.broadcasted_iota(jnp.int32, (group, group), 1) // frames

    def one_group(g, carry):
        span = pl.ds(pl.multiple_of(g * group, group), group)

        def keep(head, probs):
            p_ref[g, head] = probs

        mix_ref[span, :] = attention(q_ref[span, :], k_ref[span, :], v_ref[span, :], keep, mask)
        return carry

    lax.fori_loop(0, rows.shape[0] // group, one_group, 0)
    out_ref[...] = rows + dot(mix_ref[...], w_ref[:, 3 * D :]) + table[MIX + 1 : MIX + 2, :]


def time_tiles(places, frames):
    per_group = largest_divisor(places, 128 // frames)
    per_tile = per_group * largest_divisor(places // per_group, 4)
    return per_tile * frames, per_group * frames


def time_forward(after_a, table, weights, frames):
    tokens = after_a.shape[0]
    tile, group = time_tiles(tokens // frames, frames)
    rows = pl.BlockSpec((tile, D), lambda i: (i, 0))
    return pl.pallas_call(
        functools.partial(time_kernel, frames, group),
        grid=(tokens // tile,),
        in_specs=[rows, fixed(table.shape), fixed((D, 4 * D))],
        out_specs=[rows] * 5
        + [pl.BlockSpec((tile // group, HEADS, group, group), lambda i: (i, 0, 0, 0)), rows],
        out_shape=[jax.ShapeDtypeStruct((tokens, D), BF16)] * 5
        + [
            jax.ShapeDtypeStruct((tokens // group, HEADS, group, group), BF16),
            jax.ShapeDtypeStruct((tokens, D), F32),
        ],
        compiler_params=PARAMS,
        name="time_forward",
    )(after_a, table, weights)


def gelu_parts(u):
    bell = jnp.exp(-0.5 * u * u)
    base = 1.0 + 0.2316418886 * jnp.abs(u)
    t = 1.0 / base
    poly = t * (
        0.127414796 + t * (-0.142248368 + t * (0.7107068705 + t * (-0.7265760135 + t * 0.5307027145)))
    )
    tail = poly * bell
    area = jnp.where(u >= 0, 1.0 - tail, tail)
    return u * area, area + 0.3989422804014327 * (u * bell)


FF_CHUNK = 768


def feed_kernel(
    a_ref, t_ref, valid_ref, scale_ref, table, up_bias, up_ref, down_ref,
    out_ref, g_ref, d_up_ref, d_down_ref, rows_ref, bias_ref, square_ref,
    hidden, slope, d_up, d_down, stage, sems,
):
    step, last = pl.program_id(0), pl.num_programs(0) - 1
    first = step == 0
    after = a_ref[...]
    hat, inverse = normalize(after)
    normed = (hat * table[GAIN + 2 : GAIN + 3, :] + table[SHIFT + 2 : SHIFT + 3, :]).astype(BF16)
    total = after + table[MIX + 2 : MIX + 3, :]
    chunks = [slice(c, c + FF_CHUNK) for c in range(0, FF, FF_CHUNK)]
    for c in chunks:
        act, rise = gelu_parts(dot(normed, up_ref[:, c]) + up_bias[:, c])
        act = act.astype(BF16)
        hidden[:, c] = act
        slope[:, c] = rise.astype(BF16)
        total = total + dot(act, down_ref[c, :])
    out_ref[...] = total.astype(BF16)
    diff = (total - t_ref[...].astype(F32)) * valid_ref[...]
    accumulate(square_ref, column_sum(diff * diff), first)
    grad = diff * scale_ref[0, 0]
    grad_low = grad.astype(BF16)
    bias_c = column_sum(grad_low.astype(F32))
    back = jnp.zeros_like(grad)
    for c in chunks:
        grad_pre = dot_nt(grad_low, down_ref[c, :]) * slope[:, c].astype(F32)
        grad_pre = grad_pre.astype(BF16)
        accumulate(bias_ref.at[:, c], column_sum(grad_pre.astype(F32)), first)
        accumulate(d_down.at[c, :], dot_tn(hidden[:, c], grad_low), first)
        accumulate(d_up.at[:, c], dot_tn(normed, grad_pre), first)
        back = back + dot_nt(grad_pre, up_ref[:, c])
    accumulate(
        rows_ref, jnp.concatenate([column_sum(back * hat), column_sum(back), bias_c], 0), first
    )
    g_ref[...] = grad + normalize_back(back, hat, inverse, table[GAIN + 2 : GAIN + 3, :])

    @pl.when(step == last)
    def _():
        flush([(d_up.at[:, c], d_up_ref.at[:, c]) for c in chunks], stage, sems)
        flush([(d_down.at[c, :], d_down_ref.at[c, :]) for c in chunks], stage, sems)


def flush(moves, stage, sems):
    copies = []
    for i, (source, target) in enumerate(moves):
        if i >= 2:
            copies[i - 2].wait()
        stage[i % 2] = source[...].astype(BF16)
        copies.append(pltpu.make_async_copy(stage.at[i % 2], target, sems.at[i % 2]))
        copies[i].start()
    for copy in copies[-2:]:
        copy.wait()


def feed_forward(after_b, teacher, valid, scale, table, up_bias, w_up, w_down, tile):
    tokens = after_b.shape[0]
    rows = pl.BlockSpec((tile, D), lambda i: (i, 0))
    hbm = pl.BlockSpec(memory_space=pl.ANY)
    return pl.pallas_call(
        feed_kernel,
        grid=(tokens // tile,),
        in_specs=[
            rows,
            rows,
            pl.BlockSpec((tile, 1), lambda i: (i, 0)),
            pl.BlockSpec(memory_space=pltpu.SMEM),
            fixed(table.shape),
            fixed((1, FF)),
            fixed((D, FF)),
            fixed((FF, D)),
        ],
        out_specs=[rows, rows, hbm, hbm, fixed((3, D)), fixed((1, FF)), fixed((1, D))],
        out_shape=[
            jax.ShapeDtypeStruct((tokens, D), BF16),
            jax.ShapeDtypeStruct((tokens, D), F32),
            jax.ShapeDtypeStruct((D, FF), BF16),
            jax.ShapeDtypeStruct((FF, D), BF16),
            jax.ShapeDtypeStruct((3, D), F32),
            jax.ShapeDtypeStruct((1, FF), F32),
            jax.ShapeDtypeStruct((1, D), F32),
        ],
        scratch_shapes=[
            pltpu.VMEM((tile, FF), BF16),
            pltpu.VMEM((tile, FF), BF16),
            pltpu.VMEM((D, FF), F32),
            pltpu.VMEM((FF, D), F32),
            pltpu.VMEM((2, D, FF_CHUNK), BF16),
            pltpu.SemaphoreType.DMA((2,)),
        ],
        compiler_params=PARAMS,
        name="feed_forward",
    )(after_b, teacher, valid, scale, table, up_bias, w_up, w_down)


def time_back_kernel(
    group, g_ref, a_ref, in_ref, q_ref, k_ref, v_ref, mix_ref, p_ref, table, w_ref,
    out_ref, d_ref, rows_ref, grad_mix, grad_proj, d_proj, d_out, stage, sems,
):
    step, last = pl.program_id(0), pl.num_programs(0) - 1
    first = step == 0
    grad = g_ref[...]
    grad_low = grad.astype(BF16)
    accumulate(d_out, dot_tn(mix_ref[...], grad_low), first)
    grad_mix[...] = dot_nt(grad_low, w_ref[:, 3 * D :]).astype(BF16)

    def one_group(g, carry):
        span = pl.ds(pl.multiple_of(g * group, group), group)
        grad_proj[span, :] = attention_back(
            q_ref[span, :], k_ref[span, :], v_ref[span, :], grad_mix[span, :], lambda h: p_ref[g, h]
        )
        return carry

    lax.fori_loop(0, grad.shape[0] // group, one_group, 0)
    proj = grad_proj[...]
    accumulate(d_proj, dot_tn(in_ref[...], proj), first)
    sums = column_sum(proj.astype(F32))
    back = dot_nt(proj, w_ref[:, : 3 * D])
    hat, inverse = normalize(a_ref[...].astype(F32))
    accumulate(
        rows_ref,
        jnp.concatenate(
            [
                column_sum(back * hat),
                column_sum(back),
                sums[:, :D],
                sums[:, 2 * D :],
                column_sum(grad_low.astype(F32)),
            ],
            0,
        ),
        first,
    )
    out_ref[...] = (grad + normalize_back(back, hat, inverse, table[GAIN + 1 : GAIN + 2, :])).astype(BF16)

    @pl.when(step == last)
    def _():
        moves = [(d_proj.at[:, pl.ds(c * D, D)], d_ref.at[:, pl.ds(c * D, D)]) for c in range(3)]
        flush(moves + [(d_out, d_ref.at[:, pl.ds(3 * D, D)])], stage, sems)


def time_back(grad, after_a, saved, table, weights, frames):
    tokens = grad.shape[0]
    tile, group = time_tiles(tokens // frames, frames)
    rows = pl.BlockSpec((tile, D), lambda i: (i, 0))
    return pl.pallas_call(
        functools.partial(time_back_kernel, group),
        grid=(tokens // tile,),
        in_specs=[rows] * 7
        + [
            pl.BlockSpec((tile // group, HEADS, group, group), lambda i: (i, 0, 0, 0)),
            fixed(table.shape),
            fixed((D, 4 * D)),
        ],
        out_specs=[rows, pl.BlockSpec(memory_space=pl.ANY), fixed((5, D))],
        out_shape=[
            jax.ShapeDtypeStruct((tokens, D), BF16),
            jax.ShapeDtypeStruct((D, 4 * D), BF16),
            jax.ShapeDtypeStruct((5, D), F32),
        ],
        scratch_shapes=[
            pltpu.VMEM((tile, D), BF16),
            pltpu.VMEM((tile, 3 * D), BF16),
            pltpu.VMEM((D, 3 * D), F32),
            pltpu.VMEM((D, D), F32),
            pltpu.VMEM((2, D, D), BF16),
            pltpu.SemaphoreType.DMA((2,)),
        ],
        compiler_params=PARAMS,
        name="time_back",
    )(grad, after_a, *saved, table, weights)


def space_back_kernel(g_ref, q_ref, k_ref, v_ref, mix_ref, p_ref, w_ref, out_ref, d_ref, bias_ref):
    first = pl.program_id(0) == 0
    grad = g_ref[0]
    accumulate(d_ref, dot_tn(mix_ref[0], grad), first)
    accumulate(bias_ref, column_sum(grad.astype(F32)), first)
    grad_mix = dot_nt(grad, w_ref[...]).astype(BF16)
    out_ref[0] = attention_back(q_ref[0], k_ref[0], v_ref[0], grad_mix, lambda h: p_ref[0, h])


def space_back(grad, saved, weights):
    frames, places, _ = grad.shape

    def frame(*tail):
        return pl.BlockSpec((1,) + tail, lambda i: (i,) + (0,) * len(tail))

    return pl.pallas_call(
        space_back_kernel,
        grid=(frames,),
        in_specs=[frame(places, D)] * 5
        + [
            frame(HEADS, places, places),
            pl.BlockSpec((D, D), lambda i: (0, 3), pipeline_mode=pl.Buffered(1)),
        ],
        out_specs=[frame(places, 3 * D), fixed((D, D)), fixed((1, D))],
        out_shape=[
            jax.ShapeDtypeStruct((frames, places, 3 * D), BF16),
            jax.ShapeDtypeStruct((D, D), F32),
            jax.ShapeDtypeStruct((1, D), F32),
        ],
        compiler_params=PARAMS,
        name="space_back",
    )(grad, *saved, weights)


def space_weight_kernel(parts, frames, *refs):
    ins, projs, outs = refs[:parts], refs[parts : 2 * parts], refs[2 * parts : 3 * parts]
    d_ref, rows_ref, d_proj, stage, sems = refs[3 * parts :]
    step, last = pl.program_id(0), pl.num_programs(0) - 1

    @pl.when(step == 0)
    def _():
        d_proj[...] = jnp.zeros_like(d_proj)
        rows_ref[...] = jnp.zeros_like(rows_ref)

    for part in range(parts):

        @pl.when(step // frames == part)
        def _():
            proj = projs[part][0]
            d_proj[...] += dot_tn(ins[part][0], proj)
            rows_ref[...] += column_sum(proj.astype(F32))

    @pl.when(step == last)
    def _():
        total = outs[0][...]
        for ref in outs[1:]:
            total = total + ref[...]
        outs_sum = total
        stage[0] = outs_sum.astype(BF16)
        copy = pltpu.make_async_copy(stage.at[0], d_ref.at[:, pl.ds(3 * D, D)], sems.at[0])
        copy.start()
        copy.wait()
        flush(
            [(d_proj.at[:, pl.ds(c * D, D)], d_ref.at[:, pl.ds(c * D, D)]) for c in range(3)], stage, sems
        )


def space_weights(ins, projs, outs):
    parts = len(ins)
    frames, places, _ = ins[0].shape

    def frame(part, width):
        return pl.BlockSpec(
            (1, places, width), lambda i: (jnp.clip(i - part * frames, 0, frames - 1), 0, 0)
        )

    return pl.pallas_call(
        functools.partial(space_weight_kernel, parts, frames),
        grid=(parts * frames,),
        in_specs=[frame(p, D) for p in range(parts)]
        + [frame(p, 3 * D) for p in range(parts)]
        + [fixed((D, D))] * parts,
        out_specs=[pl.BlockSpec(memory_space=pl.ANY), fixed((1, 3 * D))],
        out_shape=[jax.ShapeDtypeStruct((D, 4 * D), BF16), jax.ShapeDtypeStruct((1, 3 * D), F32)],
        scratch_shapes=[
            pltpu.VMEM((D, 3 * D), F32),
            pltpu.VMEM((2, D, D), BF16),
            pltpu.SemaphoreType.DMA((2,)),
        ],
        compiler_params=PARAMS,
        name="space_weights",
    )(*ins, *projs, *outs)


def input_kernel(parts, frames, clips, *refs):
    grads, projs = refs[:parts], refs[parts : 2 * parts]
    x_ref, table, w_ref, out_ref, rows_ref = refs[2 * parts :]
    step = pl.program_id(0)

    @pl.when(step == 0)
    def _():
        rows_ref[...] = jnp.zeros_like(rows_ref)

    for part in range(parts):

        @pl.when(step // frames == part)
        def _():
            back = dot_nt(projs[part][0], w_ref[...])
            hat, inverse = normalize(x_ref[0, 0].astype(F32))
            rows_ref[...] += jnp.concatenate([column_sum(back * hat), column_sum(back)], 0)
            grad = grads[part][0].astype(F32) + normalize_back(
                back, hat, inverse, table[GAIN : GAIN + 1, :]
            )
            out_ref[0, 0] = grad.astype(BF16)


def input_grads(clips, grads, projs, inputs, table, weights):
    parts = len(grads)
    frames, places, _ = grads[0].shape

    def frame(part, width):
        return pl.BlockSpec(
            (1, places, width), lambda i, c: (jnp.clip(i - part * frames, 0, frames - 1), 0, 0)
        )

    clip = pl.BlockSpec((1, 1, places, D), lambda i, c: (c[i // frames], i % frames, 0, 0))
    return pl.pallas_call(
        functools.partial(input_kernel, parts, frames),
        grid_spec=pltpu.PrefetchScalarGridSpec(
            num_scalar_prefetch=1,
            grid=(parts * frames,),
            in_specs=[frame(p, D) for p in range(parts)]
            + [frame(p, 3 * D) for p in range(parts)]
            + [
                clip,
                fixed(table.shape),
                pl.BlockSpec((D, 3 * D), lambda *_: (0, 0), pipeline_mode=pl.Buffered(1)),
            ],
            out_specs=[clip, fixed((2, D))],
        ),
        out_shape=[jax.ShapeDtypeStruct(inputs.shape, BF16), jax.ShapeDtypeStruct((2, D), F32)],
        compiler_params=PARAMS,
        name="input_grads",
    )(clips, *grads, *projs, inputs, table, weights)


AXES = ("clip", "frame")


def gather(block):
    return lax.all_gather(block, AXES, axis=0, tiled=True)


def scatter(block):
    return lax.psum_scatter(block, AXES, scatter_dimension=0, tiled=True)


def shards(
    clips_in, teacher, valid, norm_gain, norm_shift, w_space, qv_bias, w_space_out, mix_bias,
    w_time, w_time_out, w_up, up_bias, w_down,
):
    batch, frames, places, _ = clips_in.shape
    ring = lax.axis_size("frame")
    pieces = ring // batch
    chunk = places // pieces
    all_frames = ring * frames
    me = lax.axis_index("frame")
    depth = w_up.shape[0]

    def swap(block, step):
        if step == 0:
            return block
        return lax.ppermute(block, "frame", [(i, i ^ step) for i in range(ring)])

    def clip_of(step):
        return (me // pieces) ^ (step // pieces)

    def place_of(step):
        return ((me % pieces) ^ (step % pieces)) * chunk

    def cut(block, step):
        if pieces == 1:
            return block
        return lax.dynamic_slice_in_dim(block, place_of(step), chunk, 0)

    def spread(block):
        got = []
        for step in range(ring):
            mine = lax.dynamic_index_in_dim(block, clip_of(step), 0, keepdims=False)
            got.append(swap(cut(jnp.swapaxes(mine, 0, 1), step), step))
        return jnp.concatenate(got, 1)

    count = jnp.sum(valid)
    counts = jnp.stack([count // 256, count % 256]).astype(BF16)
    smalls = jnp.concatenate(
        [
            norm_gain, norm_shift, qv_bias, mix_bias, up_bias.reshape(depth, -1),
            jnp.broadcast_to(counts[None], (depth, 2)),
        ],
        1,
    )
    smalls = jnp.pad(smalls, ((0, 0), (0, 128 - smalls.shape[1])))
    first = gather(jnp.concatenate([w_space, w_space_out, smalls], 1))
    second = gather(jnp.concatenate([w_time, w_time_out, w_up], 1))
    third = gather(w_down)
    columns = first[:, 4 * D : 4 * D + 24].astype(F32)
    table = jnp.swapaxes(columns, 0, 1)[:16]
    up_row = columns[:, UP : UP + 4].reshape(1, FF)
    counted = columns[::depth, UP + 4 : UP + 6]
    total_count = jnp.sum(counted[:, 0]) * 256.0 + jnp.sum(counted[:, 1])
    scale = (2.0 / (total_count * D)).reshape(1, 1)

    order = [(me // pieces) ^ j for j in range(batch)]
    clip_ids = [jnp.reshape(c, (1,)).astype(jnp.int32) for c in order]
    saved, sent = [None] * batch, [None] * ring
    for j in list(range(batch))[::-1]:
        *kept, after = space_forward(clip_ids[j], clips_in, table, first)
        saved[j] = kept
        after = jnp.swapaxes(after, 0, 1)
        for r in range(pieces):
            step = j * pieces + r
            sent[step] = swap(cut(after, step), step)
    after_a = jnp.concatenate(sent, 1).reshape(-1, D)
    teach = spread(teacher).reshape(-1, D)
    valid_column = spread(valid).reshape(-1, 1).astype(F32)

    in_b, q_b, k_b, v_b, mix_b, p_b, after_b = time_forward(after_a, table, second, all_frames)
    tile, _ = time_tiles(chunk, all_frames)
    layer_rows, grad_b, d_up, d_down, rows_c, bias_up, squares = feed_forward(
        after_b, teach, valid_column, scale, table, up_row, second[:, 4 * D :], third, tile
    )
    d_up, d_down = scatter(d_up), scatter(d_down)
    grad_a, d_time, rows_b = time_back(
        grad_b, after_a, (in_b, q_b, k_b, v_b, mix_b, p_b), table, second, all_frames
    )
    d_time = scatter(d_time)

    def give_back(rows):
        split = rows.reshape(chunk, ring, frames, D)
        return [swap(split[:, step], step) for step in range(ring)]

    def join(parts, j):
        if pieces == 1:
            return jnp.swapaxes(parts[j], 0, 1)
        whole = jnp.zeros((places, frames, D), BF16)
        for r in range(pieces):
            step = j * pieces + r
            whole = lax.dynamic_update_slice_in_dim(whole, parts[step], place_of(step), 0)
        return jnp.swapaxes(whole, 0, 1)

    layer_parts, grad_parts = give_back(layer_rows), give_back(grad_a)
    grads = [join(grad_parts, j) for j in range(batch)]
    projs, outs, biases = [], [], []
    for j in range(batch):
        proj, d_out, bias = space_back(grads[j], saved[j][1:], first)
        projs.append(proj)
        outs.append(d_out)
        biases.append(bias)
    d_space, sums_a = space_weights([s[0] for s in saved], projs, outs)
    d_space = scatter(d_space)
    input_grad, rows_a = input_grads(
        jnp.stack(order).astype(jnp.int32), grads, projs, clips_in, table, first
    )
    layer_out = jnp.zeros(clips_in.shape, BF16)
    for j in range(batch):
        layer_out = lax.dynamic_update_index_in_dim(layer_out, join(layer_parts, j), order[j], 0)

    small = jnp.concatenate(
        [
            rows_a[0:1], rows_b[0:1], rows_c[0:1],
            rows_a[1:2], rows_b[1:2], rows_c[1:2],
            sums_a[:, :D], sums_a[:, 2 * D :], rows_b[3:4], rows_b[2:3],
            sum(biases), rows_b[4:5], rows_c[2:3],
            jnp.swapaxes(bias_up.reshape(D, 4), 0, 1),
            squares,
        ],
        0,
    )
    small = lax.psum(small, AXES)
    loss_value = jnp.sum(small[17]) / (total_count * D)
    here = lax.dynamic_slice_in_dim(
        jnp.swapaxes(small, 0, 1), (lax.axis_index("clip") * ring + me) * depth, depth, 0
    )
    return (
        layer_out,
        loss_value,
        input_grad,
        here[:, 0:3],
        here[:, 3:6],
        d_space[:, : 3 * D].astype(F32),
        here[:, 6:9],
        here[:, 9],
        d_space[:, 3 * D :].astype(F32),
        here[:, 10:13],
        d_time[:, : 3 * D].astype(F32),
        d_time[:, 3 * D :].astype(F32),
        d_up.astype(F32),
        here[:, 13:17].reshape(-1),
        d_down.astype(F32),
    )


def solution(mesh):
    tokens, rows = P("clip", "frame", None, None), P(AXES, None)
    in_specs = (tokens, tokens, P("clip", "frame", None)) + (rows,) * 9 + (P(AXES), rows)
    out_specs = (
        (tokens, P(), tokens, rows, rows, rows, rows, P(AXES)) + (rows,) * 5 + (P(AXES), rows)
    )
    return jax.shard_map(shards, mesh=mesh, in_specs=in_specs, out_specs=out_specs, check_vma=False)
```

```python
import functools

import jax
import jax.numpy as jnp
from jax import lax
from jax.experimental import pallas as pl
from jax.experimental.pallas import tpu as pltpu
from jax.sharding import PartitionSpec as P

D = 768
HEADS = 12
HEAD = 64
FF = 3072
EPS = 1e-06
F32 = jnp.float32
BF16 = jnp.bfloat16
PARAMS = pltpu.CompilerParams(vmem_limit_bytes=60 << 20)


def cost(flops, moved=0):
    return pl.CostEstimate(flops=int(flops), bytes_accessed=int(moved), transcendentals=0)


GAIN, SHIFT, QV, MIX, UP = 0, 3, 6, 10, 13


def dot(left, right):
    return jnp.dot(left, right, preferred_element_type=F32)


def dot_nt(left, right):
    return lax.dot_general(left, right, (((1,), (1,)), ((), ())), preferred_element_type=F32)


def dot_tn(left, right):
    return lax.dot_general(left, right, (((0,), (0,)), ((), ())), preferred_element_type=F32)


def normalize(rows):
    center = rows - jnp.mean(rows, -1, keepdims=True)
    inverse = lax.rsqrt(jnp.mean(center * center, -1, keepdims=True) + EPS)
    return center * inverse, inverse


def normalize_back(grad_out, hat, inverse, gain):
    grad_hat = grad_out * gain
    return inverse * (
        grad_hat
        - jnp.mean(grad_hat, -1, keepdims=True)
        - hat * jnp.mean(grad_hat * hat, -1, keepdims=True)
    )


def column_sum(rows):
    return jnp.sum(rows, 0, keepdims=True)


def first_lanes(shape):
    return lax.broadcasted_iota(jnp.int32, shape, 1) < HEAD


def halves(block):
    low = first_lanes(block.shape)
    zero = jnp.zeros_like(block)
    return jnp.where(low, block, zero), jnp.where(low, zero, block)


def pair(index):
    return slice(2 * HEAD * index, 2 * HEAD * (index + 1))


def grow(block, rows):
    if rows == block.shape[0]:
        return block
    return jnp.concatenate([block, jnp.zeros((rows - block.shape[0], block.shape[1]), block.dtype)], 0)


def stack(block):
    return jnp.concatenate(halves(block), 0)


def merge(two):
    rows = two.shape[0] // 2
    return jnp.where(first_lanes((rows, two.shape[1])), two[:rows], two[rows:])


def kept(rows):
    return HEADS // 2, 2 * padded(rows), rows


def padded(rows):
    return -(-rows // 16) * 16


def attention(query, key, value, keep_probs, frames=None):
    rows = query.shape[0]
    full = padded(rows)
    place = lax.broadcasted_iota(jnp.int32, (full, rows), 0)
    if frames is not None:
        mask = place // frames == lax.broadcasted_iota(jnp.int32, (full, rows), 1) // frames
    else:
        mask = place < rows
    outs = []

    def score(p):
        return dot_nt(stack(grow(key[:, pair(p)], full)), query[:, pair(p)])

    scores = score(0)
    for p in range(HEADS // 2):
        now = scores
        if p + 1 < HEADS // 2:
            scores = score(p + 1)
        probs = []
        for one in (now[:full], now[full:]):
            one = jnp.where(mask, one, -1e30)
            expo = jnp.exp(one - jnp.max(one, 0, keepdims=True))
            probs.append((expo * (1.0 / jnp.sum(expo, 0, keepdims=True))).astype(BF16))
        probs = jnp.concatenate(probs, 0)
        keep_probs(p, probs)
        outs.append(dot_tn(probs, stack(grow(value[:, pair(p)], full))).astype(BF16))
    return jnp.concatenate(outs, 1)


def attention_back(query, key, value, grad_mix, probs_of):
    rows = query.shape[0]
    full = padded(rows)
    grad_q, grad_k, grad_v = [], [], []

    def probs_grad(p):
        return dot_nt(stack(grow(value[:, pair(p)], full)), grad_mix[:, pair(p)])

    grad_p = probs_grad(0)
    for p in range(HEADS // 2):
        probs = probs_of(p)
        wide = probs.astype(F32)
        term = wide * grad_p
        grad_s = []
        for head in (slice(0, full), slice(full, 2 * full)):
            grad_s.append((term[head] - wide[head] * column_sum(term[head])).astype(BF16))
        grad_s = jnp.concatenate(grad_s, 0)
        if p + 1 < HEADS // 2:
            grad_p = probs_grad(p + 1)
        to_v = merge(dot(probs, grad_mix[:, pair(p)]))
        to_k = merge(dot(grad_s, query[:, pair(p)]))
        to_q = dot_tn(grad_s, stack(grow(key[:, pair(p)], full)))
        grad_q.append((to_q * HEAD ** (-0.5)).astype(BF16))
        grad_k.append(to_k[:rows].astype(BF16))
        grad_v.append(to_v[:rows].astype(BF16))
    return jnp.concatenate(grad_q + grad_k + grad_v, 1)


def project(rows, weights, table, query_row):
    proj = dot(rows, weights)
    query = (proj[:, :D] + table[query_row : query_row + 1, :]).astype(BF16)
    key = proj[:, D : 2 * D].astype(BF16)
    value = (proj[:, 2 * D :] + table[query_row + 1 : query_row + 2, :]).astype(BF16)
    return (query.astype(F32) * HEAD ** (-0.5)).astype(BF16), key, value


def fixed(shape):
    return pl.BlockSpec(shape, lambda *_: (0,) * len(shape), pipeline_mode=pl.Buffered(1))


def columns_of(width, index):
    return pl.BlockSpec((D, width), lambda *_: (0, index), pipeline_mode=pl.Buffered(1))


def collect(refs, scratch):
    frames = refs[0].shape[1]
    for n, ref in enumerate(refs):
        scratch[:, n * frames : (n + 1) * frames, :] = ref[...].astype(F32)
    return scratch[...].reshape(-1, D)


def deal(rows, scratch, refs):
    frames = refs[0].shape[1]
    scratch[...] = rows.reshape(scratch.shape)
    for n, ref in enumerate(refs):
        ref[...] = scratch[:, n * frames : (n + 1) * frames, :].astype(BF16)


def clear(first, *refs):
    @pl.when(first)
    def _():
        for ref in refs:
            ref[...] = jnp.zeros_like(ref)


def space_kernel(clip, x_ref, table, w_ref, in_ref, q_ref, k_ref, v_ref, mix_ref, p_ref, out_ref):
    rows = x_ref[0, 0].astype(F32)
    hat, _ = normalize(rows)
    normed = (hat * table[GAIN : GAIN + 1, :] + table[SHIFT : SHIFT + 1, :]).astype(BF16)
    in_ref[0] = normed
    query, key, value = project(normed, w_ref[:, : 3 * D], table, QV)
    q_ref[0], k_ref[0], v_ref[0] = query, key, value

    def keep(heads, probs):
        p_ref[0, heads] = probs

    mixed = attention(query, key, value, keep)
    mix_ref[0] = mixed
    after = rows + dot(mixed, w_ref[:, 3 * D : 4 * D]) + table[MIX : MIX + 1, :]
    out_ref[0] = after.astype(BF16)


def space_forward(clip, inputs, table, weights):
    _, frames, places, _ = inputs.shape

    def frame(*tail):
        return pl.BlockSpec((1,) + tail, lambda i, c: (i,) + (0,) * len(tail))

    def shape(*tail):
        return jax.ShapeDtypeStruct((frames,) + tail, BF16)

    return pl.pallas_call(
        space_kernel,
        grid_spec=pltpu.PrefetchScalarGridSpec(
            num_scalar_prefetch=1,
            grid=(frames,),
            in_specs=[
                pl.BlockSpec((1, 1, places, D), lambda i, c: (c[0], i, 0, 0)),
                fixed(table.shape),
                fixed((D, 4 * D)),
            ],
            out_specs=[frame(places, D)] * 5 + [frame(*kept(places)), frame(places, D)],
        ),
        out_shape=[shape(places, D)] * 5 + [shape(*kept(places)), shape(places, D)],
        compiler_params=PARAMS,
        cost_estimate=cost(24 * frames * places * D * D),
        name="space_forward",
    )(clip, inputs, table, weights)


def largest_divisor(number, limit):
    return max(n for n in range(1, limit + 1) if number % n == 0)


def time_kernel(frames, group, ring, *refs):
    parts, (table, w_ref) = refs[:ring], refs[ring : ring + 2]
    a_ref, in_ref, q_ref, k_ref, v_ref, mix_ref, p_ref, out_ref, scratch = refs[ring + 2 :]
    rows = collect(parts, scratch)
    a_ref[...] = rows.astype(BF16)
    hat, _ = normalize(rows)
    normed = (hat * table[GAIN + 1 : GAIN + 2, :] + table[SHIFT + 1 : SHIFT + 2, :]).astype(BF16)
    in_ref[...] = normed
    query, key, value = project(normed, w_ref[:, : 3 * D], table, QV + 2)
    q_ref[...], k_ref[...], v_ref[...] = query, key, value

    def one_group(g):
        span = slice(g * group, (g + 1) * group)

        def keep(heads, probs):
            p_ref[g, heads] = probs

        mix_ref[span, :] = attention(q_ref[span, :], k_ref[span, :], v_ref[span, :], keep, frames)

    for g in range(rows.shape[0] // group):
        one_group(g)
    out_ref[...] = rows + dot(mix_ref[...], w_ref[:, 3 * D :]) + table[MIX + 1 : MIX + 2, :]


def time_tiles(places, frames):
    per_group = largest_divisor(places, 128 // frames)
    per_tile = per_group * largest_divisor(places // per_group, 4)
    return per_tile * frames, per_group * frames


def piece_specs(parts, tile):
    frames = parts[0].shape[1]
    places = tile // (frames * len(parts))
    return [pl.BlockSpec((places, frames, D), lambda i: (i, 0, 0))] * len(parts)


def join_scratch(parts, tile):
    frames = parts[0].shape[1] * len(parts)
    return pltpu.VMEM((tile // frames, frames, D), F32)


def time_forward(parts, table, weights):
    places, frames = parts[0].shape[0], parts[0].shape[1] * len(parts)
    tokens = places * frames
    tile, group = time_tiles(places, frames)
    rows = pl.BlockSpec((tile, D), lambda i: (i, 0))
    return pl.pallas_call(
        functools.partial(time_kernel, frames, group, len(parts)),
        grid=(tokens // tile,),
        in_specs=piece_specs(parts, tile) + [fixed(table.shape), columns_of(4 * D, 0)],
        out_specs=[rows] * 6
        + [pl.BlockSpec((tile // group,) + kept(group), lambda i: (i, 0, 0, 0)), rows],
        out_shape=[jax.ShapeDtypeStruct((tokens, D), BF16)] * 6
        + [
            jax.ShapeDtypeStruct((tokens // group,) + kept(group), BF16),
            jax.ShapeDtypeStruct((tokens, D), F32),
        ],
        scratch_shapes=[join_scratch(parts, tile)],
        compiler_params=PARAMS,
        cost_estimate=cost(24 * tokens * D * D),
        name="time_forward",
    )(*parts, table, weights)


def gelu_parts(u):
    bell = jnp.exp(-0.5 * u * u)
    base = 1.0 + 0.2316418886 * jnp.abs(u)
    t = 1.0 / base
    poly = t * (
        0.127414796 + t * (-0.142248368 + t * (0.7107068705 + t * (-0.7265760135 + t * 0.5307027145)))
    )
    tail = poly * bell
    area = jnp.where(u >= 0, 1.0 - tail, tail)
    return u * area, area + 0.3989422804014327 * (u * bell)


FF_CHUNK = 768


def feed_kernel(ring, *refs):
    teachers, refs = refs[:ring], refs[ring:]
    (a_ref, valid_ref, scale_ref, table, up_bias, up_ref, down_ref), refs = refs[:7], refs[7:]
    outs, refs = refs[:ring], refs[ring:]
    g_ref, d_ref, rows_ref, bias_ref, square_ref, hidden, slope, d_up, d_down, stage, sems, scratch = refs
    step, last = pl.program_id(0), pl.num_programs(0) - 1
    clear(step == 0, d_up, d_down, rows_ref, bias_ref, square_ref)
    after = a_ref[...]
    hat, inverse = normalize(after)
    normed = (hat * table[GAIN + 2 : GAIN + 3, :] + table[SHIFT + 2 : SHIFT + 3, :]).astype(BF16)
    total = after + table[MIX + 2 : MIX + 3, :]
    chunks = [slice(c, c + FF_CHUNK) for c in range(0, FF, FF_CHUNK)]
    for c in chunks:
        act, rise = gelu_parts(dot(normed, up_ref[:, c]) + up_bias[:, c])
        act = act.astype(BF16)
        hidden[:, c] = act
        slope[:, c] = rise.astype(BF16)
        total = total + dot(act, down_ref[:, c])
    deal(total, scratch, outs)
    diff = (total - collect(teachers, scratch)) * valid_ref[...]
    square_ref[...] += column_sum(diff * diff)
    grad = diff * scale_ref[0, 0]
    grad_low = grad.astype(BF16)
    bias_c = column_sum(grad_low.astype(F32))
    back = jnp.zeros_like(grad)
    for c in chunks:
        grad_pre = dot_nt(grad_low, down_ref[:, c]) * slope[:, c].astype(F32)
        grad_pre = grad_pre.astype(BF16)
        bias_ref[:, c] += column_sum(grad_pre.astype(F32))
        d_down[:, c] += dot_tn(hidden[:, c], grad_low)
        d_up[:, c] += dot_tn(normed, grad_pre)
        back = back + dot_nt(grad_pre, up_ref[:, c])
    rows_ref[...] += jnp.concatenate([column_sum(back * hat), column_sum(back), bias_c], 0)
    g_ref[...] = grad + normalize_back(back, hat, inverse, table[GAIN + 2 : GAIN + 3, :])

    @pl.when(step == last)
    def _():
        moves = []
        for source, start in ((d_up, 4 * D), (d_down, 4 * D + FF)):
            moves += [(source.at[:, c], d_ref.at[:, start + c.start : start + c.stop]) for c in chunks]
        flush(moves, stage, sems)


def flush(moves, stage, sems):
    copies = []
    for i, (source, target) in enumerate(moves):
        if i >= 2:
            copies[i - 2].wait()
        stage[i % 2] = source[...].astype(BF16)
        copies.append(pltpu.make_async_copy(stage.at[i % 2], target, sems.at[i % 2]))
        copies[i].start()
    for copy in copies[-2:]:
        copy.wait()


def feed_forward(after_b, teachers, valid, scale, table, up_bias, weights, tile):
    tokens, ring = after_b.shape[0], len(teachers)
    rows = pl.BlockSpec((tile, D), lambda i: (i, 0))
    *outs, grad, d_feed, sums, bias, squares = pl.pallas_call(
        functools.partial(feed_kernel, ring),
        grid=(tokens // tile,),
        in_specs=piece_specs(teachers, tile)
        + [
            rows,
            pl.BlockSpec((tile, 1), lambda i: (i, 0)),
            pl.BlockSpec(memory_space=pltpu.SMEM),
            fixed(table.shape),
            fixed((1, FF)),
            columns_of(FF, 1),
            columns_of(FF, 2),
        ],
        out_specs=piece_specs(teachers, tile)
        + [rows, pl.BlockSpec(memory_space=pl.ANY), fixed((3, D)), fixed((1, FF)), fixed((1, D))],
        out_shape=[jax.ShapeDtypeStruct(t.shape, BF16) for t in teachers]
        + [
            jax.ShapeDtypeStruct((tokens, D), F32),
            jax.ShapeDtypeStruct((D, 4 * D + 2 * FF), BF16),
            jax.ShapeDtypeStruct((3, D), F32),
            jax.ShapeDtypeStruct((1, FF), F32),
            jax.ShapeDtypeStruct((1, D), F32),
        ],
        scratch_shapes=[
            pltpu.VMEM((tile, FF), BF16),
            pltpu.VMEM((tile, FF), BF16),
            pltpu.VMEM((D, FF), F32),
            pltpu.VMEM((D, FF), F32),
            pltpu.VMEM((2, D, FF_CHUNK), BF16),
            pltpu.SemaphoreType.DMA((2,)),
            join_scratch(teachers, tile),
        ],
        compiler_params=PARAMS,
        cost_estimate=cost(80 * tokens * D * D),
        name="feed_forward",
    )(*teachers, after_b, valid, scale, table, up_bias, weights, weights)
    return outs, grad, d_feed, sums, bias, squares


def time_back_kernel(group, ring, *refs):
    (g_ref, a_ref, in_ref, q_ref, k_ref, v_ref, mix_ref, p_ref, table, w_ref), refs = refs[:10], refs[11:]
    outs, refs = refs[:ring], refs[ring:]
    d_ref, rows_ref, grad_mix, grad_proj, d_proj, d_out, stage, sems, scratch = refs
    step, last = pl.program_id(0), pl.num_programs(0) - 1
    clear(step == 0, d_proj, d_out, rows_ref)
    grad = g_ref[...]
    grad_low = grad.astype(BF16)
    d_out[...] += dot_tn(mix_ref[...], grad_low)
    grad_mix[...] = dot_nt(grad_low, w_ref[:, 3 * D :]).astype(BF16)

    def one_group(g):
        span = slice(g * group, (g + 1) * group)
        grad_proj[span, :] = attention_back(
            q_ref[span, :],
            k_ref[span, :],
            v_ref[span, :],
            grad_mix[span, :],
            lambda heads: p_ref[g, heads],
        )

    for g in range(grad.shape[0] // group):
        one_group(g)
    proj = grad_proj[...]
    d_proj[...] += dot_tn(in_ref[...], proj)
    sums = column_sum(proj.astype(F32))
    back = dot_nt(proj, w_ref[:, : 3 * D])
    hat, inverse = normalize(a_ref[...].astype(F32))
    rows_ref[...] += jnp.concatenate(
        [
            column_sum(back * hat),
            column_sum(back),
            sums[:, :D],
            sums[:, 2 * D :],
            column_sum(grad_low.astype(F32)),
        ],
        0,
    )
    deal(grad + normalize_back(back, hat, inverse, table[GAIN + 1 : GAIN + 2, :]), scratch, outs)

    @pl.when(step == last)
    def _():
        moves = [(d_proj.at[:, pl.ds(c * D, D)], d_ref.at[:, pl.ds(c * D, D)]) for c in range(3)]
        flush(moves + [(d_out, d_ref.at[:, pl.ds(3 * D, D)])], stage, sems)


def time_back(grad, saved, like, table, weights, matrix):
    ring, tokens = len(like), grad.shape[0]
    places, frames = like[0].shape[0], like[0].shape[1] * ring
    tile, group = time_tiles(places, frames)
    rows = pl.BlockSpec((tile, D), lambda i: (i, 0))
    *outs, d_time, sums = pl.pallas_call(
        functools.partial(time_back_kernel, group, ring),
        grid=(tokens // tile,),
        in_specs=[rows] * 7
        + [
            pl.BlockSpec((tile // group,) + kept(group), lambda i: (i, 0, 0, 0)),
            fixed(table.shape),
            columns_of(4 * D, 0),
            pl.BlockSpec(memory_space=pl.ANY),
        ],
        out_specs=piece_specs(like, tile) + [pl.BlockSpec(memory_space=pl.ANY), fixed((5, D))],
        out_shape=[jax.ShapeDtypeStruct(t.shape, BF16) for t in like]
        + [jax.ShapeDtypeStruct(matrix.shape, BF16), jax.ShapeDtypeStruct((5, D), F32)],
        input_output_aliases={10: ring},
        scratch_shapes=[
            pltpu.VMEM((tile, D), BF16),
            pltpu.VMEM((tile, 3 * D), BF16),
            pltpu.VMEM((D, 3 * D), F32),
            pltpu.VMEM((D, D), F32),
            pltpu.VMEM((2, D, D), BF16),
            pltpu.SemaphoreType.DMA((2,)),
            join_scratch(like, tile),
        ],
        compiler_params=PARAMS,
        cost_estimate=cost(42 * tokens * D * D),
        name="time_back",
    )(grad, *saved, table, weights, matrix)
    return outs, d_time, sums


def space_back_kernel(g_ref, q_ref, k_ref, v_ref, mix_ref, p_ref, w_ref, out_ref, d_ref, bias_ref):
    clear(pl.program_id(0) == 0, d_ref, bias_ref)
    grad = g_ref[0]
    d_ref[...] += dot_tn(mix_ref[0], grad)
    bias_ref[...] += column_sum(grad.astype(F32))
    grad_mix = dot_nt(grad, w_ref[...]).astype(BF16)
    out_ref[0] = attention_back(
        q_ref[0], k_ref[0], v_ref[0], grad_mix, lambda heads: p_ref[0, heads]
    )


def space_back(grad, saved, weights):
    frames, places, _ = grad.shape

    def frame(*tail):
        return pl.BlockSpec((1,) + tail, lambda i: (i,) + (0,) * len(tail))

    return pl.pallas_call(
        space_back_kernel,
        grid=(frames,),
        in_specs=[frame(places, D)] * 5
        + [
            frame(*kept(places)),
            pl.BlockSpec((D, D), lambda i: (0, 3), pipeline_mode=pl.Buffered(1)),
        ],
        out_specs=[frame(places, 3 * D), fixed((D, D)), fixed((1, D))],
        out_shape=[
            jax.ShapeDtypeStruct((frames, places, 3 * D), BF16),
            jax.ShapeDtypeStruct((D, D), F32),
            jax.ShapeDtypeStruct((1, D), F32),
        ],
        compiler_params=PARAMS,
        cost_estimate=cost(24 * frames * places * D * D),
        name="space_back",
    )(grad, *saved, weights)


SMALL = 128


def space_weight_kernel(parts, steps, *refs):
    ins, projs, outs = refs[:parts], refs[parts : 2 * parts], refs[2 * parts : 3 * parts]
    d_ref, rows_ref, d_proj, d_out, stage, sems = refs[3 * parts :]
    step, last = pl.program_id(0), pl.num_programs(0) - 1
    clear(step == 0, d_proj, rows_ref)
    for part in range(parts):

        @pl.when(step // steps == part)
        def _():
            frames = range(ins[part].shape[0])
            d_proj[...] += sum(dot_tn(ins[part][f], projs[part][f]) for f in frames)
            rows_ref[...] += sum(column_sum(projs[part][f].astype(F32)) for f in frames)

    @pl.when(step == last)
    def _():
        d_out[...] = sum(ref[...] for ref in outs)
        moves = [(d_proj.at[:, pl.ds(c * D, D)], d_ref.at[:, pl.ds(c * D, D)]) for c in range(3)]
        flush(moves + [(d_out, d_ref.at[:, pl.ds(3 * D, D)])], stage, sems)


def space_weights(ins, projs, outs):
    parts = len(ins)
    frames, places, _ = ins[0].shape
    block = largest_divisor(frames, 2)
    steps = frames // block

    def frame(part, width):
        return pl.BlockSpec(
            (block, places, width), lambda i: (jnp.clip(i - part * steps, 0, steps - 1), 0, 0)
        )

    return pl.pallas_call(
        functools.partial(space_weight_kernel, parts, steps),
        grid=(parts * steps,),
        in_specs=[frame(p, D) for p in range(parts)]
        + [frame(p, 3 * D) for p in range(parts)]
        + [fixed((D, D))] * parts,
        out_specs=[pl.BlockSpec(memory_space=pl.ANY), fixed((1, 3 * D))],
        out_shape=[
            jax.ShapeDtypeStruct((D, 4 * D), BF16),
            jax.ShapeDtypeStruct((1, 3 * D), F32),
        ],
        scratch_shapes=[
            pltpu.VMEM((D, 3 * D), F32),
            pltpu.VMEM((D, D), F32),
            pltpu.VMEM((2, D, D), BF16),
            pltpu.SemaphoreType.DMA((2,)),
        ],
        compiler_params=PARAMS,
        cost_estimate=cost(18 * parts * frames * places * D * D),
        name="space_weights",
    )(*ins, *projs, *outs)


def small_kernel(count, *refs):
    rows, (out_ref, table) = refs[:count], refs[count:]
    table[...] = jnp.zeros_like(table)
    at = 0
    for ref in rows:
        table[at : at + ref.shape[0], :] = ref[...]
        at += ref.shape[0]
    out_ref[...] = jnp.swapaxes(table[...], 0, 1)


def as_columns(rows):
    return pl.pallas_call(
        functools.partial(small_kernel, len(rows)),
        out_shape=jax.ShapeDtypeStruct((D, SMALL), F32),
        scratch_shapes=[pltpu.VMEM((SMALL, D), F32)],
        name="as_columns",
    )(*rows)


def input_kernel(clip, g_ref, p_ref, x_ref, table, w_ref, *refs):
    out_ref, rows_ref = refs[-2:]
    clear(pl.program_id(0) == 0, rows_ref)
    back = dot_nt(p_ref[0], w_ref[...])
    hat, inverse = normalize(x_ref[0, 0].astype(F32))
    rows_ref[...] += jnp.concatenate([column_sum(back * hat), column_sum(back)], 0)
    grad = g_ref[0].astype(F32) + normalize_back(back, hat, inverse, table[GAIN : GAIN + 1, :])
    out_ref[0, 0] = grad.astype(BF16)


def input_grads(clip, grad, proj, inputs, table, weights, before):
    frames, places, _ = grad.shape
    frame = pl.BlockSpec((1, places, D), lambda i, c: (i, 0, 0))
    block = pl.BlockSpec((1, 1, places, D), lambda i, c: (c[0], i, 0, 0))
    more = [] if before is None else [before]
    return pl.pallas_call(
        input_kernel,
        grid_spec=pltpu.PrefetchScalarGridSpec(
            num_scalar_prefetch=1,
            grid=(frames,),
            in_specs=[
                frame,
                pl.BlockSpec((1, places, 3 * D), lambda i, c: (i, 0, 0)),
                block,
                fixed(table.shape),
                columns_of(3 * D, 0),
            ]
            + [pl.BlockSpec(memory_space=pl.ANY) for _ in more],
            out_specs=[block, fixed((2, D))],
        ),
        out_shape=[jax.ShapeDtypeStruct(inputs.shape, BF16), jax.ShapeDtypeStruct((2, D), F32)],
        input_output_aliases={6: 0} if more else {},
        compiler_params=PARAMS,
        cost_estimate=cost(18 * frames * places * D * D),
        name="input_grads",
    )(clip, grad, proj, inputs, table, weights, *more)


def place_kernel(order, *refs):
    blocks, out_ref = refs[:-1], refs[-1]
    for n, ref in enumerate(blocks):

        @pl.when(pl.program_id(0) == n)
        def _():
            out_ref[0] = ref[...]


def place_clips(order, blocks):
    shape = blocks[0].shape
    return pl.pallas_call(
        place_kernel,
        grid_spec=pltpu.PrefetchScalarGridSpec(
            num_scalar_prefetch=1,
            grid=(len(blocks),),
            in_specs=[fixed(shape)] * len(blocks),
            out_specs=pl.BlockSpec((1,) + shape, lambda i, order: (order[i], 0, 0, 0)),
        ),
        out_shape=jax.ShapeDtypeStruct((len(blocks),) + shape, BF16),
        compiler_params=PARAMS,
        name="place_clips",
    )(order, *blocks)


AXES = ("clip", "frame")
MESH = pl.DeviceIdType.MESH


def position():
    clip, frame = lax.axis_index("clip"), lax.axis_index("frame")
    return clip // 2, clip % 2, frame // 2, frame % 2


def device(z, x, y, core):
    return (2 * z + x, 2 * y + core)


def greet(partners):
    barrier = pltpu.get_barrier_semaphore()
    for partner in partners:
        pl.semaphore_signal(barrier, inc=1, device_id=partner, device_id_type=MESH)
    pl.semaphore_wait(barrier, len(partners))


def neighbours(depth, height):
    z, x, y, core = position()
    return (
        [device(lax.rem(z + d, depth), x, y, core) for d in range(1, depth)]
        + [device(z, x, lax.rem(y + d, height), core) for d in range(1, height)]
        + [device(z, 1 - x, y, core), device(z, x, y, 1 - core)]
    )


def gather_kernel(depth, height, in_ref, out_ref, local, y_send, y_recv, z_send, z_recv, x_send, x_recv, c_send, c_recv):
    z, x, y, core = position()
    greet(neighbours(depth, height))

    def send(source, target, sems, slot, index, to):
        copy = pltpu.make_async_remote_copy(
            src_ref=source, dst_ref=target, send_sem=sems[0].at[slot], recv_sem=sems[1].at[index],
            device_id=to, device_id_type=MESH,
        )
        copy.start()
        return copy

    def block(zz, xx, cc):
        return out_ref.at[2 * zz + xx, :, cc]

    def arrival(ref, sem):
        return pltpu.make_async_remote_copy(
            src_ref=ref, dst_ref=ref, send_sem=sem, recv_sem=sem, device_id=device(z, 1 - x, y, core), device_id_type=MESH
        )

    sent = []
    own = out_ref.at[2 * z + x, y, core]
    for d in range(1, height):
        sent.append(send(in_ref, own, (y_send, y_recv), d - 1, y, device(z, x, lax.rem(y + d, height), core)))
    mine = pltpu.make_async_copy(in_ref, own, local)
    mine.start()
    mine.wait()
    for d in range(1, height):
        other = lax.rem(y + height - d, height)
        arrival(out_ref.at[2 * z + x, other, core], y_recv.at[other]).wait_recv()
    here = block(z, x, core)
    for d in range(1, depth):
        sent.append(send(here, here, (z_send, z_recv), d - 1, z, device(lax.rem(z + d, depth), x, y, core)))

    def to_x(step, zz):
        sent.append(send(block(zz, x, core), block(zz, x, core), (x_send, x_recv), step, zz, device(z, 1 - x, y, core)))

    def to_core(step, zz, xx):
        sent.append(
            send(block(zz, xx, core), block(zz, xx, core), (c_send, c_recv), step, 2 * zz + xx, device(z, x, y, 1 - core))
        )

    to_x(0, z)
    to_core(0, z, x)
    for d in range(1, depth):
        zz = lax.rem(z + depth - d, depth)
        arrival(block(zz, x, core), z_recv.at[zz]).wait_recv()
        to_x(d, zz)
        to_core(d, zz, x)
    for d in range(depth):
        zz = lax.rem(z + depth - d, depth)
        arrival(block(zz, 1 - x, core), x_recv.at[zz]).wait_recv()
        to_core(depth + d, zz, 1 - x)
    for d in range(depth):
        zz = lax.rem(z + depth - d, depth)
        arrival(block(zz, x, 1 - core), c_recv.at[2 * zz + x]).wait_recv()
        arrival(block(zz, 1 - x, 1 - core), c_recv.at[2 * zz + 1 - x]).wait_recv()
    for copy in sent:
        copy.wait_send()


def gather_rows(block):
    clips, frames = lax.axis_size("clip"), lax.axis_size("frame")
    depth, height = clips // 2, frames // 2
    sems = pltpu.SemaphoreType.DMA
    out = pl.pallas_call(
        functools.partial(gather_kernel, depth, height),
        in_specs=[pl.BlockSpec(memory_space=pl.ANY)],
        out_specs=pl.BlockSpec(memory_space=pl.ANY),
        out_shape=jax.ShapeDtypeStruct((clips, height, 2) + block.shape, block.dtype),
        scratch_shapes=[
            sems,
            sems((max(height - 1, 1),)), sems((height,)),
            sems((depth - 1,)), sems((depth,)),
            sems((depth,)), sems((depth,)),
            sems((clips,)), sems((clips,)),
        ],
        compiler_params=pltpu.CompilerParams(collective_id=0, has_side_effects=True),
        name="gather_rows",
    )(block)
    return out.reshape(-1, block.shape[1])


def reduce_kernel(depth, height, part_ref, small_ref, out_ref, out_small, *refs):
    own, from_core, to_x, from_x, to_z, from_z, to_y, from_y = refs[:8]
    low_core, low_to_x, low_x, low_to_z, low_z, low_to_y, low_y = refs[8:15]
    c_send, c_recv, x_send, x_recv, z_send, z_recv, y_send, y_recv = refs[15:23]
    lc_send, lc_recv, lx_send, lx_recv, lz_send, lz_recv, ly_send, ly_recv, local = refs[23:]
    z, x, y, core = position()
    greet(neighbours(depth, height))

    def remote(source, target, send_sem, recv_sem, to):
        return pltpu.make_async_remote_copy(
            src_ref=source, dst_ref=target, send_sem=send_sem, recv_sem=recv_sem, device_id=to, device_id_type=MESH
        )

    def away(d):
        return lax.rem(z + d, depth)

    order = list(range(1, depth)) + [0]
    core_device, x_device = device(z, x, y, 1 - core), device(z, 1 - x, y, core)
    sent = []

    def start(copy):
        copy.start()
        sent.append(copy)
        return copy

    low_c = start(remote(small_ref.at[:, :, 1 - core], low_core, lc_send, lc_recv, core_device))
    c_copies, mine = [], []
    for side in range(2):
        xx = (1 - x) if side == 0 else x
        for d in order:
            slot, block = side * depth + d, 2 * away(d) + xx
            c_copies.append(
                start(
                    remote(
                        part_ref.at[block, :, 1 - core], from_core.at[slot],
                        c_send.at[slot], c_recv.at[slot], core_device,
                    )
                )
            )
            mine.append(pltpu.make_async_copy(part_ref.at[block, :, core], own.at[slot], local.at[slot]))
            mine[-1].start()

    def pair_sum(slot):
        return own[slot].astype(F32) + from_core[slot].astype(F32)

    x_copies = []
    for n, d in enumerate(order):
        mine[n].wait()
        c_copies[n].wait_recv()
        to_x[d] = pair_sum(d).astype(BF16)
        x_copies.append(start(remote(to_x.at[d], from_x.at[d], x_send.at[d], x_recv.at[d], x_device)))
    low_c.wait_recv()
    for zz in range(depth):
        low_to_x[zz] = small_ref[2 * zz + 1 - x, :, core] + low_core[2 * zz + 1 - x]
    low_xc = start(remote(low_to_x, low_x, lx_send, lx_recv, x_device))
    for n, d in enumerate(order):
        mine[depth + n].wait()
        c_copies[depth + n].wait_recv()
        x_copies[n].wait_recv()
        total = pair_sum(depth + d) + from_x[d].astype(F32)
        if d:
            to_z[d] = total.astype(BF16)
            start(remote(to_z.at[d], from_z.at[z], z_send.at[d], z_recv.at[z], device(away(d), x, y, core)))
        else:
            from_z[z] = total.astype(BF16)
    low_xc.wait_recv()
    for d in order:
        block = 2 * away(d) + x
        total = small_ref[block, :, core] + low_core[block] + low_x[away(d)]
        if d:
            low_to_z[d] = total
            start(remote(low_to_z.at[d], low_z.at[z], lz_send.at[d], lz_recv.at[z], device(away(d), x, y, core)))
        else:
            low_z[z] = total
    for d in range(1, depth):
        zz, to = lax.rem(z + depth - d, depth), device(away(d), x, y, core)
        remote(to_z.at[d], from_z.at[zz], z_send.at[d], z_recv.at[zz], to).wait_recv()
        remote(low_to_z.at[d], low_z.at[zz], lz_send.at[d], lz_recv.at[zz], to).wait_recv()

    def over(ref, *row):
        total = ref[(0,) + row].astype(F32)
        for n in range(1, ref.shape[0]):
            total = total + ref[(n,) + row].astype(F32)
        return total

    for d in range(1, height):
        other = lax.rem(y + d, height)
        to = device(z, x, other, core)
        to_y[d] = over(from_z, other).astype(BF16)
        start(remote(to_y.at[d], from_y.at[y], y_send.at[d], y_recv.at[y], to))
        low_to_y[d] = over(low_z, other)
        start(remote(low_to_y.at[d], low_y.at[y], ly_send.at[d], ly_recv.at[y], to))
    from_y[y] = over(from_z, y).astype(BF16)
    low_y[y] = over(low_z, y)
    for d in range(1, height):
        yy, to = lax.rem(y + height - d, height), device(z, x, lax.rem(y + d, height), core)
        remote(to_y.at[d], from_y.at[yy], y_send.at[d], y_recv.at[yy], to).wait_recv()
        remote(low_to_y.at[d], low_y.at[yy], ly_send.at[d], ly_recv.at[yy], to).wait_recv()
    out_ref[...] = over(from_y)
    out_small[...] = over(low_y)
    for copy in sent:
        copy.wait_send()


def reduce_rows(block, small):
    clips, frames = lax.axis_size("clip"), lax.axis_size("frame")
    depth, height = clips // 2, frames // 2
    rows = block.shape[0] // (clips * frames)
    sems, tail, low = pltpu.SemaphoreType.DMA, (rows, block.shape[1]), (rows, small.shape[1])
    lead = (clips, height, 2)
    return pl.pallas_call(
        functools.partial(reduce_kernel, depth, height),
        in_specs=[pl.BlockSpec(memory_space=pl.ANY), pl.BlockSpec(memory_space=pltpu.VMEM)],
        out_specs=[pl.BlockSpec(memory_space=pltpu.VMEM)] * 2,
        out_shape=[jax.ShapeDtypeStruct(tail, F32), jax.ShapeDtypeStruct(low, F32)],
        scratch_shapes=[
            pltpu.VMEM((2 * depth, height) + tail, BF16),
            pltpu.VMEM((2 * depth, height) + tail, BF16),
            pltpu.VMEM((depth, height) + tail, BF16),
            pltpu.VMEM((depth, height) + tail, BF16),
            pltpu.VMEM((depth, height) + tail, BF16),
            pltpu.VMEM((depth, height) + tail, BF16),
            pltpu.VMEM((height,) + tail, BF16),
            pltpu.VMEM((height,) + tail, BF16),
            pltpu.VMEM((clips, height) + low, F32),
            pltpu.VMEM((depth, height) + low, F32),
            pltpu.VMEM((depth, height) + low, F32),
            pltpu.VMEM((depth, height) + low, F32),
            pltpu.VMEM((depth, height) + low, F32),
            pltpu.VMEM((height,) + low, F32),
            pltpu.VMEM((height,) + low, F32),
            sems((2 * depth,)), sems((2 * depth,)),
            sems((depth,)), sems((depth,)),
            sems((depth,)), sems((depth,)),
            sems((height,)), sems((height,)),
            sems, sems,
            sems, sems,
            sems((depth,)), sems((depth,)),
            sems((height,)), sems((height,)),
            sems((2 * depth,)),
        ],
        compiler_params=pltpu.CompilerParams(
            collective_id=1, has_side_effects=True, vmem_limit_bytes=60 << 20
        ),
        name="reduce_rows",
    )(block.reshape(lead + tail), small.reshape(lead + low))


def gather(block):
    return lax.all_gather(block, AXES, axis=0, tiled=True)


def scatter(block):
    return lax.psum_scatter(block, AXES, scatter_dimension=0, tiled=True)


def shards(
    clips_in, teacher, valid, norm_gain, norm_shift, w_space, qv_bias, w_space_out, mix_bias,
    w_time, w_time_out, w_up, up_bias, w_down,
):
    batch, frames, places, _ = clips_in.shape
    ring = lax.axis_size("frame")
    pieces = ring // batch
    chunk = places // pieces
    all_frames = ring * frames
    me = lax.axis_index("frame")
    depth = w_up.shape[0]

    def swap(block, step):
        if step == 0:
            return block
        return lax.ppermute(block, "frame", [(i, i ^ step) for i in range(ring)])

    def clip_of(step):
        return (me // pieces) ^ (step // pieces)

    def place_of(step):
        return ((me % pieces) ^ (step % pieces)) * chunk

    def cut(block, step):
        if pieces == 1:
            return block
        return lax.dynamic_slice_in_dim(block, place_of(step), chunk, 0)

    def spread(block):
        got = []
        for step in range(ring):
            mine = lax.dynamic_index_in_dim(block, clip_of(step), 0, keepdims=False)
            got.append(swap(cut(jnp.swapaxes(mine, 0, 1), step), step))
        return got

    many = FF // D
    count = jnp.sum(valid)
    counts = jnp.stack([count // 256, count % 256]).astype(BF16)
    smalls = jnp.concatenate(
        [
            norm_gain, norm_shift, qv_bias, mix_bias, up_bias.reshape(depth, many),
            jnp.broadcast_to(counts[None], (depth, 2)),
        ],
        1,
    )
    smalls = jnp.pad(smalls, ((0, 0), (0, SMALL - smalls.shape[1])))
    first = gather_rows(jnp.concatenate([w_space, w_space_out, smalls], 1))
    up_turned = jnp.swapaxes(w_up.reshape(depth, D, many), 1, 2).reshape(depth, FF)
    rest = gather(jnp.concatenate([w_time, w_time_out, up_turned, w_down.reshape(depth, FF)], 1))
    table = jnp.swapaxes(first[:, 4 * D : 4 * D + 24].astype(F32), 0, 1)
    up_row = table[UP : UP + many].reshape(1, FF)
    counted = table[UP + many : UP + many + 2, ::depth]
    total_count = jnp.sum(counted[0]) * 256.0 + jnp.sum(counted[1])
    scale = (2.0 / (total_count * D)).reshape(1, 1)
    table = table[:16]

    order = [((me // pieces) ^ j).astype(jnp.int32) for j in range(batch)]
    clip_ids = [jnp.reshape(c, (1,)) for c in order]
    valid_column = jnp.concatenate(spread(valid), 1).reshape(-1, 1).astype(F32)
    saved, sent = [None] * batch, [None] * ring
    for j in list(range(batch))[::-1]:
        *kept_j, after = space_forward(clip_ids[j], clips_in, table, first)
        saved[j] = kept_j
        after = jnp.swapaxes(after, 0, 1)
        for r in range(pieces):
            step = j * pieces + r
            sent[step] = swap(cut(after, step), step)
        if j == batch // 2:
            teacher, after = lax.optimization_barrier((teacher, after))

    teachers = spread(teacher)
    *saved_b, after_b = time_forward(sent, table, rest)
    tile, _ = time_tiles(chunk, all_frames)
    layer_parts, grad_b, d_feed, rows_c, bias_up, squares = feed_forward(
        after_b, teachers, valid_column, scale, table, up_row, rest, tile
    )
    squares = jnp.broadcast_to(jnp.sum(squares).reshape(1, 1), (1, D))
    grad_parts, d_rest, rows_b = time_back(grad_b, saved_b, sent, table, rest, d_feed)
    d_rest = scatter(d_rest)
    d_time, d_feed = d_rest[:, : 4 * D], d_rest[:, 4 * D :]
    grad_parts = [swap(part, step) for step, part in enumerate(grad_parts)]
    grad_parts[-1], layer_parts = lax.optimization_barrier((grad_parts[-1], layer_parts))
    layer_parts = [swap(part, step) for step, part in enumerate(layer_parts)]

    def join(parts, j):
        if pieces == 1:
            return parts[j]
        whole = jnp.zeros((places, frames, D), BF16)
        for r in range(pieces):
            step = j * pieces + r
            whole = lax.dynamic_update_slice_in_dim(whole, parts[step], place_of(step), 0)
        return whole

    projs, outs, biases, rows_a, input_grad = [], [], [], [], None
    for j in range(batch):
        grad = jnp.swapaxes(join(grad_parts, j), 0, 1)
        proj, d_out, bias = space_back(grad, saved[j][1:], first)
        projs.append(proj)
        outs.append(d_out)
        biases.append(bias)
        input_grad, rows = input_grads(clip_ids[j], grad, proj, clips_in, table, first, input_grad)
        rows_a.append(rows)
    d_space, sums_a = space_weights([kept_j[0] for kept_j in saved], projs, outs)
    rows_a, biases = sum(rows_a), sum(biases)
    columns = as_columns(
        [
            rows_a[0:1], rows_b[0:1], rows_c[0:1],
            rows_a[1:2], rows_b[1:2], rows_c[1:2],
            sums_a[:, :D], sums_a[:, 2 * D :], rows_b[3:4], rows_b[2:3],
            biases, rows_b[4:5], rows_c[2:3],
            bias_up.reshape(many, D), squares,
        ]
    )
    d_space, here = reduce_rows(d_space, columns)
    layer_out = place_clips(jnp.stack(order), [join(layer_parts, j) for j in range(batch)])
    d_up = jnp.swapaxes(d_feed[:, :FF].reshape(depth, many, D), 1, 2).reshape(depth, FF)
    return (
        jnp.swapaxes(layer_out, 1, 2),
        here[0, 13 + many] / (total_count * D),
        input_grad,
        here[:, 0:3],
        here[:, 3:6],
        d_space[:, : 3 * D],
        here[:, 6:9],
        here[:, 9],
        d_space[:, 3 * D : 4 * D],
        here[:, 10:13],
        d_time[:, : 3 * D].astype(F32),
        d_time[:, 3 * D :].astype(F32),
        d_up.astype(F32),
        here[:, 13 : 13 + many].reshape(-1),
        d_feed[:, FF:].reshape(-1, D).astype(F32),
    )


def solution(mesh):
    tokens, rows = P("clip", "frame", None, None), P(AXES, None)
    in_specs = (tokens, tokens, P("clip", "frame", None)) + (rows,) * 9 + (P(AXES), rows)
    out_specs = (
        (tokens, P(), tokens, rows, rows, rows, rows, P(AXES)) + (rows,) * 5 + (P(AXES), rows)
    )
    return jax.shard_map(shards, mesh=mesh, in_specs=in_specs, out_specs=out_specs, check_vma=False)
```

```python
import functools

import jax
import jax.numpy as jnp
from jax import lax
from jax.experimental import pallas as pl
from jax.experimental.pallas import tpu as pltpu
from jax.sharding import PartitionSpec as P

D = 768
HEADS = 12
HEAD = 64
FF = 3072
EPS = 1e-06
F32 = jnp.float32
BF16 = jnp.bfloat16
PARAMS = pltpu.CompilerParams(vmem_limit_bytes=60 << 20)


def cost(flops, moved=0):
    return pl.CostEstimate(flops=int(flops) // 16, bytes_accessed=int(moved), transcendentals=0)


GAIN, SHIFT, QV, MIX, UP = 0, 3, 6, 10, 13


def dot(left, right):
    return jnp.dot(left, right, preferred_element_type=F32)


def dot_nt(left, right):
    return lax.dot_general(left, right, (((1,), (1,)), ((), ())), preferred_element_type=F32)


def dot_tn(left, right):
    return lax.dot_general(left, right, (((0,), (0,)), ((), ())), preferred_element_type=F32)


def normalize(rows):
    center = rows - jnp.mean(rows, -1, keepdims=True)
    inverse = lax.rsqrt(jnp.mean(center * center, -1, keepdims=True) + EPS)
    return center * inverse, inverse


def normalize_back(grad_out, hat, inverse, gain):
    grad_hat = grad_out * gain
    return inverse * (
        grad_hat
        - jnp.mean(grad_hat, -1, keepdims=True)
        - hat * jnp.mean(grad_hat * hat, -1, keepdims=True)
    )


def column_sum(rows):
    return jnp.sum(rows, 0, keepdims=True)


def first_lanes(shape):
    return lax.broadcasted_iota(jnp.int32, shape, 1) < HEAD


def halves(block):
    low = first_lanes(block.shape)
    zero = jnp.zeros_like(block)
    return jnp.where(low, block, zero), jnp.where(low, zero, block)


def pair(index):
    return slice(2 * HEAD * index, 2 * HEAD * (index + 1))


def grow(block, rows):
    if rows == block.shape[0]:
        return block
    return jnp.concatenate([block, jnp.zeros((rows - block.shape[0], block.shape[1]), block.dtype)], 0)


def stack(block):
    return jnp.concatenate(halves(block), 0)


def merge(two):
    rows = two.shape[0] // 2
    return jnp.where(first_lanes((rows, two.shape[1])), two[:rows], two[rows:])


def kept(rows):
    return HEADS // 2, 2 * padded(rows), rows


def padded(rows):
    return -(-rows // 16) * 16


def attention(units, rows, frames=None):
    full = padded(rows)
    place = lax.broadcasted_iota(jnp.int32, (full, rows), 0)
    if frames is not None:
        mask = place // frames == lax.broadcasted_iota(jnp.int32, (full, rows), 1) // frames
    else:
        mask = place < rows

    def score(unit):
        return dot_nt(stack(grow(unit[1](), full)), unit[0]())

    scores = score(units[0])
    for n, (_, _, value, keep_probs, keep_mix) in enumerate(units):
        now = scores
        if n + 1 < len(units):
            scores = score(units[n + 1])
        probs = []
        for one in (now[:full], now[full:]):
            one = jnp.where(mask, one, -1e30)
            expo = jnp.exp(one - jnp.max(one, 0, keepdims=True))
            probs.append((expo * (1.0 / column_sum(expo))).astype(BF16))
        probs = jnp.concatenate(probs, 0)
        keep_probs(probs)
        keep_mix(dot_tn(probs, stack(grow(value(), full))).astype(BF16))


def attention_back(units, rows):
    full = padded(rows)

    def probs_grad(unit):
        return dot_nt(stack(grow(unit[2](), full)), unit[3]())

    grad_p = probs_grad(units[0])
    for n, (query, key, _, grad_mix, probs_of, keep) in enumerate(units):
        probs = probs_of()
        wide = probs.astype(F32)
        term = wide * grad_p
        grad_s = []
        for head in (slice(0, full), slice(full, 2 * full)):
            grad_s.append((term[head] - wide[head] * column_sum(term[head])).astype(BF16))
        grad_s = jnp.concatenate(grad_s, 0)
        if n + 1 < len(units):
            grad_p = probs_grad(units[n + 1])
        to_v = merge(dot(probs, grad_mix()))
        to_k = merge(dot(grad_s, query()))
        to_q = dot_tn(grad_s, stack(grow(key(), full)))
        keep((to_q * HEAD ** (-0.5)).astype(BF16), to_k[:rows].astype(BF16), to_v[:rows].astype(BF16))


def reader(ref, *index):
    return lambda: ref[index]


def writer(ref, *index):
    def write(value):
        ref[index] = value

    return write


def writer3(ref, lead, rows, p):
    def write(*values):
        for n, value in enumerate(values):
            ref[lead + (rows, pair(n * HEADS // 2 + p))] = value

    return write


def project(rows, weights, table, query_row):
    proj = dot(rows, weights)
    query = (proj[:, :D] + table[query_row : query_row + 1, :]).astype(BF16)
    key = proj[:, D : 2 * D].astype(BF16)
    value = (proj[:, 2 * D :] + table[query_row + 1 : query_row + 2, :]).astype(BF16)
    return (query.astype(F32) * HEAD ** (-0.5)).astype(BF16), key, value


def fixed(shape):
    return pl.BlockSpec(shape, lambda *_: (0,) * len(shape), pipeline_mode=pl.Buffered(1))


def columns_of(width, index):
    return pl.BlockSpec((D, width), lambda *_: (0, index), pipeline_mode=pl.Buffered(1))


def collect(refs, scratch):
    frames = refs[0].shape[1]
    for n, ref in enumerate(refs):
        scratch[:, n * frames : (n + 1) * frames, :] = ref[...].astype(F32)
    return scratch[...].reshape(-1, D)


def deal(rows, scratch, refs):
    frames = refs[0].shape[1]
    scratch[...] = rows.reshape(scratch.shape)
    for n, ref in enumerate(refs):
        ref[...] = scratch[:, n * frames : (n + 1) * frames, :].astype(BF16)


def clear(first, *refs):
    @pl.when(first)
    def _():
        for ref in refs:
            ref[...] = jnp.zeros_like(ref)


def put_rows(ref, value):
    rows, full = value.shape[0], ref.shape[0]
    ref[:rows, :] = value
    if full > rows:
        ref[rows:, :] = jnp.zeros((full - rows, value.shape[1]), value.dtype)


def space_kernel(clip, x_ref, table, w_ref, *refs):
    in_ref, q_ref, k_ref, v_ref, mix_ref, p_ref, out_ref = refs[-7:]
    rows = x_ref[0, 0].astype(F32)
    hat, _ = normalize(rows)
    normed = (hat * table[GAIN : GAIN + 1, :] + table[SHIFT : SHIFT + 1, :]).astype(BF16)
    put_rows(in_ref.at[0, 0], normed)
    q_ref[0], k_ref[0], v_ref[0] = project(normed, w_ref[:, : 3 * D], table, QV)
    every = slice(None)
    attention(
        [
            tuple(reader(ref, 0, every, pair(p)) for ref in (q_ref, k_ref, v_ref))
            + (writer(p_ref, 0, p), writer(mix_ref, 0, every, pair(p)))
            for p in range(HEADS // 2)
        ],
        rows.shape[0],
    )
    after = rows + dot(mix_ref[0], w_ref[:, 3 * D : 4 * D]) + table[MIX : MIX + 1, :]
    out_ref[0] = after.astype(BF16)


def space_forward(clip, step, inputs, table, weights, before):
    batch, frames, places, _ = inputs.shape
    full = padded(places)
    more = [] if before is None else [before]

    def frame(*tail):
        return pl.BlockSpec((1,) + tail, lambda i, c: (i,) + (0,) * len(tail))

    def shape(*tail):
        return jax.ShapeDtypeStruct((frames,) + tail, BF16)

    return pl.pallas_call(
        space_kernel,
        grid_spec=pltpu.PrefetchScalarGridSpec(
            num_scalar_prefetch=1,
            grid=(frames,),
            in_specs=[
                pl.BlockSpec((1, 1, places, D), lambda i, c: (c[0], i, 0, 0)),
                fixed(table.shape),
                columns_of(4 * D, 0),
            ]
            + [pl.BlockSpec(memory_space=pl.ANY) for _ in more],
            out_specs=[pl.BlockSpec((1, 1, full, D), lambda i, c: (step, i, 0, 0))]
            + [frame(places, D)] * 4
            + [frame(*kept(places)), frame(places, D)],
        ),
        out_shape=[jax.ShapeDtypeStruct((batch, frames, full, D), BF16)]
        + [shape(places, D)] * 4
        + [shape(*kept(places)), shape(places, D)],
        input_output_aliases={4: 0} if more else {},
        compiler_params=PARAMS,
        cost_estimate=cost(24 * frames * places * D * D),
        name="space_forward",
    )(clip, inputs, table, weights, *more)


def largest_divisor(number, limit):
    return max(n for n in range(1, limit + 1) if number % n == 0)


def time_kernel(frames, group, ring, *refs):
    parts, (table, w_ref) = refs[:ring], refs[ring : ring + 2]
    a_ref, in_ref, q_ref, k_ref, v_ref, mix_ref, p_ref, out_ref, scratch = refs[ring + 2 :]
    rows = collect(parts, scratch)
    a_ref[...] = rows.astype(BF16)
    hat, _ = normalize(rows)
    normed = (hat * table[GAIN + 1 : GAIN + 2, :] + table[SHIFT + 1 : SHIFT + 2, :]).astype(BF16)
    in_ref[...] = normed
    q_ref[...], k_ref[...], v_ref[...] = project(normed, w_ref[:, : 3 * D], table, QV + 2)
    units = []
    for g in range(rows.shape[0] // group):
        span = slice(g * group, (g + 1) * group)
        for p in range(HEADS // 2):
            units.append(
                tuple(reader(ref, span, pair(p)) for ref in (q_ref, k_ref, v_ref))
                + (writer(p_ref, g, p), writer(mix_ref, span, pair(p)))
            )
    attention(units, group, frames)
    out_ref[...] = rows + dot(mix_ref[...], w_ref[:, 3 * D :]) + table[MIX + 1 : MIX + 2, :]


def time_tiles(places, frames):
    per_group = largest_divisor(places, 128 // frames)
    per_tile = per_group * largest_divisor(places // per_group, 4)
    return per_tile * frames, per_group * frames


def piece_specs(parts, tile):
    frames = parts[0].shape[1]
    places = tile // (frames * len(parts))
    return [pl.BlockSpec((places, frames, D), lambda i: (i, 0, 0))] * len(parts)


def join_scratch(parts, tile):
    frames = parts[0].shape[1] * len(parts)
    return pltpu.VMEM((tile // frames, frames, D), F32)


def time_forward(parts, table, weights):
    places, frames = parts[0].shape[0], parts[0].shape[1] * len(parts)
    tokens = places * frames
    tile, group = time_tiles(places, frames)
    rows = pl.BlockSpec((tile, D), lambda i: (i, 0))
    return pl.pallas_call(
        functools.partial(time_kernel, frames, group, len(parts)),
        grid=(tokens // tile,),
        in_specs=piece_specs(parts, tile) + [fixed(table.shape), columns_of(4 * D, 0)],
        out_specs=[rows] * 6
        + [pl.BlockSpec((tile // group,) + kept(group), lambda i: (i, 0, 0, 0)), rows],
        out_shape=[jax.ShapeDtypeStruct((tokens, D), BF16)] * 6
        + [
            jax.ShapeDtypeStruct((tokens // group,) + kept(group), BF16),
            jax.ShapeDtypeStruct((tokens, D), F32),
        ],
        scratch_shapes=[join_scratch(parts, tile)],
        compiler_params=PARAMS,
        cost_estimate=cost(24 * tokens * D * D),
        name="time_forward",
    )(*parts, table, weights)


def gelu_parts(u):
    area = 0.5 + 0.5 * lax.erf(u * 0.7071067811865476)
    bell = jnp.exp2((-0.5 * 1.4426950408889634) * (u * u))
    return u * area, area + 0.3989422804014327 * (u * bell)


FF_CHUNK = 768


def feed_kernel(ring, *refs):
    teachers, refs = refs[:ring], refs[ring:]
    (a_ref, valid_ref, scale_ref, table, up_bias, up_ref, down_ref), refs = refs[:7], refs[7:]
    outs, refs = refs[:ring], refs[ring:]
    g_ref, d_ref, rows_ref, bias_ref, square_ref, hidden, slope, d_up, d_down, stage, sems, scratch = refs
    step, last = pl.program_id(0), pl.num_programs(0) - 1
    clear(step == 0, d_up, d_down, rows_ref, bias_ref, square_ref)
    after = a_ref[...]
    hat, inverse = normalize(after)
    normed = (hat * table[GAIN + 2 : GAIN + 3, :] + table[SHIFT + 2 : SHIFT + 3, :]).astype(BF16)
    total = after + table[MIX + 2 : MIX + 3, :]
    chunks = [slice(c, c + FF_CHUNK) for c in range(0, FF, FF_CHUNK)]
    for c in chunks:
        act, rise = gelu_parts(dot(normed, up_ref[:, c]) + up_bias[:, c])
        act = act.astype(BF16)
        hidden[:, c] = act
        slope[:, c] = rise.astype(BF16)
        total = total + dot(act, down_ref[:, c])
    deal(total, scratch, outs)
    diff = (total - collect(teachers, scratch)) * valid_ref[...]
    square_ref[...] += column_sum(diff * diff)
    grad = diff * scale_ref[0, 0]
    grad_low = grad.astype(BF16)
    bias_c = column_sum(grad_low.astype(F32))
    back = jnp.zeros_like(grad)
    for c in chunks:
        grad_pre = dot_nt(grad_low, down_ref[:, c]) * slope[:, c].astype(F32)
        grad_pre = grad_pre.astype(BF16)
        bias_ref[:, c] += column_sum(grad_pre.astype(F32))
        d_down[:, c] += dot_tn(hidden[:, c], grad_low)
        d_up[:, c] += dot_tn(normed, grad_pre)
        back = back + dot_nt(grad_pre, up_ref[:, c])
    rows_ref[...] += jnp.concatenate([column_sum(back * hat), column_sum(back), bias_c], 0)
    g_ref[...] = grad + normalize_back(back, hat, inverse, table[GAIN + 2 : GAIN + 3, :])

    @pl.when(step == last)
    def _():
        moves = []
        for source, start in ((d_up, 4 * D), (d_down, 4 * D + FF)):
            moves += [(source.at[:, c], d_ref.at[:, start + c.start : start + c.stop]) for c in chunks]
        flush(moves, stage, sems)


def flush(moves, stage, sems):
    copies = []
    for i, (source, target) in enumerate(moves):
        if i >= 2:
            copies[i - 2].wait()
        stage[i % 2] = source[...].astype(BF16)
        copies.append(pltpu.make_async_copy(stage.at[i % 2], target, sems.at[i % 2]))
        copies[i].start()
    for copy in copies[-2:]:
        copy.wait()


def feed_forward(after_b, teachers, valid, scale, table, up_bias, weights, tile):
    tokens, ring = after_b.shape[0], len(teachers)
    rows = pl.BlockSpec((tile, D), lambda i: (i, 0))
    *outs, grad, d_feed, sums, bias, squares = pl.pallas_call(
        functools.partial(feed_kernel, ring),
        grid=(tokens // tile,),
        in_specs=piece_specs(teachers, tile)
        + [
            rows,
            pl.BlockSpec((tile, 1), lambda i: (i, 0)),
            pl.BlockSpec(memory_space=pltpu.SMEM),
            fixed(table.shape),
            fixed((1, FF)),
            columns_of(FF, 0),
            columns_of(FF, 1),
        ],
        out_specs=piece_specs(teachers, tile)
        + [rows, pl.BlockSpec(memory_space=pl.ANY), fixed((3, D)), fixed((1, FF)), fixed((1, D))],
        out_shape=[jax.ShapeDtypeStruct(t.shape, BF16) for t in teachers]
        + [
            jax.ShapeDtypeStruct((tokens, D), F32),
            jax.ShapeDtypeStruct((D, 4 * D + 2 * FF), BF16),
            jax.ShapeDtypeStruct((3, D), F32),
            jax.ShapeDtypeStruct((1, FF), F32),
            jax.ShapeDtypeStruct((1, D), F32),
        ],
        scratch_shapes=[
            pltpu.VMEM((tile, FF), BF16),
            pltpu.VMEM((tile, FF), BF16),
            pltpu.VMEM((D, FF), F32),
            pltpu.VMEM((D, FF), F32),
            pltpu.VMEM((2, D, FF_CHUNK), BF16),
            pltpu.SemaphoreType.DMA((2,)),
            join_scratch(teachers, tile),
        ],
        compiler_params=PARAMS,
        cost_estimate=cost(80 * tokens * D * D),
        name="feed_forward",
    )(*teachers, after_b, valid, scale, table, up_bias, weights, weights)
    return outs, grad, d_feed, sums, bias, squares


def time_back_kernel(group, ring, *refs):
    (g_ref, a_ref, in_ref, q_ref, k_ref, v_ref, mix_ref, p_ref, table, w_ref), refs = refs[:10], refs[11:]
    outs, refs = refs[:ring], refs[ring:]
    d_ref, rows_ref, grad_mix, grad_proj, d_proj, d_out, stage, sems, scratch = refs
    step, last = pl.program_id(0), pl.num_programs(0) - 1
    clear(step == 0, d_proj, d_out, rows_ref)
    grad = g_ref[...]
    grad_low = grad.astype(BF16)
    d_out[...] += dot_tn(mix_ref[...], grad_low)
    grad_mix[...] = dot_nt(grad_low, w_ref[:, 3 * D :]).astype(BF16)

    units = []
    for g in range(grad.shape[0] // group):
        span = slice(g * group, (g + 1) * group)
        for p in range(HEADS // 2):
            units.append(
                tuple(reader(ref, span, pair(p)) for ref in (q_ref, k_ref, v_ref, grad_mix))
                + (reader(p_ref, g, p), writer3(grad_proj, (), span, p))
            )
    attention_back(units, group)
    proj = grad_proj[...]
    d_proj[...] += dot_tn(in_ref[...], proj)
    sums = column_sum(proj.astype(F32))
    back = dot_nt(proj, w_ref[:, : 3 * D])
    hat, inverse = normalize(a_ref[...].astype(F32))
    rows_ref[...] += jnp.concatenate(
        [
            column_sum(back * hat),
            column_sum(back),
            sums[:, :D],
            sums[:, 2 * D :],
            column_sum(grad_low.astype(F32)),
        ],
        0,
    )
    deal(grad + normalize_back(back, hat, inverse, table[GAIN + 1 : GAIN + 2, :]), scratch, outs)

    @pl.when(step == last)
    def _():
        moves = [(d_proj.at[:, pl.ds(c * D, D)], d_ref.at[:, pl.ds(c * D, D)]) for c in range(3)]
        flush(moves + [(d_out, d_ref.at[:, pl.ds(3 * D, D)])], stage, sems)


def time_back(grad, saved, like, table, weights, matrix):
    ring, tokens = len(like), grad.shape[0]
    places, frames = like[0].shape[0], like[0].shape[1] * ring
    tile, group = time_tiles(places, frames)
    rows = pl.BlockSpec((tile, D), lambda i: (i, 0))
    *outs, d_time, sums = pl.pallas_call(
        functools.partial(time_back_kernel, group, ring),
        grid=(tokens // tile,),
        in_specs=[rows] * 7
        + [
            pl.BlockSpec((tile // group,) + kept(group), lambda i: (i, 0, 0, 0)),
            fixed(table.shape),
            columns_of(4 * D, 0),
            pl.BlockSpec(memory_space=pl.ANY),
        ],
        out_specs=piece_specs(like, tile) + [pl.BlockSpec(memory_space=pl.ANY), fixed((5, D))],
        out_shape=[jax.ShapeDtypeStruct(t.shape, BF16) for t in like]
        + [jax.ShapeDtypeStruct(matrix.shape, BF16), jax.ShapeDtypeStruct((5, D), F32)],
        input_output_aliases={10: ring},
        scratch_shapes=[
            pltpu.VMEM((tile, D), BF16),
            pltpu.VMEM((tile, 3 * D), BF16),
            pltpu.VMEM((D, 3 * D), F32),
            pltpu.VMEM((D, D), F32),
            pltpu.VMEM((2, D, D), BF16),
            pltpu.SemaphoreType.DMA((2,)),
            join_scratch(like, tile),
        ],
        compiler_params=PARAMS,
        cost_estimate=cost(42 * tokens * D * D),
        name="time_back",
    )(grad, *saved, table, weights, matrix)
    return outs, d_time, sums


def space_back_kernel(g_ref, q_ref, k_ref, v_ref, mix_ref, p_ref, w_ref, *refs):
    out_ref, d_ref, bias_ref, grad_mix = refs[-4:]
    clear(pl.program_id(0) == 0, d_ref, bias_ref)
    grad = g_ref[0]
    rows, full = grad.shape[0], out_ref.shape[2]
    d_ref[...] += dot_tn(mix_ref[0], grad)
    bias_ref[...] += column_sum(grad.astype(F32))
    grad_mix[...] = dot_nt(grad, w_ref[...]).astype(BF16)
    every = slice(None)
    attention_back(
        [
            tuple(reader(ref, 0, every, pair(p)) for ref in (q_ref, k_ref, v_ref))
            + (reader(grad_mix, every, pair(p)), reader(p_ref, 0, p))
            + (writer3(out_ref, (0, 0), slice(0, rows), p),)
            for p in range(HEADS // 2)
        ],
        rows,
    )
    if full > rows:
        out_ref[0, 0, rows:, :] = jnp.zeros((full - rows, out_ref.shape[3]), BF16)


def space_back(grad, step, batch, saved, weights, before):
    frames, places, _ = grad.shape
    full = padded(places)
    more = [] if before is None else [before]

    def frame(*tail):
        return pl.BlockSpec((1,) + tail, lambda i: (i,) + (0,) * len(tail))

    return pl.pallas_call(
        space_back_kernel,
        grid=(frames,),
        in_specs=[frame(places, D)] * 5
        + [frame(*kept(places)), columns_of(D, 3)]
        + [pl.BlockSpec(memory_space=pl.ANY) for _ in more],
        out_specs=[
            pl.BlockSpec((1, 1, full, 3 * D), lambda i: (step, i, 0, 0)),
            fixed((D, D)),
            fixed((1, D)),
        ],
        out_shape=[
            jax.ShapeDtypeStruct((batch, frames, full, 3 * D), BF16),
            jax.ShapeDtypeStruct((D, D), F32),
            jax.ShapeDtypeStruct((1, D), F32),
        ],
        scratch_shapes=[pltpu.VMEM((places, D), BF16)],
        input_output_aliases={7: 0} if more else {},
        compiler_params=PARAMS,
        cost_estimate=cost(24 * frames * places * D * D),
        name="space_back",
    )(grad, *saved, weights, *more)


SMALL = 128


def space_weight_kernel(parts, in_ref, proj_ref, w_ref, table, c_ref, b_ref, up_ref, square_ref, *refs):
    outs, biases, refs = refs[:parts], refs[parts : 2 * parts], refs[2 * parts :]
    d_ref, small_ref, d_proj, d_out, sums, rows, stage, sems = refs
    step, last = pl.program_id(0), pl.num_programs(0) - 1
    clear(step == 0, d_proj, sums, rows)
    proj = proj_ref[0].reshape(-1, 3 * D)
    d_proj[...] += dot_tn(in_ref[0].reshape(-1, D), proj)
    sums[...] += column_sum(proj.astype(F32))

    @pl.when(step == last)
    def _():
        d_out[...] = sum(ref[...] for ref in outs)
        moves = [(d_proj.at[:, pl.ds(c * D, D)], d_ref.at[:, pl.ds(c * D, D)]) for c in range(3)]
        flush(moves + [(d_out, d_ref.at[:, pl.ds(3 * D, D)])], stage, sems)
        many = up_ref.shape[0]
        rows[1:2, :], rows[2:3, :] = b_ref[0:1, :], c_ref[0:1, :]
        rows[4:5, :], rows[5:6, :] = b_ref[1:2, :], c_ref[1:2, :]
        rows[6:7, :], rows[7:8, :] = sums[:, :D], sums[:, 2 * D :]
        rows[8:9, :], rows[9:10, :] = b_ref[3:4, :], b_ref[2:3, :]
        rows[10:11, :] = sum(ref[...] for ref in biases)
        rows[11:12, :], rows[12:13, :] = b_ref[4:5, :], c_ref[2:3, :]
        rows[13 : 13 + many, :] = up_ref[...]
        square = jnp.sum(square_ref[...], -1, keepdims=True)
        rows[13 + many : 14 + many, :] = jnp.broadcast_to(square, square_ref.shape)
        rows[SMALL - 2 : SMALL - 1, :] = table[GAIN : GAIN + 1, :]
        rows[SMALL - 1 : SMALL, :] = table[SHIFT : SHIFT + 1, :]
        columns = jnp.swapaxes(rows[...], 0, 1)
        wide = w_ref[...].astype(F32)
        with_grad = jnp.sum(wide * d_proj[...], -1, keepdims=True)
        shift_grad = jnp.sum(wide * sums[...], -1, keepdims=True)
        gain, shift = columns[:, SMALL - 2 : SMALL - 1], columns[:, SMALL - 1 :]
        gain_grad = (with_grad - shift * shift_grad) / gain
        lane = lax.broadcasted_iota(jnp.int32, columns.shape, 1)
        small_ref[...] = jnp.where(lane == 0, gain_grad, jnp.where(lane == 3, shift_grad, columns))


def space_weights(ins, projs, weights, table, rows_c, rows_b, bias_up, squares, outs, biases):
    batch, frames, full, _ = ins.shape

    def clip(width):
        return pl.BlockSpec((1, frames, full, width), lambda i: (i, 0, 0, 0))

    smalls = [table, rows_c, rows_b, bias_up, squares]
    return pl.pallas_call(
        functools.partial(space_weight_kernel, batch),
        grid=(batch,),
        in_specs=[clip(D), clip(3 * D), columns_of(3 * D, 0)]
        + [fixed(a.shape) for a in smalls]
        + [fixed((D, D))] * batch
        + [fixed((1, D))] * batch,
        out_specs=[pl.BlockSpec(memory_space=pl.ANY), fixed((D, SMALL))],
        out_shape=[jax.ShapeDtypeStruct((D, 4 * D), BF16), jax.ShapeDtypeStruct((D, SMALL), F32)],
        scratch_shapes=[
            pltpu.VMEM((D, 3 * D), F32),
            pltpu.VMEM((D, D), F32),
            pltpu.VMEM((1, 3 * D), F32),
            pltpu.VMEM((SMALL, D), F32),
            pltpu.VMEM((2, D, D), BF16),
            pltpu.SemaphoreType.DMA((2,)),
        ],
        compiler_params=PARAMS,
        cost_estimate=cost(18 * batch * frames * full * D * D),
        name="space_weights",
    )(ins, projs, weights, *smalls, *outs, *biases)


def input_kernel(clip, g_ref, p_ref, x_ref, table, w_ref, *refs):
    out_ref = refs[-1]
    back = dot_nt(p_ref[0, 0, : g_ref.shape[1], :], w_ref[...])
    hat, inverse = normalize(x_ref[0, 0].astype(F32))
    grad = g_ref[0].astype(F32) + normalize_back(back, hat, inverse, table[GAIN : GAIN + 1, :])
    out_ref[0, 0] = grad.astype(BF16)


def input_grads(clip, step, grad, projs, inputs, table, weights, before):
    frames, places, _ = grad.shape
    block = pl.BlockSpec((1, 1, places, D), lambda i, c: (c[0], i, 0, 0))
    more = [] if before is None else [before]
    return pl.pallas_call(
        input_kernel,
        grid_spec=pltpu.PrefetchScalarGridSpec(
            num_scalar_prefetch=1,
            grid=(frames,),
            in_specs=[
                pl.BlockSpec((1, places, D), lambda i, c: (i, 0, 0)),
                pl.BlockSpec((1, 1) + projs.shape[2:], lambda i, c: (step, i, 0, 0)),
                block,
                fixed(table.shape),
                columns_of(3 * D, 0),
            ]
            + [pl.BlockSpec(memory_space=pl.ANY) for _ in more],
            out_specs=block,
        ),
        out_shape=jax.ShapeDtypeStruct(inputs.shape, BF16),
        input_output_aliases={6: 0} if more else {},
        compiler_params=PARAMS,
        cost_estimate=cost(18 * frames * places * D * D),
        name="input_grads",
    )(clip, grad, projs, inputs, table, weights, *more)


def place_kernel(order, *refs):
    blocks, out_ref = refs[:-1], refs[-1]
    for n, ref in enumerate(blocks):

        @pl.when(pl.program_id(0) == n)
        def _():
            out_ref[0] = ref[...]


def place_clips(order, blocks):
    shape = blocks[0].shape
    return pl.pallas_call(
        place_kernel,
        grid_spec=pltpu.PrefetchScalarGridSpec(
            num_scalar_prefetch=1,
            grid=(len(blocks),),
            in_specs=[fixed(shape)] * len(blocks),
            out_specs=pl.BlockSpec((1,) + shape, lambda i, order: (order[i], 0, 0, 0)),
        ),
        out_shape=jax.ShapeDtypeStruct((len(blocks),) + shape, BF16),
        compiler_params=PARAMS,
        name="place_clips",
    )(order, *blocks)


AXES = ("clip", "frame")
MESH = pl.DeviceIdType.MESH


def position():
    clip, frame = lax.axis_index("clip"), lax.axis_index("frame")
    return clip // 2, clip % 2, frame // 2, frame % 2


def device(z, x, y, core):
    return (2 * z + x, 2 * y + core)


def greet(partners):
    barrier = pltpu.get_barrier_semaphore()
    for partner in partners:
        pl.semaphore_signal(barrier, inc=1, device_id=partner, device_id_type=MESH)
    pl.semaphore_wait(barrier, len(partners))


def neighbours(depth, height):
    z, x, y, core = position()
    return (
        [device(lax.rem(z + d, depth), x, y, core) for d in range(1, depth)]
        + [device(z, x, lax.rem(y + d, height), core) for d in range(1, height)]
        + [device(z, 1 - x, y, core), device(z, x, y, 1 - core)]
    )


def gather_kernel(depth, height, in_ref, out_ref, local, y_send, y_recv, z_send, z_recv, x_send, x_recv, c_send, c_recv):
    z, x, y, core = position()
    greet(neighbours(depth, height))

    def send(source, target, sems, slot, index, to):
        copy = pltpu.make_async_remote_copy(
            src_ref=source, dst_ref=target, send_sem=sems[0].at[slot], recv_sem=sems[1].at[index],
            device_id=to, device_id_type=MESH,
        )
        copy.start()
        return copy

    def block(zz, xx, cc):
        return out_ref.at[2 * zz + xx, :, cc]

    def arrival(ref, sem):
        return pltpu.make_async_remote_copy(
            src_ref=ref, dst_ref=ref, send_sem=sem, recv_sem=sem, device_id=device(z, 1 - x, y, core), device_id_type=MESH
        )

    sent = []
    own = out_ref.at[2 * z + x, y, core]
    for d in range(1, height):
        sent.append(send(in_ref, own, (y_send, y_recv), d - 1, y, device(z, x, lax.rem(y + d, height), core)))
    mine = pltpu.make_async_copy(in_ref, own, local)
    mine.start()
    mine.wait()
    for d in range(1, height):
        other = lax.rem(y + height - d, height)
        arrival(out_ref.at[2 * z + x, other, core], y_recv.at[other]).wait_recv()
    here = block(z, x, core)
    for d in range(1, depth):
        sent.append(send(here, here, (z_send, z_recv), d - 1, z, device(lax.rem(z + d, depth), x, y, core)))

    def to_x(step, zz):
        sent.append(send(block(zz, x, core), block(zz, x, core), (x_send, x_recv), step, zz, device(z, 1 - x, y, core)))

    def to_core(step, zz, xx):
        sent.append(
            send(block(zz, xx, core), block(zz, xx, core), (c_send, c_recv), step, 2 * zz + xx, device(z, x, y, 1 - core))
        )

    to_x(0, z)
    to_core(0, z, x)
    for d in range(1, depth):
        zz = lax.rem(z + depth - d, depth)
        arrival(block(zz, x, core), z_recv.at[zz]).wait_recv()
        to_x(d, zz)
        to_core(d, zz, x)
    for d in range(depth):
        zz = lax.rem(z + depth - d, depth)
        arrival(block(zz, 1 - x, core), x_recv.at[zz]).wait_recv()
        to_core(depth + d, zz, 1 - x)
    for d in range(depth):
        zz = lax.rem(z + depth - d, depth)
        arrival(block(zz, x, 1 - core), c_recv.at[2 * zz + x]).wait_recv()
        arrival(block(zz, 1 - x, 1 - core), c_recv.at[2 * zz + 1 - x]).wait_recv()
    for copy in sent:
        copy.wait_send()


def gather_rows(block):
    clips, frames = lax.axis_size("clip"), lax.axis_size("frame")
    depth, height = clips // 2, frames // 2
    sems = pltpu.SemaphoreType.DMA
    out = pl.pallas_call(
        functools.partial(gather_kernel, depth, height),
        in_specs=[pl.BlockSpec(memory_space=pl.ANY)],
        out_specs=pl.BlockSpec(memory_space=pl.ANY),
        out_shape=jax.ShapeDtypeStruct((clips, height, 2) + block.shape, block.dtype),
        scratch_shapes=[
            sems,
            sems((max(height - 1, 1),)), sems((height,)),
            sems((depth - 1,)), sems((depth,)),
            sems((depth,)), sems((depth,)),
            sems((clips,)), sems((clips,)),
        ],
        compiler_params=pltpu.CompilerParams(collective_id=0, has_side_effects=True),
        name="gather_rows",
    )(block)
    return out.reshape(-1, block.shape[1])


def reduce_kernel(depth, height, part_ref, small_ref, out_ref, out_small, *refs):
    own, from_core, to_x, from_x, to_z, from_z, to_y, from_y = refs[:8]
    low_core, low_to_x, low_x, low_to_z, low_z, low_to_y, low_y = refs[8:15]
    c_send, c_recv, x_send, x_recv, z_send, z_recv, y_send, y_recv = refs[15:23]
    lc_send, lc_recv, lx_send, lx_recv, lz_send, lz_recv, ly_send, ly_recv, local = refs[23:]
    z, x, y, core = position()
    greet(neighbours(depth, height))

    def remote(source, target, send_sem, recv_sem, to):
        return pltpu.make_async_remote_copy(
            src_ref=source, dst_ref=target, send_sem=send_sem, recv_sem=recv_sem, device_id=to, device_id_type=MESH
        )

    def away(d):
        return lax.rem(z + d, depth)

    order = list(range(1, depth)) + [0]
    core_device, x_device = device(z, x, y, 1 - core), device(z, 1 - x, y, core)
    sent = []

    def start(copy):
        copy.start()
        sent.append(copy)
        return copy

    low_c = start(remote(small_ref.at[:, :, 1 - core], low_core, lc_send, lc_recv, core_device))
    c_copies, mine = [], []
    for side in range(2):
        xx = (1 - x) if side == 0 else x
        for d in order:
            slot, block = side * depth + d, 2 * away(d) + xx
            c_copies.append(
                start(
                    remote(
                        part_ref.at[block, :, 1 - core], from_core.at[slot],
                        c_send.at[slot], c_recv.at[slot], core_device,
                    )
                )
            )
            mine.append(pltpu.make_async_copy(part_ref.at[block, :, core], own.at[slot], local.at[slot]))
            mine[-1].start()

    def pair_sum(slot):
        return own[slot].astype(F32) + from_core[slot].astype(F32)

    x_copies = []
    for n, d in enumerate(order):
        mine[n].wait()
        c_copies[n].wait_recv()
        to_x[d] = pair_sum(d).astype(BF16)
        x_copies.append(start(remote(to_x.at[d], from_x.at[d], x_send.at[d], x_recv.at[d], x_device)))
    low_c.wait_recv()
    for zz in range(depth):
        low_to_x[zz] = small_ref[2 * zz + 1 - x, :, core] + low_core[2 * zz + 1 - x]
    low_xc = start(remote(low_to_x, low_x, lx_send, lx_recv, x_device))
    for n, d in enumerate(order):
        mine[depth + n].wait()
        c_copies[depth + n].wait_recv()
        x_copies[n].wait_recv()
        total = pair_sum(depth + d) + from_x[d].astype(F32)
        if d:
            to_z[d] = total.astype(BF16)
            start(remote(to_z.at[d], from_z.at[z], z_send.at[d], z_recv.at[z], device(away(d), x, y, core)))
        else:
            from_z[z] = total.astype(BF16)
    low_xc.wait_recv()
    for d in order:
        block = 2 * away(d) + x
        total = small_ref[block, :, core] + low_core[block] + low_x[away(d)]
        if d:
            low_to_z[d] = total
            start(remote(low_to_z.at[d], low_z.at[z], lz_send.at[d], lz_recv.at[z], device(away(d), x, y, core)))
        else:
            low_z[z] = total
    for d in range(1, depth):
        zz, to = lax.rem(z + depth - d, depth), device(away(d), x, y, core)
        remote(to_z.at[d], from_z.at[zz], z_send.at[d], z_recv.at[zz], to).wait_recv()
        remote(low_to_z.at[d], low_z.at[zz], lz_send.at[d], lz_recv.at[zz], to).wait_recv()

    def over(ref, *row):
        total = ref[(0,) + row].astype(F32)
        for n in range(1, ref.shape[0]):
            total = total + ref[(n,) + row].astype(F32)
        return total

    for d in range(1, height):
        other = lax.rem(y + d, height)
        to = device(z, x, other, core)
        to_y[d] = over(from_z, other).astype(BF16)
        start(remote(to_y.at[d], from_y.at[y], y_send.at[d], y_recv.at[y], to))
        low_to_y[d] = over(low_z, other)
        start(remote(low_to_y.at[d], low_y.at[y], ly_send.at[d], ly_recv.at[y], to))
    from_y[y] = over(from_z, y).astype(BF16)
    low_y[y] = over(low_z, y)
    for d in range(1, height):
        yy, to = lax.rem(y + height - d, height), device(z, x, lax.rem(y + d, height), core)
        remote(to_y.at[d], from_y.at[yy], y_send.at[d], y_recv.at[yy], to).wait_recv()
        remote(low_to_y.at[d], low_y.at[yy], ly_send.at[d], ly_recv.at[yy], to).wait_recv()
    out_ref[...] = over(from_y)
    out_small[...] = over(low_y)
    for copy in sent:
        copy.wait_send()


def reduce_rows(block, small):
    clips, frames = lax.axis_size("clip"), lax.axis_size("frame")
    depth, height = clips // 2, frames // 2
    rows = block.shape[0] // (clips * frames)
    sems, tail, low = pltpu.SemaphoreType.DMA, (rows, block.shape[1]), (rows, small.shape[1])
    lead = (clips, height, 2)
    return pl.pallas_call(
        functools.partial(reduce_kernel, depth, height),
        in_specs=[pl.BlockSpec(memory_space=pl.ANY), pl.BlockSpec(memory_space=pltpu.VMEM)],
        out_specs=[pl.BlockSpec(memory_space=pltpu.VMEM)] * 2,
        out_shape=[jax.ShapeDtypeStruct(tail, F32), jax.ShapeDtypeStruct(low, F32)],
        scratch_shapes=[
            pltpu.VMEM((2 * depth, height) + tail, BF16),
            pltpu.VMEM((2 * depth, height) + tail, BF16),
            pltpu.VMEM((depth, height) + tail, BF16),
            pltpu.VMEM((depth, height) + tail, BF16),
            pltpu.VMEM((depth, height) + tail, BF16),
            pltpu.VMEM((depth, height) + tail, BF16),
            pltpu.VMEM((height,) + tail, BF16),
            pltpu.VMEM((height,) + tail, BF16),
            pltpu.VMEM((clips, height) + low, F32),
            pltpu.VMEM((depth, height) + low, F32),
            pltpu.VMEM((depth, height) + low, F32),
            pltpu.VMEM((depth, height) + low, F32),
            pltpu.VMEM((depth, height) + low, F32),
            pltpu.VMEM((height,) + low, F32),
            pltpu.VMEM((height,) + low, F32),
            sems((2 * depth,)), sems((2 * depth,)),
            sems((depth,)), sems((depth,)),
            sems((depth,)), sems((depth,)),
            sems((height,)), sems((height,)),
            sems, sems,
            sems, sems,
            sems((depth,)), sems((depth,)),
            sems((height,)), sems((height,)),
            sems((2 * depth,)),
        ],
        compiler_params=pltpu.CompilerParams(
            collective_id=1, has_side_effects=True, vmem_limit_bytes=60 << 20
        ),
        name="reduce_rows",
    )(block.reshape(lead + tail), small.reshape(lead + low))


def gather(block):
    return lax.all_gather(block, AXES, axis=0, tiled=True)


def scatter(block):
    return lax.psum_scatter(block, AXES, scatter_dimension=0, tiled=True)


def shards(
    clips_in, teacher, valid, norm_gain, norm_shift, w_space, qv_bias, w_space_out, mix_bias,
    w_time, w_time_out, w_up, up_bias, w_down,
):
    batch, frames, places, _ = clips_in.shape
    ring = lax.axis_size("frame")
    pieces = ring // batch
    chunk = places // pieces
    all_frames = ring * frames
    me = lax.axis_index("frame")
    depth = w_up.shape[0]

    def swap(block, step):
        if step == 0:
            return block
        return lax.ppermute(block, "frame", [(i, i ^ step) for i in range(ring)])

    def clip_of(step):
        return (me // pieces) ^ (step // pieces)

    def place_of(step):
        return ((me % pieces) ^ (step % pieces)) * chunk

    def cut(block, step):
        if pieces == 1:
            return block
        return lax.dynamic_slice_in_dim(block, place_of(step), chunk, 0)

    def spread(block):
        got = []
        for step in range(ring):
            mine = lax.dynamic_index_in_dim(block, clip_of(step), 0, keepdims=False)
            got.append(cut(jnp.swapaxes(mine, 0, 1), step))
        return got

    many = FF // D
    count = jnp.sum(valid)
    counts = jnp.stack([count // 256, count % 256]).astype(BF16)
    smalls = jnp.concatenate(
        [
            norm_gain, norm_shift, qv_bias, mix_bias, up_bias.reshape(depth, many),
            jnp.broadcast_to(counts[None], (depth, 2)),
        ],
        1,
    )
    smalls = jnp.pad(smalls, ((0, 0), (0, SMALL - smalls.shape[1])))
    first = gather_rows(jnp.concatenate([w_space, w_space_out, smalls], 1))
    up_turned = jnp.swapaxes(w_up.reshape(depth, D, many), 1, 2).reshape(depth, FF)
    time_weights = gather(jnp.concatenate([w_time, w_time_out], 1))
    to_feed = jnp.concatenate([up_turned, w_down.reshape(depth, FF)], 1)
    table = jnp.swapaxes(first[:, 4 * D : 4 * D + 24].astype(F32), 0, 1)
    up_row = table[UP : UP + many].reshape(1, FF)
    counted = table[UP + many : UP + many + 2, ::depth]
    total_count = jnp.sum(counted[0]) * 256.0 + jnp.sum(counted[1])
    scale = (2.0 / (total_count * D)).reshape(1, 1)
    table = table[:16]

    order = [((me // pieces) ^ j).astype(jnp.int32) for j in range(batch)]
    clip_ids = [jnp.reshape(c, (1,)) for c in order]
    valid_column = [swap(part, step) for step, part in enumerate(spread(valid))]
    valid_column = jnp.concatenate(valid_column, 1).reshape(-1, 1).astype(F32)
    saved, sent, ins = [None] * batch, [None] * ring, None
    near = min(1, batch - 1)
    turns = [j for j in range(batch - 1, -1, -1) if j != near] + [near]
    cuts = spread(teacher)
    for turn, j in enumerate(turns):
        if turn == 3:
            ins, sent[-1], cuts = lax.optimization_barrier((ins, sent[-1], cuts))
        ins, *kept_j, after = space_forward(clip_ids[j], j, clips_in, table, first, ins)
        saved[j] = kept_j
        after = jnp.swapaxes(after, 0, 1)
        if turn == 0:
            after, to_feed = lax.optimization_barrier((after, to_feed))
        if j == 0:
            cuts, after = lax.optimization_barrier((cuts, after))
        for r in range(pieces):
            step = j * pieces + r
            sent[step] = swap(cut(after, step), step)
    feed_weights = gather(to_feed)
    teachers = [swap(part, step) for step, part in enumerate(cuts)]
    *saved_b, after_b = time_forward(sent, table, time_weights)
    tile, _ = time_tiles(chunk, all_frames)
    layer_parts, grad_b, d_feed, rows_c, bias_up, squares = feed_forward(
        after_b, teachers, valid_column, scale, table, up_row, feed_weights, tile
    )
    grad_parts, d_rest, rows_b = time_back(grad_b, saved_b, sent, table, time_weights, d_feed)
    d_rest = scatter(d_rest)
    d_time, d_feed = d_rest[:, : 4 * D], d_rest[:, 4 * D :]
    grad_parts = [swap(part, step) for step, part in enumerate(grad_parts)]

    def join(parts, j):
        if pieces == 1:
            return parts[j]
        whole = jnp.zeros((places, frames, D), BF16)
        for r in range(pieces):
            step = j * pieces + r
            whole = lax.dynamic_update_slice_in_dim(whole, parts[step], place_of(step), 0)
        return whole

    outs, biases, projs, input_grad = [], [], None, None
    grads = [jnp.swapaxes(join(grad_parts, 0), 0, 1)] + [None] * (batch - 1)
    for j in range(batch):
        projs, d_out, bias = space_back(grads[j], j, batch, saved[j], first, projs)
        outs.append(d_out)
        biases.append(bias)
        if j == batch // 2:
            projs, layer_parts = lax.optimization_barrier((projs, layer_parts))
            layer_parts = [swap(part, step) for step, part in enumerate(layer_parts)]
        if j + 1 < batch:
            following = jnp.swapaxes(join(grad_parts, j + 1), 0, 1)
            grads[j + 1] = following
        input_grad = input_grads(clip_ids[j], j, grads[j], projs, clips_in, table, first, input_grad)
    d_space, small = space_weights(
        ins, projs, first, table, rows_c, rows_b, bias_up.reshape(many, D), squares, outs, biases
    )
    d_space, here = reduce_rows(d_space, small)
    layer_out = place_clips(jnp.stack(order), [join(layer_parts, j) for j in range(batch)])
    d_up = jnp.swapaxes(d_feed[:, :FF].reshape(depth, many, D), 1, 2).reshape(depth, FF)
    return (
        jnp.swapaxes(layer_out, 1, 2),
        here[0, 13 + many] / (total_count * D),
        input_grad,
        here[:, 0:3],
        here[:, 3:6],
        d_space[:, : 3 * D],
        here[:, 6:9],
        here[:, 9],
        d_space[:, 3 * D : 4 * D],
        here[:, 10:13],
        d_time[:, : 3 * D].astype(F32),
        d_time[:, 3 * D :].astype(F32),
        d_up.astype(F32),
        here[:, 13 : 13 + many].reshape(-1),
        d_feed[:, FF:].reshape(-1, D).astype(F32),
    )


def solution(mesh):
    tokens, rows = P("clip", "frame", None, None), P(AXES, None)
    in_specs = (tokens, tokens, P("clip", "frame", None)) + (rows,) * 9 + (P(AXES), rows)
    out_specs = (
        (tokens, P(), tokens, rows, rows, rows, rows, P(AXES)) + (rows,) * 5 + (P(AXES), rows)
    )
    return jax.shard_map(shards, mesh=mesh, in_specs=in_specs, out_specs=out_specs, check_vma=False)
```

```python
import functools

import jax
import jax.numpy as jnp
from jax import lax
from jax.experimental import pallas as pl
from jax.experimental.pallas import tpu as pltpu
from jax.sharding import PartitionSpec as P

D = 768
HEADS = 12
HEAD = 64
FF = 3072
EPS = 1e-06
F32 = jnp.float32
BF16 = jnp.bfloat16
PARAMS = pltpu.CompilerParams(vmem_limit_bytes=60 << 20)


def cost(flops, moved=0):
    return pl.CostEstimate(flops=int(flops) // 16, bytes_accessed=int(moved), transcendentals=0)


GAIN, SHIFT, QV, MIX, UP = 0, 3, 6, 10, 13


def dot(left, right):
    return jnp.dot(left, right, preferred_element_type=F32)


def dot_nt(left, right):
    return lax.dot_general(left, right, (((1,), (1,)), ((), ())), preferred_element_type=F32)


def dot_tn(left, right):
    return lax.dot_general(left, right, (((0,), (0,)), ((), ())), preferred_element_type=F32)


def normalize(rows):
    center = rows - jnp.mean(rows, -1, keepdims=True)
    inverse = lax.rsqrt(jnp.mean(center * center, -1, keepdims=True) + EPS)
    return center * inverse, inverse


def normalize_back(grad_out, hat, inverse, gain):
    grad_hat = grad_out * gain
    return inverse * (
        grad_hat
        - jnp.mean(grad_hat, -1, keepdims=True)
        - hat * jnp.mean(grad_hat * hat, -1, keepdims=True)
    )


def column_sum(rows):
    return jnp.sum(rows, 0, keepdims=True)


def first_lanes(shape):
    return lax.broadcasted_iota(jnp.int32, shape, 1) < HEAD


def halves(block):
    low = first_lanes(block.shape)
    zero = jnp.zeros_like(block)
    return jnp.where(low, block, zero), jnp.where(low, zero, block)


def pair(index):
    return slice(2 * HEAD * index, 2 * HEAD * (index + 1))


def grow(block, rows):
    if rows == block.shape[0]:
        return block
    return jnp.concatenate([block, jnp.zeros((rows - block.shape[0], block.shape[1]), block.dtype)], 0)


def stack(block):
    return jnp.concatenate(halves(block), 0)


def merge(two):
    rows = two.shape[0] // 2
    return jnp.where(first_lanes((rows, two.shape[1])), two[:rows], two[rows:])


def kept(rows):
    return HEADS // 2, 2 * padded(rows), rows


def padded(rows):
    return -(-rows // 16) * 16


def attention(units, rows, frames=None):
    full = padded(rows)
    place = lax.broadcasted_iota(jnp.int32, (full, rows), 0)
    if frames is not None:
        mask = place // frames == lax.broadcasted_iota(jnp.int32, (full, rows), 1) // frames
    else:
        mask = place < rows

    def score(unit):
        return dot_nt(stack(grow(unit[1](), full)), unit[0]())

    scores = score(units[0])
    for n, (_, _, value, keep_probs, keep_mix) in enumerate(units):
        now = scores
        if n + 1 < len(units):
            scores = score(units[n + 1])
        probs = []
        for one in (now[:full], now[full:]):
            one = jnp.where(mask, one, -1e30)
            expo = jnp.exp(one - jnp.max(one, 0, keepdims=True))
            probs.append((expo * (1.0 / column_sum(expo))).astype(BF16))
        probs = jnp.concatenate(probs, 0)
        keep_probs(probs)
        keep_mix(dot_tn(probs, stack(grow(value(), full))).astype(BF16))


def attention_back(units, rows):
    full = padded(rows)

    def probs_grad(unit):
        return dot_nt(stack(grow(unit[2](), full)), unit[3]())

    grad_p = probs_grad(units[0])
    for n, (query, key, _, grad_mix, probs_of, keep) in enumerate(units):
        probs = probs_of()
        wide = probs.astype(F32)
        term = wide * grad_p
        grad_s = []
        for head in (slice(0, full), slice(full, 2 * full)):
            grad_s.append((term[head] - wide[head] * column_sum(term[head])).astype(BF16))
        grad_s = jnp.concatenate(grad_s, 0)
        if n + 1 < len(units):
            grad_p = probs_grad(units[n + 1])
        to_v = merge(dot(probs, grad_mix()))
        to_k = merge(dot(grad_s, query()))
        to_q = dot_tn(grad_s, stack(grow(key(), full)))
        keep((to_q * HEAD ** (-0.5)).astype(BF16), to_k[:rows].astype(BF16), to_v[:rows].astype(BF16))


def reader(ref, *index):
    return lambda: ref[index]


def writer(ref, *index):
    def write(value):
        ref[index] = value

    return write


def writer3(ref, lead, rows, p):
    def write(*values):
        for n, value in enumerate(values):
            ref[lead + (rows, pair(n * HEADS // 2 + p))] = value

    return write


def project(rows, weights, table, query_row):
    proj = dot(rows, weights)
    query = (proj[:, :D] + table[query_row : query_row + 1, :]).astype(BF16)
    key = proj[:, D : 2 * D].astype(BF16)
    value = (proj[:, 2 * D :] + table[query_row + 1 : query_row + 2, :]).astype(BF16)
    return (query.astype(F32) * HEAD ** (-0.5)).astype(BF16), key, value


def fixed(shape):
    return pl.BlockSpec(shape, lambda *_: (0,) * len(shape), pipeline_mode=pl.Buffered(1))


def columns_of(width, index):
    return pl.BlockSpec((D, width), lambda *_: (0, index), pipeline_mode=pl.Buffered(1))


def collect(refs, scratch):
    frames = refs[0].shape[1]
    for n, ref in enumerate(refs):
        scratch[:, n * frames : (n + 1) * frames, :] = ref[...].astype(F32)
    return scratch[...].reshape(-1, D)


def deal(rows, scratch, refs):
    frames = refs[0].shape[1]
    scratch[...] = rows.reshape(scratch.shape)
    for n, ref in enumerate(refs):
        ref[...] = scratch[:, n * frames : (n + 1) * frames, :].astype(BF16)


def clear(first, *refs):
    @pl.when(first)
    def _():
        for ref in refs:
            ref[...] = jnp.zeros_like(ref)


def put_rows(ref, value):
    rows, full = value.shape[0], ref.shape[0]
    ref[:rows, :] = value
    if full > rows:
        ref[rows:, :] = jnp.zeros((full - rows, value.shape[1]), value.dtype)


def space_kernel(clip, x_ref, table, w_ref, *refs):
    in_ref, q_ref, k_ref, v_ref, mix_ref, p_ref, out_ref = refs[-7:]
    rows = x_ref[0, 0].astype(F32)
    hat, _ = normalize(rows)
    normed = (hat * table[GAIN : GAIN + 1, :] + table[SHIFT : SHIFT + 1, :]).astype(BF16)
    put_rows(in_ref.at[0, 0], normed)
    q_ref[0], k_ref[0], v_ref[0] = project(normed, w_ref[:, : 3 * D], table, QV)
    every = slice(None)
    attention(
        [
            tuple(reader(ref, 0, every, pair(p)) for ref in (q_ref, k_ref, v_ref))
            + (writer(p_ref, 0, p), writer(mix_ref, 0, every, pair(p)))
            for p in range(HEADS // 2)
        ],
        rows.shape[0],
    )
    after = rows + dot(mix_ref[0], w_ref[:, 3 * D : 4 * D]) + table[MIX : MIX + 1, :]
    out_ref[0] = after.astype(BF16)


def space_forward(clip, step, inputs, table, weights, before):
    batch, frames, places, _ = inputs.shape
    full = padded(places)
    more = [] if before is None else [before]

    def frame(*tail):
        return pl.BlockSpec((1,) + tail, lambda i, c: (i,) + (0,) * len(tail))

    def shape(*tail):
        return jax.ShapeDtypeStruct((frames,) + tail, BF16)

    return pl.pallas_call(
        space_kernel,
        grid_spec=pltpu.PrefetchScalarGridSpec(
            num_scalar_prefetch=1,
            grid=(frames,),
            in_specs=[
                pl.BlockSpec((1, 1, places, D), lambda i, c: (c[0], i, 0, 0)),
                fixed(table.shape),
                columns_of(4 * D, 0),
            ]
            + [pl.BlockSpec(memory_space=pl.ANY) for _ in more],
            out_specs=[pl.BlockSpec((1, 1, full, D), lambda i, c: (step, i, 0, 0))]
            + [frame(places, D)] * 4
            + [frame(*kept(places)), frame(places, D)],
        ),
        out_shape=[jax.ShapeDtypeStruct((batch, frames, full, D), BF16)]
        + [shape(places, D)] * 4
        + [shape(*kept(places)), shape(places, D)],
        input_output_aliases={4: 0} if more else {},
        compiler_params=PARAMS,
        cost_estimate=cost(24 * frames * places * D * D),
        name="space_forward",
    )(clip, inputs, table, weights, *more)


def largest_divisor(number, limit):
    return max(n for n in range(1, limit + 1) if number % n == 0)


def time_kernel(frames, group, ring, *refs):
    parts, (table, w_ref) = refs[:ring], refs[ring : ring + 2]
    a_ref, in_ref, q_ref, k_ref, v_ref, mix_ref, p_ref, out_ref, scratch = refs[ring + 2 :]
    rows = collect(parts, scratch)
    a_ref[...] = rows.astype(BF16)
    hat, _ = normalize(rows)
    normed = (hat * table[GAIN + 1 : GAIN + 2, :] + table[SHIFT + 1 : SHIFT + 2, :]).astype(BF16)
    in_ref[...] = normed
    q_ref[...], k_ref[...], v_ref[...] = project(normed, w_ref[:, : 3 * D], table, QV + 2)
    units = []
    for g in range(rows.shape[0] // group):
        span = slice(g * group, (g + 1) * group)
        for p in range(HEADS // 2):
            units.append(
                tuple(reader(ref, span, pair(p)) for ref in (q_ref, k_ref, v_ref))
                + (writer(p_ref, g, p), writer(mix_ref, span, pair(p)))
            )
    attention(units, group, frames)
    out_ref[...] = rows + dot(mix_ref[...], w_ref[:, 3 * D :]) + table[MIX + 1 : MIX + 2, :]


def time_tiles(places, frames):
    per_group = largest_divisor(places, 128 // frames)
    per_tile = per_group * largest_divisor(places // per_group, 4)
    return per_tile * frames, per_group * frames


def piece_specs(parts, tile):
    frames = parts[0].shape[1]
    places = tile // (frames * len(parts))
    return [pl.BlockSpec((places, frames, D), lambda i: (i, 0, 0))] * len(parts)


def join_scratch(parts, tile):
    frames = parts[0].shape[1] * len(parts)
    return pltpu.VMEM((tile // frames, frames, D), F32)


def time_forward(parts, table, weights):
    places, frames = parts[0].shape[0], parts[0].shape[1] * len(parts)
    tokens = places * frames
    tile, group = time_tiles(places, frames)
    rows = pl.BlockSpec((tile, D), lambda i: (i, 0))
    return pl.pallas_call(
        functools.partial(time_kernel, frames, group, len(parts)),
        grid=(tokens // tile,),
        in_specs=piece_specs(parts, tile) + [fixed(table.shape), columns_of(4 * D, 0)],
        out_specs=[rows] * 6
        + [pl.BlockSpec((tile // group,) + kept(group), lambda i: (i, 0, 0, 0)), rows],
        out_shape=[jax.ShapeDtypeStruct((tokens, D), BF16)] * 6
        + [
            jax.ShapeDtypeStruct((tokens // group,) + kept(group), BF16),
            jax.ShapeDtypeStruct((tokens, D), F32),
        ],
        scratch_shapes=[join_scratch(parts, tile)],
        compiler_params=PARAMS,
        cost_estimate=cost(24 * tokens * D * D),
        name="time_forward",
    )(*parts, table, weights)


def gelu_parts(u):
    area = 0.5 + 0.5 * lax.erf(u * 0.7071067811865476)
    bell = jnp.exp2((-0.5 * 1.4426950408889634) * (u * u))
    return u * area, area + 0.3989422804014327 * (u * bell)


FF_CHUNK = 768


def feed_kernel(ring, *refs):
    teachers, refs = refs[:ring], refs[ring:]
    (a_ref, valid_ref, scale_ref, table, up_bias, up_ref, down_ref), refs = refs[:7], refs[7:]
    outs, refs = refs[:ring], refs[ring:]
    g_ref, d_ref, rows_ref, bias_ref, square_ref, hidden, slope, d_up, d_down, stage, sems, scratch = refs
    step, last = pl.program_id(0), pl.num_programs(0) - 1
    clear(step == 0, d_up, d_down, rows_ref, bias_ref, square_ref)
    after = a_ref[...]
    hat, inverse = normalize(after)
    normed = (hat * table[GAIN + 2 : GAIN + 3, :] + table[SHIFT + 2 : SHIFT + 3, :]).astype(BF16)
    total = after + table[MIX + 2 : MIX + 3, :]
    chunks = [slice(c, c + FF_CHUNK) for c in range(0, FF, FF_CHUNK)]
    for c in chunks:
        act, rise = gelu_parts(dot(normed, up_ref[:, c]) + up_bias[:, c])
        act = act.astype(BF16)
        hidden[:, c] = act
        slope[:, c] = rise.astype(BF16)
        total = total + dot(act, down_ref[:, c])
    deal(total, scratch, outs)
    diff = (total - collect(teachers, scratch)) * valid_ref[...]
    square_ref[...] += column_sum(diff * diff)
    grad = diff * scale_ref[0, 0]
    grad_low = grad.astype(BF16)
    bias_c = column_sum(grad_low.astype(F32))
    back = jnp.zeros_like(grad)
    for c in chunks:
        grad_pre = dot_nt(grad_low, down_ref[:, c]) * slope[:, c].astype(F32)
        grad_pre = grad_pre.astype(BF16)
        bias_ref[:, c] += column_sum(grad_pre.astype(F32))
        d_down[:, c] += dot_tn(hidden[:, c], grad_low)
        d_up[:, c] += dot_tn(normed, grad_pre)
        back = back + dot_nt(grad_pre, up_ref[:, c])
    rows_ref[...] += jnp.concatenate([column_sum(back * hat), column_sum(back), bias_c], 0)
    g_ref[...] = grad + normalize_back(back, hat, inverse, table[GAIN + 2 : GAIN + 3, :])

    @pl.when(step == last)
    def _():
        moves = []
        for source, start in ((d_up, 0), (d_down, FF)):
            moves += [(source.at[:, c], d_ref.at[:, start + c.start : start + c.stop]) for c in chunks]
        flush(moves, stage, sems)


def flush(moves, stage, sems):
    copies = []
    for i, (source, target) in enumerate(moves):
        if i >= 2:
            copies[i - 2].wait()
        stage[i % 2] = source[...].astype(BF16)
        copies.append(pltpu.make_async_copy(stage.at[i % 2], target, sems.at[i % 2]))
        copies[i].start()
    for copy in copies[-2:]:
        copy.wait()


def feed_forward(after_b, teachers, valid, scale, table, up_bias, weights, tile):
    tokens, ring = after_b.shape[0], len(teachers)
    rows = pl.BlockSpec((tile, D), lambda i: (i, 0))
    *outs, grad, d_feed, sums, bias, squares = pl.pallas_call(
        functools.partial(feed_kernel, ring),
        grid=(tokens // tile,),
        in_specs=piece_specs(teachers, tile)
        + [
            rows,
            pl.BlockSpec((tile, 1), lambda i: (i, 0)),
            pl.BlockSpec(memory_space=pltpu.SMEM),
            fixed(table.shape),
            fixed((1, FF)),
            columns_of(FF, 0),
            columns_of(FF, 1),
        ],
        out_specs=piece_specs(teachers, tile)
        + [rows, pl.BlockSpec(memory_space=pl.ANY), fixed((3, D)), fixed((1, FF)), fixed((1, D))],
        out_shape=[jax.ShapeDtypeStruct(t.shape, BF16) for t in teachers]
        + [
            jax.ShapeDtypeStruct((tokens, D), F32),
            jax.ShapeDtypeStruct((D, 2 * FF), BF16),
            jax.ShapeDtypeStruct((3, D), F32),
            jax.ShapeDtypeStruct((1, FF), F32),
            jax.ShapeDtypeStruct((1, D), F32),
        ],
        scratch_shapes=[
            pltpu.VMEM((tile, FF), BF16),
            pltpu.VMEM((tile, FF), BF16),
            pltpu.VMEM((D, FF), F32),
            pltpu.VMEM((D, FF), F32),
            pltpu.VMEM((2, D, FF_CHUNK), BF16),
            pltpu.SemaphoreType.DMA((2,)),
            join_scratch(teachers, tile),
        ],
        compiler_params=PARAMS,
        cost_estimate=cost(80 * tokens * D * D),
        name="feed_forward",
    )(*teachers, after_b, valid, scale, table, up_bias, weights, weights)
    return outs, grad, d_feed, sums, bias, squares


def time_back_kernel(group, ring, *refs):
    (g_ref, a_ref, in_ref, q_ref, k_ref, v_ref, mix_ref, p_ref, table, w_ref), refs = refs[:10], refs[10:]
    outs, refs = refs[:ring], refs[ring:]
    d_ref, rows_ref, grad_mix, grad_proj, d_proj, d_out, stage, sems, scratch = refs
    step, last = pl.program_id(0), pl.num_programs(0) - 1
    clear(step == 0, d_proj, d_out, rows_ref)
    grad = g_ref[...]
    grad_low = grad.astype(BF16)
    d_out[...] += dot_tn(mix_ref[...], grad_low)
    grad_mix[...] = dot_nt(grad_low, w_ref[:, 3 * D :]).astype(BF16)

    units = []
    for g in range(grad.shape[0] // group):
        span = slice(g * group, (g + 1) * group)
        for p in range(HEADS // 2):
            units.append(
                tuple(reader(ref, span, pair(p)) for ref in (q_ref, k_ref, v_ref, grad_mix))
                + (reader(p_ref, g, p), writer3(grad_proj, (), span, p))
            )
    attention_back(units, group)
    proj = grad_proj[...]
    d_proj[...] += dot_tn(in_ref[...], proj)
    sums = column_sum(proj.astype(F32))
    back = dot_nt(proj, w_ref[:, : 3 * D])
    hat, inverse = normalize(a_ref[...].astype(F32))
    rows_ref[...] += jnp.concatenate(
        [
            column_sum(back * hat),
            column_sum(back),
            sums[:, :D],
            sums[:, 2 * D :],
            column_sum(grad_low.astype(F32)),
        ],
        0,
    )
    deal(grad + normalize_back(back, hat, inverse, table[GAIN + 1 : GAIN + 2, :]), scratch, outs)

    @pl.when(step == last)
    def _():
        moves = [(d_proj.at[:, pl.ds(c * D, D)], d_ref.at[:, pl.ds(c * D, D)]) for c in range(3)]
        flush(moves + [(d_out, d_ref.at[:, pl.ds(3 * D, D)])], stage, sems)


def time_back(grad, saved, like, table, weights):
    ring, tokens = len(like), grad.shape[0]
    places, frames = like[0].shape[0], like[0].shape[1] * ring
    tile, group = time_tiles(places, frames)
    rows = pl.BlockSpec((tile, D), lambda i: (i, 0))
    *outs, d_time, sums = pl.pallas_call(
        functools.partial(time_back_kernel, group, ring),
        grid=(tokens // tile,),
        in_specs=[rows] * 7
        + [
            pl.BlockSpec((tile // group,) + kept(group), lambda i: (i, 0, 0, 0)),
            fixed(table.shape),
            columns_of(4 * D, 0),
        ],
        out_specs=piece_specs(like, tile) + [pl.BlockSpec(memory_space=pl.ANY), fixed((5, D))],
        out_shape=[jax.ShapeDtypeStruct(t.shape, BF16) for t in like]
        + [jax.ShapeDtypeStruct((D, 8 * D), BF16), jax.ShapeDtypeStruct((5, D), F32)],
        scratch_shapes=[
            pltpu.VMEM((tile, D), BF16),
            pltpu.VMEM((tile, 3 * D), BF16),
            pltpu.VMEM((D, 3 * D), F32),
            pltpu.VMEM((D, D), F32),
            pltpu.VMEM((2, D, D), BF16),
            pltpu.SemaphoreType.DMA((2,)),
            join_scratch(like, tile),
        ],
        compiler_params=PARAMS,
        cost_estimate=cost(42 * tokens * D * D),
        name="time_back",
    )(grad, *saved, table, weights)
    return outs, d_time, sums


def space_back_kernel(g_ref, q_ref, k_ref, v_ref, mix_ref, p_ref, w_ref, *refs):
    out_ref, d_ref, bias_ref, grad_mix = refs[-4:]
    clear(pl.program_id(0) == 0, d_ref, bias_ref)
    grad = g_ref[0]
    rows, full = grad.shape[0], out_ref.shape[2]
    d_ref[...] += dot_tn(mix_ref[0], grad)
    bias_ref[...] += column_sum(grad.astype(F32))
    grad_mix[...] = dot_nt(grad, w_ref[...]).astype(BF16)
    every = slice(None)
    attention_back(
        [
            tuple(reader(ref, 0, every, pair(p)) for ref in (q_ref, k_ref, v_ref))
            + (reader(grad_mix, every, pair(p)), reader(p_ref, 0, p))
            + (writer3(out_ref, (0, 0), slice(0, rows), p),)
            for p in range(HEADS // 2)
        ],
        rows,
    )
    if full > rows:
        out_ref[0, 0, rows:, :] = jnp.zeros((full - rows, out_ref.shape[3]), BF16)


def space_back(grad, step, batch, saved, weights, before):
    frames, places, _ = grad.shape
    full = padded(places)
    more = [] if before is None else [before]

    def frame(*tail):
        return pl.BlockSpec((1,) + tail, lambda i: (i,) + (0,) * len(tail))

    return pl.pallas_call(
        space_back_kernel,
        grid=(frames,),
        in_specs=[frame(places, D)] * 5
        + [frame(*kept(places)), columns_of(D, 3)]
        + [pl.BlockSpec(memory_space=pl.ANY) for _ in more],
        out_specs=[
            pl.BlockSpec((1, 1, full, 3 * D), lambda i: (step, i, 0, 0)),
            fixed((D, D)),
            fixed((1, D)),
        ],
        out_shape=[
            jax.ShapeDtypeStruct((batch, frames, full, 3 * D), BF16),
            jax.ShapeDtypeStruct((D, D), F32),
            jax.ShapeDtypeStruct((1, D), F32),
        ],
        scratch_shapes=[pltpu.VMEM((places, D), BF16)],
        input_output_aliases={7: 0} if more else {},
        compiler_params=PARAMS,
        cost_estimate=cost(24 * frames * places * D * D),
        name="space_back",
    )(grad, *saved, weights, *more)


SMALL = 128


def space_weight_kernel(parts, in_ref, proj_ref, w_ref, table, c_ref, b_ref, up_ref, square_ref, *refs):
    outs, biases, refs = refs[:parts], refs[parts : 2 * parts], refs[2 * parts + 1 :]
    d_ref, small_ref, d_proj, d_out, sums, rows, stage, sems = refs
    step, last = pl.program_id(0), pl.num_programs(0) - 1
    clear(step == 0, d_proj, sums, rows)
    proj = proj_ref[0].reshape(-1, 3 * D)
    d_proj[...] += dot_tn(in_ref[0].reshape(-1, D), proj)
    sums[...] += column_sum(proj.astype(F32))

    @pl.when(step == last)
    def _():
        d_out[...] = sum(ref[...] for ref in outs)
        moves = [(d_proj.at[:, pl.ds(c * D, D)], d_ref.at[:, pl.ds((4 + c) * D, D)]) for c in range(3)]
        flush(moves + [(d_out, d_ref.at[:, pl.ds(7 * D, D)])], stage, sems)
        many = up_ref.shape[0]
        rows[1:2, :], rows[2:3, :] = b_ref[0:1, :], c_ref[0:1, :]
        rows[4:5, :], rows[5:6, :] = b_ref[1:2, :], c_ref[1:2, :]
        rows[6:7, :], rows[7:8, :] = sums[:, :D], sums[:, 2 * D :]
        rows[8:9, :], rows[9:10, :] = b_ref[3:4, :], b_ref[2:3, :]
        rows[10:11, :] = sum(ref[...] for ref in biases)
        rows[11:12, :], rows[12:13, :] = b_ref[4:5, :], c_ref[2:3, :]
        rows[13 : 13 + many, :] = up_ref[...]
        square = jnp.sum(square_ref[...], -1, keepdims=True)
        rows[13 + many : 14 + many, :] = jnp.broadcast_to(square, square_ref.shape)
        rows[SMALL - 2 : SMALL - 1, :] = table[GAIN : GAIN + 1, :]
        rows[SMALL - 1 : SMALL, :] = table[SHIFT : SHIFT + 1, :]
        columns = jnp.swapaxes(rows[...], 0, 1)
        wide = w_ref[...].astype(F32)
        with_grad = jnp.sum(wide * d_proj[...], -1, keepdims=True)
        shift_grad = jnp.sum(wide * sums[...], -1, keepdims=True)
        gain, shift = columns[:, SMALL - 2 : SMALL - 1], columns[:, SMALL - 1 :]
        gain_grad = (with_grad - shift * shift_grad) / gain
        lane = lax.broadcasted_iota(jnp.int32, columns.shape, 1)
        small_ref[...] = jnp.where(lane == 0, gain_grad, jnp.where(lane == 3, shift_grad, columns))


def space_weights(ins, projs, weights, table, rows_c, rows_b, bias_up, squares, outs, biases, matrix):
    batch, frames, full, _ = ins.shape

    def clip(width):
        return pl.BlockSpec((1, frames, full, width), lambda i: (i, 0, 0, 0))

    smalls = [table, rows_c, rows_b, bias_up, squares]
    return pl.pallas_call(
        functools.partial(space_weight_kernel, batch),
        grid=(batch,),
        in_specs=[clip(D), clip(3 * D), columns_of(3 * D, 0)]
        + [fixed(a.shape) for a in smalls]
        + [fixed((D, D))] * batch
        + [fixed((1, D))] * batch
        + [pl.BlockSpec(memory_space=pl.ANY)],
        out_specs=[pl.BlockSpec(memory_space=pl.ANY), fixed((D, SMALL))],
        out_shape=[jax.ShapeDtypeStruct(matrix.shape, BF16), jax.ShapeDtypeStruct((D, SMALL), F32)],
        input_output_aliases={8 + 2 * batch: 0},
        scratch_shapes=[
            pltpu.VMEM((D, 3 * D), F32),
            pltpu.VMEM((D, D), F32),
            pltpu.VMEM((1, 3 * D), F32),
            pltpu.VMEM((SMALL, D), F32),
            pltpu.VMEM((2, D, D), BF16),
            pltpu.SemaphoreType.DMA((2,)),
        ],
        compiler_params=PARAMS,
        cost_estimate=cost(18 * batch * frames * full * D * D),
        name="space_weights",
    )(ins, projs, weights, *smalls, *outs, *biases, matrix)


def place_kernel(order, *refs):
    blocks, out_ref = refs[:-1], refs[-1]
    for n, ref in enumerate(blocks):

        @pl.when(pl.program_id(0) == n)
        def _():
            out_ref[0] = ref[...]


def place_clips(order, blocks):
    shape = blocks[0].shape
    return pl.pallas_call(
        place_kernel,
        grid_spec=pltpu.PrefetchScalarGridSpec(
            num_scalar_prefetch=1,
            grid=(len(blocks),),
            in_specs=[fixed(shape)] * len(blocks),
            out_specs=pl.BlockSpec((1,) + shape, lambda i, order: (order[i], 0, 0, 0)),
        ),
        out_shape=jax.ShapeDtypeStruct((len(blocks),) + shape, BF16),
        compiler_params=PARAMS,
        name="place_clips",
    )(order, *blocks)


AXES = ("clip", "frame")
MESH = pl.DeviceIdType.MESH


def position():
    clip, frame = lax.axis_index("clip"), lax.axis_index("frame")
    return clip // 2, clip % 2, frame // 2, frame % 2


def device(z, x, y, core):
    return (2 * z + x, 2 * y + core)


def greet(partners):
    barrier = pltpu.get_barrier_semaphore()
    for partner in partners:
        pl.semaphore_signal(barrier, inc=1, device_id=partner, device_id_type=MESH)
    pl.semaphore_wait(barrier, len(partners))


def neighbours(depth, height):
    z, x, y, core = position()
    return (
        [device(lax.rem(z + d, depth), x, y, core) for d in range(1, depth)]
        + [device(z, x, lax.rem(y + d, height), core) for d in range(1, height)]
        + [device(z, 1 - x, y, core), device(z, x, y, 1 - core)]
    )


def gather_kernel(depth, height, in_ref, out_ref, local, y_send, y_recv, z_send, z_recv, x_send, x_recv, c_send, c_recv):
    z, x, y, core = position()
    greet(neighbours(depth, height))

    def send(source, target, sems, slot, index, to):
        copy = pltpu.make_async_remote_copy(
            src_ref=source, dst_ref=target, send_sem=sems[0].at[slot], recv_sem=sems[1].at[index],
            device_id=to, device_id_type=MESH,
        )
        copy.start()
        return copy

    def block(zz, xx, cc):
        return out_ref.at[2 * zz + xx, :, cc]

    def arrival(ref, sem):
        return pltpu.make_async_remote_copy(
            src_ref=ref, dst_ref=ref, send_sem=sem, recv_sem=sem, device_id=device(z, 1 - x, y, core), device_id_type=MESH
        )

    sent = []
    own = out_ref.at[2 * z + x, y, core]
    for d in range(1, height):
        sent.append(send(in_ref, own, (y_send, y_recv), d - 1, y, device(z, x, lax.rem(y + d, height), core)))
    mine = pltpu.make_async_copy(in_ref, own, local)
    mine.start()
    mine.wait()
    for d in range(1, height):
        other = lax.rem(y + height - d, height)
        arrival(out_ref.at[2 * z + x, other, core], y_recv.at[other]).wait_recv()
    here = block(z, x, core)
    for d in range(1, depth):
        sent.append(send(here, here, (z_send, z_recv), d - 1, z, device(lax.rem(z + d, depth), x, y, core)))

    def to_x(step, zz):
        sent.append(send(block(zz, x, core), block(zz, x, core), (x_send, x_recv), step, zz, device(z, 1 - x, y, core)))

    def to_core(step, zz, xx):
        sent.append(
            send(block(zz, xx, core), block(zz, xx, core), (c_send, c_recv), step, 2 * zz + xx, device(z, x, y, 1 - core))
        )

    to_x(0, z)
    to_core(0, z, x)
    for d in range(1, depth):
        zz = lax.rem(z + depth - d, depth)
        arrival(block(zz, x, core), z_recv.at[zz]).wait_recv()
        to_x(d, zz)
        to_core(d, zz, x)
    for d in range(depth):
        zz = lax.rem(z + depth - d, depth)
        arrival(block(zz, 1 - x, core), x_recv.at[zz]).wait_recv()
        to_core(depth + d, zz, 1 - x)
    for d in range(depth):
        zz = lax.rem(z + depth - d, depth)
        arrival(block(zz, x, 1 - core), c_recv.at[2 * zz + x]).wait_recv()
        arrival(block(zz, 1 - x, 1 - core), c_recv.at[2 * zz + 1 - x]).wait_recv()
    for copy in sent:
        copy.wait_send()


def gather_rows(block):
    clips, frames = lax.axis_size("clip"), lax.axis_size("frame")
    depth, height = clips // 2, frames // 2
    sems = pltpu.SemaphoreType.DMA
    out = pl.pallas_call(
        functools.partial(gather_kernel, depth, height),
        in_specs=[pl.BlockSpec(memory_space=pl.ANY)],
        out_specs=pl.BlockSpec(memory_space=pl.ANY),
        out_shape=jax.ShapeDtypeStruct((clips, height, 2) + block.shape, block.dtype),
        scratch_shapes=[
            sems,
            sems((max(height - 1, 1),)), sems((height,)),
            sems((depth - 1,)), sems((depth,)),
            sems((depth,)), sems((depth,)),
            sems((clips,)), sems((clips,)),
        ],
        compiler_params=pltpu.CompilerParams(collective_id=0, has_side_effects=True),
        name="gather_rows",
    )(block)
    return out.reshape(-1, block.shape[1])


def turned(number, flips, size):
    total, bit = 0, 1
    while bit < size:
        value = (number // bit) % 2
        total = total + bit * (1 - value if flips & bit else value)
        bit *= 2
    return total


def reduce_kernel(depth, height, many, batch, part_ref, small_ref, projs, x_ref, table, all_w, *refs):
    grads, outs, refs = refs[:batch], refs[batch : batch + many], refs[batch + many :]
    out_small, dx_ref, refs = refs[0], refs[1], refs[2:]
    refs, (p_buf, g_buf, x_buf, o_buf, i_sems, o_sems, w_ref, w_sem) = refs[:-8], refs[-8:]
    weights = pltpu.make_async_copy(all_w.at[:, pl.ds(0, 3 * D)], w_ref, w_sem)
    weights.start()
    frames, places = x_ref.shape[1], x_ref.shape[2]
    group = lax.axis_index("frame") // (lax.axis_size("frame") // batch)

    def input_grads(j):
        clip = turned(group, j, batch)

        def loads(f, slot):
            return [
                pltpu.make_async_copy(projs.at[j, f], p_buf.at[slot], i_sems.at[slot, 0]),
                pltpu.make_async_copy(grads[j].at[f], g_buf.at[slot], i_sems.at[slot, 1]),
                pltpu.make_async_copy(x_ref.at[clip, f], x_buf.at[slot], i_sems.at[slot, 2]),
            ]

        def store(f, slot):
            return pltpu.make_async_copy(o_buf.at[slot], dx_ref.at[clip, f], o_sems.at[slot])

        def one(f, carry):
            slot = lax.rem(f, 2)

            @pl.when(f + 1 < frames)
            def _():
                for copy in loads(f + 1, 1 - slot):
                    copy.start()

            for copy in loads(f, slot):
                copy.wait()

            @pl.when(f >= 2)
            def _():
                store(f - 2, slot).wait()

            back = dot_nt(p_buf[slot, :places, :], w_ref[...])
            hat, inverse = normalize(x_buf[slot].astype(F32))
            grad = g_buf[slot].astype(F32) + normalize_back(back, hat, inverse, table[GAIN : GAIN + 1, :])
            o_buf[slot] = grad.astype(BF16)
            store(f, slot).start()
            return carry

        for copy in loads(0, 0):
            copy.start()
        lax.fori_loop(0, frames, one, 0)
        for f in range(max(frames - 2, 0), frames):
            store(f, f % 2).wait()

    own, from_core, to_x, from_x, to_z, from_z, to_y, from_y = refs[:8]
    low_core, low_to_x, low_x, low_to_z, low_z, low_to_y, low_y = refs[8:15]
    c_send, c_recv, x_send, x_recv, z_send, z_recv, y_send, y_recv = refs[15:23]
    lc_send, lc_recv, lx_send, lx_recv, lz_send, lz_recv, ly_send, ly_recv, local = refs[23:]
    z, x, y, core = position()
    greet(neighbours(depth, height))

    def remote(source, target, send_sem, recv_sem, to):
        return pltpu.make_async_remote_copy(
            src_ref=source, dst_ref=target, send_sem=send_sem, recv_sem=recv_sem, device_id=to, device_id_type=MESH
        )

    def away(d):
        return lax.rem(z + d, depth)

    order = list(range(1, depth)) + [0]
    core_device, x_device = device(z, x, y, 1 - core), device(z, 1 - x, y, core)
    sent = []

    def start(copy):
        copy.start()
        sent.append(copy)
        return copy

    low_c = start(remote(small_ref.at[:, :, 1 - core], low_core, lc_send, lc_recv, core_device))
    c_copies, mine = [], []
    for side in range(2):
        xx = (1 - x) if side == 0 else x
        for d in order:
            slot, block = side * depth + d, 2 * away(d) + xx
            c_copies.append(
                start(
                    remote(
                        part_ref.at[block, :, 1 - core], from_core.at[slot],
                        c_send.at[slot], c_recv.at[slot], core_device,
                    )
                )
            )
            mine.append(pltpu.make_async_copy(part_ref.at[block, :, core], own.at[slot], local.at[slot]))
            mine[-1].start()

    def pair_sum(slot):
        return own[slot].astype(F32) + from_core[slot].astype(F32)

    x_copies = []
    for n, d in enumerate(order):
        mine[n].wait()
        c_copies[n].wait_recv()
        to_x[d] = pair_sum(d).astype(BF16)
        x_copies.append(start(remote(to_x.at[d], from_x.at[d], x_send.at[d], x_recv.at[d], x_device)))
    low_c.wait_recv()
    for zz in range(depth):
        low_to_x[zz] = small_ref[2 * zz + 1 - x, :, core] + low_core[2 * zz + 1 - x]
    low_xc = start(remote(low_to_x, low_x, lx_send, lx_recv, x_device))
    weights.wait()
    for n, d in enumerate(order):
        for j in range(n * batch // depth, (n + 1) * batch // depth):
            input_grads(j)
        mine[depth + n].wait()
        c_copies[depth + n].wait_recv()
        x_copies[n].wait_recv()
        total = pair_sum(depth + d) + from_x[d].astype(F32)
        if d:
            to_z[d] = total.astype(BF16)
            start(remote(to_z.at[d], from_z.at[z], z_send.at[d], z_recv.at[z], device(away(d), x, y, core)))
        else:
            from_z[z] = total.astype(BF16)
    low_xc.wait_recv()
    for d in order:
        block = 2 * away(d) + x
        total = small_ref[block, :, core] + low_core[block] + low_x[away(d)]
        if d:
            low_to_z[d] = total
            start(remote(low_to_z.at[d], low_z.at[z], lz_send.at[d], lz_recv.at[z], device(away(d), x, y, core)))
        else:
            low_z[z] = total
    for d in range(1, depth):
        zz, to = lax.rem(z + depth - d, depth), device(away(d), x, y, core)
        remote(to_z.at[d], from_z.at[zz], z_send.at[d], z_recv.at[zz], to).wait_recv()
        remote(low_to_z.at[d], low_z.at[zz], lz_send.at[d], lz_recv.at[zz], to).wait_recv()

    def over(ref, *row):
        total = ref[(0,) + row].astype(F32)
        for n in range(1, ref.shape[0]):
            total = total + ref[(n,) + row].astype(F32)
        return total

    for d in range(1, height):
        other = lax.rem(y + d, height)
        to = device(z, x, other, core)
        to_y[d] = over(from_z, other).astype(BF16)
        start(remote(to_y.at[d], from_y.at[y], y_send.at[d], y_recv.at[y], to))
        low_to_y[d] = over(low_z, other)
        start(remote(low_to_y.at[d], low_y.at[y], ly_send.at[d], ly_recv.at[y], to))
    from_y[y] = over(from_z, y).astype(BF16)
    low_y[y] = over(low_z, y)
    for d in range(1, height):
        yy, to = lax.rem(y + height - d, height), device(z, x, lax.rem(y + d, height), core)
        remote(to_y.at[d], from_y.at[yy], y_send.at[d], y_recv.at[yy], to).wait_recv()
        remote(low_to_y.at[d], low_y.at[yy], ly_send.at[d], ly_recv.at[yy], to).wait_recv()
    total, at = over(from_y), 0
    for ref in outs:
        ref[...] = total[:, at : at + ref.shape[1]]
        at += ref.shape[1]
    out_small[...] = over(low_y)
    for copy in sent:
        copy.wait_send()


def reduce_rows(block, small, widths, projs, grads, inputs, table, weights):
    clips, frames = lax.axis_size("clip"), lax.axis_size("frame")
    depth, height = clips // 2, frames // 2
    rows = block.shape[0] // (clips * frames)
    sems, tail, low = pltpu.SemaphoreType.DMA, (rows, block.shape[1]), (rows, small.shape[1])
    lead = (clips, height, 2)
    hbm, vmem = pl.BlockSpec(memory_space=pl.ANY), pl.BlockSpec(memory_space=pltpu.VMEM)
    frame = (2,) + inputs.shape[2:]
    return pl.pallas_call(
        functools.partial(reduce_kernel, depth, height, len(widths), len(grads)),
        in_specs=[hbm, vmem, hbm, hbm, vmem, hbm] + [hbm] * len(grads),
        out_specs=[vmem] * (len(widths) + 1) + [hbm],
        out_shape=[jax.ShapeDtypeStruct((rows, width), F32) for width in (*widths, small.shape[1])]
        + [jax.ShapeDtypeStruct(inputs.shape, BF16)],
        scratch_shapes=[
            pltpu.VMEM((2 * depth, height) + tail, BF16),
            pltpu.VMEM((2 * depth, height) + tail, BF16),
            pltpu.VMEM((depth, height) + tail, BF16),
            pltpu.VMEM((depth, height) + tail, BF16),
            pltpu.VMEM((depth, height) + tail, BF16),
            pltpu.VMEM((depth, height) + tail, BF16),
            pltpu.VMEM((height,) + tail, BF16),
            pltpu.VMEM((height,) + tail, BF16),
            pltpu.VMEM((clips, height) + low, F32),
            pltpu.VMEM((depth, height) + low, F32),
            pltpu.VMEM((depth, height) + low, F32),
            pltpu.VMEM((depth, height) + low, F32),
            pltpu.VMEM((depth, height) + low, F32),
            pltpu.VMEM((height,) + low, F32),
            pltpu.VMEM((height,) + low, F32),
            sems((2 * depth,)), sems((2 * depth,)),
            sems((depth,)), sems((depth,)),
            sems((depth,)), sems((depth,)),
            sems((height,)), sems((height,)),
            sems, sems,
            sems, sems,
            sems((depth,)), sems((depth,)),
            sems((height,)), sems((height,)),
            sems((2 * depth,)),
            pltpu.VMEM((2,) + projs.shape[2:], BF16),
            pltpu.VMEM(frame, BF16),
            pltpu.VMEM(frame, BF16),
            pltpu.VMEM(frame, BF16),
            sems((2, 3)), sems((2,)),
            pltpu.VMEM((D, 3 * D), BF16),
            sems,
        ],
        compiler_params=pltpu.CompilerParams(
            collective_id=1, has_side_effects=True, vmem_limit_bytes=60 << 20
        ),
        name="reduce_rows",
    )(block.reshape(lead + tail), small.reshape(lead + low), projs, inputs, table, weights, *grads)


def gather(block):
    return lax.all_gather(block, AXES, axis=0, tiled=True)


def scatter(block):
    return lax.psum_scatter(block, AXES, scatter_dimension=0, tiled=True)


def shards(
    clips_in, teacher, valid, norm_gain, norm_shift, w_space, qv_bias, w_space_out, mix_bias,
    w_time, w_time_out, w_up, up_bias, w_down,
):
    batch, frames, places, _ = clips_in.shape
    ring = lax.axis_size("frame")
    pieces = ring // batch
    chunk = places // pieces
    all_frames = ring * frames
    me = lax.axis_index("frame")
    depth = w_up.shape[0]

    def swap(block, step):
        if step == 0:
            return block
        return lax.ppermute(block, "frame", [(i, i ^ step) for i in range(ring)])

    def clip_of(step):
        return (me // pieces) ^ (step // pieces)

    def place_of(step):
        return ((me % pieces) ^ (step % pieces)) * chunk

    def cut(block, step):
        if pieces == 1:
            return block
        return lax.dynamic_slice_in_dim(block, place_of(step), chunk, 0)

    def spread(block):
        got = []
        for step in range(ring):
            mine = lax.dynamic_index_in_dim(block, clip_of(step), 0, keepdims=False)
            got.append(cut(jnp.swapaxes(mine, 0, 1), step))
        return got

    many = FF // D
    count = jnp.sum(valid)
    counts = jnp.stack([count // 256, count % 256]).astype(BF16)
    smalls = jnp.concatenate(
        [
            norm_gain, norm_shift, qv_bias, mix_bias, up_bias.reshape(depth, many),
            jnp.broadcast_to(counts[None], (depth, 2)),
        ],
        1,
    )
    smalls = jnp.pad(smalls, ((0, 0), (0, SMALL - smalls.shape[1])))
    first = gather_rows(jnp.concatenate([w_space, w_space_out, smalls], 1))
    up_turned = jnp.swapaxes(w_up.reshape(depth, D, many), 1, 2).reshape(depth, FF)
    time_weights = gather(jnp.concatenate([w_time, w_time_out], 1))
    to_feed = jnp.concatenate([up_turned, w_down.reshape(depth, FF)], 1)
    table = jnp.swapaxes(first[:, 4 * D : 4 * D + 24].astype(F32), 0, 1)
    up_row = table[UP : UP + many].reshape(1, FF)
    counted = table[UP + many : UP + many + 2, ::depth]
    total_count = jnp.sum(counted[0]) * 256.0 + jnp.sum(counted[1])
    scale = (2.0 / (total_count * D)).reshape(1, 1)
    table = table[:16]

    order = [((me // pieces) ^ j).astype(jnp.int32) for j in range(batch)]
    clip_ids = [jnp.reshape(c, (1,)) for c in order]
    valid_column = [swap(part, step) for step, part in enumerate(spread(valid))]
    valid_column = jnp.concatenate(valid_column, 1).reshape(-1, 1).astype(F32)
    saved, sent, ins = [None] * batch, [None] * ring, None
    near = min(1, batch - 1)
    turns = [j for j in range(batch - 1, -1, -1) if j != near] + [near]
    cuts = spread(teacher)
    for turn, j in enumerate(turns):
        if turn == 3:
            ins, sent[-1], cuts = lax.optimization_barrier((ins, sent[-1], cuts))
        ins, *kept_j, after = space_forward(clip_ids[j], j, clips_in, table, first, ins)
        saved[j] = kept_j
        after = jnp.swapaxes(after, 0, 1)
        if turn == 0:
            after, to_feed = lax.optimization_barrier((after, to_feed))
        if turn == 1:
            cuts, after = lax.optimization_barrier((cuts, after))
        for r in range(pieces):
            step = j * pieces + r
            sent[step] = swap(cut(after, step), step)
    feed_weights = gather(to_feed)
    teachers = [swap(part, step) for step, part in enumerate(cuts)]
    *saved_b, after_b = time_forward(sent, table, time_weights)
    tile, _ = time_tiles(chunk, all_frames)
    layer_parts, grad_b, d_feed, rows_c, bias_up, squares = feed_forward(
        after_b, teachers, valid_column, scale, table, up_row, feed_weights, tile
    )
    d_feed = scatter(d_feed)
    grad_parts, d_both, rows_b = time_back(grad_b, saved_b, sent, table, time_weights)
    grad_parts = [swap(part, step) for step, part in enumerate(grad_parts)]

    def join(parts, j):
        if pieces == 1:
            return parts[j]
        whole = jnp.zeros((places, frames, D), BF16)
        for r in range(pieces):
            step = j * pieces + r
            whole = lax.dynamic_update_slice_in_dim(whole, parts[step], place_of(step), 0)
        return whole

    outs, biases, projs = [], [], None
    grads = [jnp.swapaxes(join(grad_parts, 0), 0, 1)] + [None] * (batch - 1)
    for j in range(batch):
        projs, d_out, bias = space_back(grads[j], j, batch, saved[j], first, projs)
        outs.append(d_out)
        biases.append(bias)
        if j == batch - 1:
            projs, layer_parts = lax.optimization_barrier((projs, layer_parts))
            layer_parts = [swap(part, step) for step, part in enumerate(layer_parts)]
        if j + 1 < batch:
            following = join(grad_parts, j + 1)
            if j:
                projs, following = lax.optimization_barrier((projs, following))
            grads[j + 1] = jnp.swapaxes(following, 0, 1)
    d_both, small = space_weights(
        ins, projs, first, table, rows_c, rows_b, bias_up.reshape(many, D), squares, outs, biases, d_both
    )
    d_time, d_time_out, d_space, d_space_out, here, input_grad = reduce_rows(
        d_both, small, (3 * D, D, 3 * D, D), projs, grads, clips_in, table, first
    )
    layer_out = place_clips(jnp.stack(order), [join(layer_parts, j) for j in range(batch)])
    d_up = jnp.swapaxes(d_feed[:, :FF].reshape(depth, many, D), 1, 2).reshape(depth, FF)
    return (
        jnp.swapaxes(layer_out, 1, 2),
        here[0, 13 + many] / (total_count * D),
        input_grad,
        here[:, 0:3],
        here[:, 3:6],
        d_space,
        here[:, 6:9],
        here[:, 9],
        d_space_out,
        here[:, 10:13],
        d_time,
        d_time_out,
        d_up.astype(F32),
        here[:, 13 : 13 + many].reshape(-1),
        d_feed[:, FF:].reshape(-1, D).astype(F32),
    )


def solution(mesh):
    tokens, rows = P("clip", "frame", None, None), P(AXES, None)
    in_specs = (tokens, tokens, P("clip", "frame", None)) + (rows,) * 9 + (P(AXES), rows)
    out_specs = (
        (tokens, P(), tokens, rows, rows, rows, rows, P(AXES)) + (rows,) * 5 + (P(AXES), rows)
    )
    return jax.shard_map(shards, mesh=mesh, in_specs=in_specs, out_specs=out_specs, check_vma=False)
```

```python
import functools

import jax
import jax.numpy as jnp
from jax import lax
from jax.experimental import pallas as pl
from jax.experimental.pallas import tpu as pltpu
from jax.sharding import PartitionSpec as P

D = 768
HEADS = 12
HEAD = 64
FF = 3072
EPS = 1e-06
F32 = jnp.float32
BF16 = jnp.bfloat16
PARAMS = pltpu.CompilerParams(vmem_limit_bytes=60 << 20)


def cost(flops, moved=0):
    return pl.CostEstimate(flops=int(flops) // 16, bytes_accessed=int(moved), transcendentals=0)


GAIN, SHIFT, QV, MIX, UP = 0, 3, 6, 10, 13


def dot(left, right):
    return jnp.dot(left, right, preferred_element_type=F32)


def dot_nt(left, right):
    return lax.dot_general(left, right, (((1,), (1,)), ((), ())), preferred_element_type=F32)


def dot_tn(left, right):
    return lax.dot_general(left, right, (((0,), (0,)), ((), ())), preferred_element_type=F32)


def normalize(rows):
    center = rows - jnp.mean(rows, -1, keepdims=True)
    inverse = lax.rsqrt(jnp.mean(center * center, -1, keepdims=True) + EPS)
    return center * inverse, inverse


def normalize_back(grad_out, hat, inverse, gain):
    grad_hat = grad_out * gain
    return inverse * (
        grad_hat
        - jnp.mean(grad_hat, -1, keepdims=True)
        - hat * jnp.mean(grad_hat * hat, -1, keepdims=True)
    )


def column_sum(rows):
    return jnp.sum(rows, 0, keepdims=True)


def first_lanes(shape):
    return lax.broadcasted_iota(jnp.int32, shape, 1) < HEAD


def halves(block):
    low = first_lanes(block.shape)
    zero = jnp.zeros_like(block)
    return jnp.where(low, block, zero), jnp.where(low, zero, block)


def pair(index):
    return slice(2 * HEAD * index, 2 * HEAD * (index + 1))


def grow(block, rows):
    if rows == block.shape[0]:
        return block
    return jnp.concatenate([block, jnp.zeros((rows - block.shape[0], block.shape[1]), block.dtype)], 0)


def stack(block):
    return jnp.concatenate(halves(block), 0)


def merge(two):
    rows = two.shape[0] // 2
    return jnp.where(first_lanes((rows, two.shape[1])), two[:rows], two[rows:])


def kept(rows):
    return HEADS // 2, 2 * padded(rows), rows


def padded(rows):
    return -(-rows // 16) * 16


def attention(units, rows, frames=None):
    full = padded(rows)
    place = lax.broadcasted_iota(jnp.int32, (full, rows), 0)
    if frames is not None:
        mask = place // frames == lax.broadcasted_iota(jnp.int32, (full, rows), 1) // frames
    else:
        mask = place < rows

    def score(unit):
        return dot_nt(stack(grow(unit[1](), full)), unit[0]())

    scores = score(units[0])
    for n, (_, _, value, keep_probs, keep_mix) in enumerate(units):
        now = scores
        if n + 1 < len(units):
            scores = score(units[n + 1])
        probs = []
        for one in (now[:full], now[full:]):
            one = jnp.where(mask, one, -1e30)
            expo = jnp.exp(one - jnp.max(one, 0, keepdims=True))
            probs.append((expo * (1.0 / column_sum(expo))).astype(BF16))
        probs = jnp.concatenate(probs, 0)
        keep_probs(probs)
        keep_mix(dot_tn(probs, stack(grow(value(), full))).astype(BF16))


def attention_back(units, rows):
    full = padded(rows)

    def probs_grad(unit):
        return dot_nt(stack(grow(unit[2](), full)), unit[3]())

    grad_p = probs_grad(units[0])
    for n, (query, key, _, grad_mix, probs_of, keep) in enumerate(units):
        probs = probs_of()
        wide = probs.astype(F32)
        term = wide * grad_p
        grad_s = []
        for head in (slice(0, full), slice(full, 2 * full)):
            grad_s.append((term[head] - wide[head] * column_sum(term[head])).astype(BF16))
        grad_s = jnp.concatenate(grad_s, 0)
        if n + 1 < len(units):
            grad_p = probs_grad(units[n + 1])
        to_v = merge(dot(probs, grad_mix()))
        to_k = merge(dot(grad_s, query()))
        to_q = dot_tn(grad_s, stack(grow(key(), full)))
        keep((to_q * HEAD ** (-0.5)).astype(BF16), to_k[:rows].astype(BF16), to_v[:rows].astype(BF16))


def reader(ref, *index):
    return lambda: ref[index]


def writer(ref, *index):
    def write(value):
        ref[index] = value

    return write


def writer3(ref, lead, rows, p):
    def write(*values):
        for n, value in enumerate(values):
            ref[lead + (rows, pair(n * HEADS // 2 + p))] = value

    return write


def project(rows, weights, table, query_row):
    proj = dot(rows, weights)
    query = (proj[:, :D] + table[query_row : query_row + 1, :]).astype(BF16)
    key = proj[:, D : 2 * D].astype(BF16)
    value = (proj[:, 2 * D :] + table[query_row + 1 : query_row + 2, :]).astype(BF16)
    return (query.astype(F32) * HEAD ** (-0.5)).astype(BF16), key, value


def fixed(shape):
    return pl.BlockSpec(shape, lambda *_: (0,) * len(shape), pipeline_mode=pl.Buffered(1))


def columns_of(width, index):
    return pl.BlockSpec((D, width), lambda *_: (0, index), pipeline_mode=pl.Buffered(1))


def collect(refs, scratch):
    frames = refs[0].shape[1]
    for n, ref in enumerate(refs):
        scratch[:, n * frames : (n + 1) * frames, :] = ref[...].astype(F32)
    return scratch[...].reshape(-1, D)


def deal(rows, scratch, refs):
    frames = refs[0].shape[1]
    scratch[...] = rows.reshape(scratch.shape)
    for n, ref in enumerate(refs):
        ref[...] = scratch[:, n * frames : (n + 1) * frames, :].astype(BF16)


def clear(first, *refs):
    @pl.when(first)
    def _():
        for ref in refs:
            ref[...] = jnp.zeros_like(ref)


def put_rows(ref, value):
    rows, full = value.shape[0], ref.shape[0]
    ref[:rows, :] = value
    if full > rows:
        ref[rows:, :] = jnp.zeros((full - rows, value.shape[1]), value.dtype)


def space_kernel(clip, x_ref, table, w_ref, *refs):
    in_ref, q_ref, k_ref, v_ref, mix_ref, p_ref, out_ref = refs[-7:]
    rows = x_ref[0, 0].astype(F32)
    hat, _ = normalize(rows)
    normed = (hat * table[GAIN : GAIN + 1, :] + table[SHIFT : SHIFT + 1, :]).astype(BF16)
    put_rows(in_ref.at[0, 0], normed)
    q_ref[0], k_ref[0], v_ref[0] = project(normed, w_ref[:, : 3 * D], table, QV)
    every = slice(None)
    attention(
        [
            tuple(reader(ref, 0, every, pair(p)) for ref in (q_ref, k_ref, v_ref))
            + (writer(p_ref, 0, p), writer(mix_ref, 0, every, pair(p)))
            for p in range(HEADS // 2)
        ],
        rows.shape[0],
    )
    after = rows + dot(mix_ref[0], w_ref[:, 3 * D : 4 * D]) + table[MIX : MIX + 1, :]
    out_ref[0] = after.astype(BF16)


def space_forward(clip, step, inputs, table, weights, before):
    batch, frames, places, _ = inputs.shape
    full = padded(places)
    more = [] if before is None else [before]

    def frame(*tail):
        return pl.BlockSpec((1,) + tail, lambda i, c: (i,) + (0,) * len(tail))

    def shape(*tail):
        return jax.ShapeDtypeStruct((frames,) + tail, BF16)

    return pl.pallas_call(
        space_kernel,
        grid_spec=pltpu.PrefetchScalarGridSpec(
            num_scalar_prefetch=1,
            grid=(frames,),
            in_specs=[
                pl.BlockSpec((1, 1, places, D), lambda i, c: (c[0], i, 0, 0)),
                fixed(table.shape),
                columns_of(4 * D, 0),
            ]
            + [pl.BlockSpec(memory_space=pl.ANY) for _ in more],
            out_specs=[pl.BlockSpec((1, 1, full, D), lambda i, c: (step, i, 0, 0))]
            + [frame(places, D)] * 4
            + [frame(*kept(places)), frame(places, D)],
        ),
        out_shape=[jax.ShapeDtypeStruct((batch, frames, full, D), BF16)]
        + [shape(places, D)] * 4
        + [shape(*kept(places)), shape(places, D)],
        input_output_aliases={4: 0} if more else {},
        compiler_params=PARAMS,
        cost_estimate=cost(24 * frames * places * D * D),
        name="space_forward",
    )(clip, inputs, table, weights, *more)


def largest_divisor(number, limit):
    return max(n for n in range(1, limit + 1) if number % n == 0)


def time_kernel(frames, group, ring, *refs):
    parts, (table, w_ref) = refs[:ring], refs[ring : ring + 2]
    a_ref, in_ref, q_ref, k_ref, v_ref, mix_ref, p_ref, out_ref, scratch = refs[ring + 2 :]
    rows = collect(parts, scratch)
    a_ref[...] = rows.astype(BF16)
    hat, _ = normalize(rows)
    normed = (hat * table[GAIN + 1 : GAIN + 2, :] + table[SHIFT + 1 : SHIFT + 2, :]).astype(BF16)
    in_ref[...] = normed
    q_ref[...], k_ref[...], v_ref[...] = project(normed, w_ref[:, : 3 * D], table, QV + 2)
    units = []
    for g in range(rows.shape[0] // group):
        span = slice(g * group, (g + 1) * group)
        for p in range(HEADS // 2):
            units.append(
                tuple(reader(ref, span, pair(p)) for ref in (q_ref, k_ref, v_ref))
                + (writer(p_ref, g, p), writer(mix_ref, span, pair(p)))
            )
    attention(units, group, frames)
    out_ref[...] = rows + dot(mix_ref[...], w_ref[:, 3 * D :]) + table[MIX + 1 : MIX + 2, :]


def time_tiles(places, frames):
    per_group = largest_divisor(places, 128 // frames)
    per_tile = per_group * largest_divisor(places // per_group, 4)
    return per_tile * frames, per_group * frames


def piece_specs(parts, tile):
    frames = parts[0].shape[1]
    places = tile // (frames * len(parts))
    return [pl.BlockSpec((places, frames, D), lambda i: (i, 0, 0))] * len(parts)


def join_scratch(parts, tile):
    frames = parts[0].shape[1] * len(parts)
    return pltpu.VMEM((tile // frames, frames, D), F32)


def time_forward(parts, table, weights):
    places, frames = parts[0].shape[0], parts[0].shape[1] * len(parts)
    tokens = places * frames
    tile, group = time_tiles(places, frames)
    rows = pl.BlockSpec((tile, D), lambda i: (i, 0))
    return pl.pallas_call(
        functools.partial(time_kernel, frames, group, len(parts)),
        grid=(tokens // tile,),
        in_specs=piece_specs(parts, tile) + [fixed(table.shape), columns_of(4 * D, 0)],
        out_specs=[rows] * 6
        + [pl.BlockSpec((tile // group,) + kept(group), lambda i: (i, 0, 0, 0)), rows],
        out_shape=[jax.ShapeDtypeStruct((tokens, D), BF16)] * 6
        + [
            jax.ShapeDtypeStruct((tokens // group,) + kept(group), BF16),
            jax.ShapeDtypeStruct((tokens, D), F32),
        ],
        scratch_shapes=[join_scratch(parts, tile)],
        compiler_params=PARAMS,
        cost_estimate=cost(24 * tokens * D * D),
        name="time_forward",
    )(*parts, table, weights)


def gelu_parts(u):
    area = 0.5 + 0.5 * lax.erf(u * 0.7071067811865476)
    bell = jnp.exp2((-0.5 * 1.4426950408889634) * (u * u))
    return u * area, area + 0.3989422804014327 * (u * bell)


FF_CHUNK = 768


def feed_kernel(ring, *refs):
    teachers, refs = refs[:ring], refs[ring:]
    (a_ref, valid_ref, scale_ref, table, up_bias, up_ref, down_ref), refs = refs[:7], refs[7:]
    outs, refs = refs[:ring], refs[ring:]
    g_ref, d_ref, rows_ref, bias_ref, square_ref, hidden, slope, d_up, d_down, stage, sems, scratch = refs
    step, last = pl.program_id(0), pl.num_programs(0) - 1
    clear(step == 0, d_up, d_down, rows_ref, bias_ref, square_ref)
    after = a_ref[...]
    hat, inverse = normalize(after)
    normed = (hat * table[GAIN + 2 : GAIN + 3, :] + table[SHIFT + 2 : SHIFT + 3, :]).astype(BF16)
    total = after + table[MIX + 2 : MIX + 3, :]
    chunks = [slice(c, c + FF_CHUNK) for c in range(0, FF, FF_CHUNK)]
    for c in chunks:
        act, rise = gelu_parts(dot(normed, up_ref[:, c]) + up_bias[:, c])
        act = act.astype(BF16)
        hidden[:, c] = act
        slope[:, c] = rise.astype(BF16)
        total = total + dot(act, down_ref[:, c])
    deal(total, scratch, outs)
    diff = (total - collect(teachers, scratch)) * valid_ref[...]
    square_ref[...] += column_sum(diff * diff)
    grad = diff * scale_ref[0, 0]
    grad_low = grad.astype(BF16)
    bias_c = column_sum(grad_low.astype(F32))
    back = jnp.zeros_like(grad)
    for c in chunks:
        grad_pre = dot_nt(grad_low, down_ref[:, c]) * slope[:, c].astype(F32)
        grad_pre = grad_pre.astype(BF16)
        bias_ref[:, c] += column_sum(grad_pre.astype(F32))
        d_down[:, c] += dot_tn(hidden[:, c], grad_low)
        d_up[:, c] += dot_tn(normed, grad_pre)
        back = back + dot_nt(grad_pre, up_ref[:, c])
    rows_ref[...] += jnp.concatenate([column_sum(back * hat), column_sum(back), bias_c], 0)
    g_ref[...] = grad + normalize_back(back, hat, inverse, table[GAIN + 2 : GAIN + 3, :])

    @pl.when(step == last)
    def _():
        moves = []
        for source, start in ((d_up, 0), (d_down, FF)):
            moves += [(source.at[:, c], d_ref.at[:, start + c.start : start + c.stop]) for c in chunks]
        flush(moves, stage, sems)


def flush(moves, stage, sems):
    copies = []
    for i, (source, target) in enumerate(moves):
        if i >= 2:
            copies[i - 2].wait()
        stage[i % 2] = source[...].astype(BF16)
        copies.append(pltpu.make_async_copy(stage.at[i % 2], target, sems.at[i % 2]))
        copies[i].start()
    for copy in copies[-2:]:
        copy.wait()


def feed_forward(after_b, teachers, valid, scale, table, up_bias, weights, tile):
    tokens, ring = after_b.shape[0], len(teachers)
    rows = pl.BlockSpec((tile, D), lambda i: (i, 0))
    *outs, grad, d_feed, sums, bias, squares = pl.pallas_call(
        functools.partial(feed_kernel, ring),
        grid=(tokens // tile,),
        in_specs=piece_specs(teachers, tile)
        + [
            rows,
            pl.BlockSpec((tile, 1), lambda i: (i, 0)),
            pl.BlockSpec(memory_space=pltpu.SMEM),
            fixed(table.shape),
            fixed((1, FF)),
            columns_of(FF, 0),
            columns_of(FF, 1),
        ],
        out_specs=piece_specs(teachers, tile)
        + [rows, pl.BlockSpec(memory_space=pl.ANY), fixed((3, D)), fixed((1, FF)), fixed((1, D))],
        out_shape=[jax.ShapeDtypeStruct(t.shape, BF16) for t in teachers]
        + [
            jax.ShapeDtypeStruct((tokens, D), F32),
            jax.ShapeDtypeStruct((D, 2 * FF), BF16),
            jax.ShapeDtypeStruct((3, D), F32),
            jax.ShapeDtypeStruct((1, FF), F32),
            jax.ShapeDtypeStruct((1, D), F32),
        ],
        scratch_shapes=[
            pltpu.VMEM((tile, FF), BF16),
            pltpu.VMEM((tile, FF), BF16),
            pltpu.VMEM((D, FF), F32),
            pltpu.VMEM((D, FF), F32),
            pltpu.VMEM((2, D, FF_CHUNK), BF16),
            pltpu.SemaphoreType.DMA((2,)),
            join_scratch(teachers, tile),
        ],
        compiler_params=PARAMS,
        cost_estimate=cost(80 * tokens * D * D),
        name="feed_forward",
    )(*teachers, after_b, valid, scale, table, up_bias, weights, weights)
    return outs, grad, d_feed, sums, bias, squares


def time_back_kernel(group, ring, *refs):
    (g_ref, a_ref, in_ref, q_ref, k_ref, v_ref, mix_ref, p_ref, table, w_ref), refs = refs[:10], refs[10:]
    outs, refs = refs[:ring], refs[ring:]
    d_ref, rows_ref, grad_mix, grad_proj, d_proj, d_out, stage, sems, scratch = refs
    step, last = pl.program_id(0), pl.num_programs(0) - 1
    clear(step == 0, d_proj, d_out, rows_ref)
    grad = g_ref[...]
    grad_low = grad.astype(BF16)
    d_out[...] += dot_tn(mix_ref[...], grad_low)
    grad_mix[...] = dot_nt(grad_low, w_ref[:, 3 * D :]).astype(BF16)

    units = []
    for g in range(grad.shape[0] // group):
        span = slice(g * group, (g + 1) * group)
        for p in range(HEADS // 2):
            units.append(
                tuple(reader(ref, span, pair(p)) for ref in (q_ref, k_ref, v_ref, grad_mix))
                + (reader(p_ref, g, p), writer3(grad_proj, (), span, p))
            )
    attention_back(units, group)
    proj = grad_proj[...]
    d_proj[...] += dot_tn(in_ref[...], proj)
    sums = column_sum(proj.astype(F32))
    back = dot_nt(proj, w_ref[:, : 3 * D])
    hat, inverse = normalize(a_ref[...].astype(F32))
    rows_ref[...] += jnp.concatenate(
        [
            column_sum(back * hat),
            column_sum(back),
            sums[:, :D],
            sums[:, 2 * D :],
            column_sum(grad_low.astype(F32)),
        ],
        0,
    )
    deal(grad + normalize_back(back, hat, inverse, table[GAIN + 1 : GAIN + 2, :]), scratch, outs)

    @pl.when(step == last)
    def _():
        moves = [(d_proj.at[:, pl.ds(c * D, D)], d_ref.at[:, pl.ds(c * D, D)]) for c in range(3)]
        flush(moves + [(d_out, d_ref.at[:, pl.ds(3 * D, D)])], stage, sems)


def time_back(grad, saved, like, table, weights):
    ring, tokens = len(like), grad.shape[0]
    places, frames = like[0].shape[0], like[0].shape[1] * ring
    tile, group = time_tiles(places, frames)
    rows = pl.BlockSpec((tile, D), lambda i: (i, 0))
    *outs, d_time, sums = pl.pallas_call(
        functools.partial(time_back_kernel, group, ring),
        grid=(tokens // tile,),
        in_specs=[rows] * 7
        + [
            pl.BlockSpec((tile // group,) + kept(group), lambda i: (i, 0, 0, 0)),
            fixed(table.shape),
            columns_of(4 * D, 0),
        ],
        out_specs=piece_specs(like, tile) + [pl.BlockSpec(memory_space=pl.ANY), fixed((5, D))],
        out_shape=[jax.ShapeDtypeStruct(t.shape, BF16) for t in like]
        + [jax.ShapeDtypeStruct((D, 8 * D), BF16), jax.ShapeDtypeStruct((5, D), F32)],
        scratch_shapes=[
            pltpu.VMEM((tile, D), BF16),
            pltpu.VMEM((tile, 3 * D), BF16),
            pltpu.VMEM((D, 3 * D), F32),
            pltpu.VMEM((D, D), F32),
            pltpu.VMEM((2, D, D), BF16),
            pltpu.SemaphoreType.DMA((2,)),
            join_scratch(like, tile),
        ],
        compiler_params=PARAMS,
        cost_estimate=cost(42 * tokens * D * D),
        name="time_back",
    )(grad, *saved, table, weights)
    return outs, d_time, sums


def space_back_kernel(g_ref, q_ref, k_ref, v_ref, mix_ref, p_ref, w_ref, *refs):
    out_ref, d_ref, bias_ref, grad_mix = refs[-4:]
    clear(pl.program_id(0) == 0, d_ref, bias_ref)
    grad = g_ref[0]
    rows, full = grad.shape[0], out_ref.shape[2]
    d_ref[...] += dot_tn(mix_ref[0], grad)
    bias_ref[...] += column_sum(grad.astype(F32))
    grad_mix[...] = dot_nt(grad, w_ref[...]).astype(BF16)
    every = slice(None)
    attention_back(
        [
            tuple(reader(ref, 0, every, pair(p)) for ref in (q_ref, k_ref, v_ref))
            + (reader(grad_mix, every, pair(p)), reader(p_ref, 0, p))
            + (writer3(out_ref, (0, 0), slice(0, rows), p),)
            for p in range(HEADS // 2)
        ],
        rows,
    )
    if full > rows:
        out_ref[0, 0, rows:, :] = jnp.zeros((full - rows, out_ref.shape[3]), BF16)


def space_back(grad, step, batch, saved, weights, before):
    frames, places, _ = grad.shape
    full = padded(places)
    more = [] if before is None else [before]

    def frame(*tail):
        return pl.BlockSpec((1,) + tail, lambda i: (i,) + (0,) * len(tail))

    return pl.pallas_call(
        space_back_kernel,
        grid=(frames,),
        in_specs=[frame(places, D)] * 5
        + [frame(*kept(places)), columns_of(D, 3)]
        + [pl.BlockSpec(memory_space=pl.ANY) for _ in more],
        out_specs=[
            pl.BlockSpec((1, 1, full, 3 * D), lambda i: (step, i, 0, 0)),
            fixed((D, D)),
            fixed((1, D)),
        ],
        out_shape=[
            jax.ShapeDtypeStruct((batch, frames, full, 3 * D), BF16),
            jax.ShapeDtypeStruct((D, D), F32),
            jax.ShapeDtypeStruct((1, D), F32),
        ],
        scratch_shapes=[pltpu.VMEM((places, D), BF16)],
        input_output_aliases={7: 0} if more else {},
        compiler_params=PARAMS,
        cost_estimate=cost(24 * frames * places * D * D),
        name="space_back",
    )(grad, *saved, weights, *more)


SMALL = 128


def space_part_kernel(in_ref, proj_ref, d_proj, sums):
    clear(pl.program_id(0) == 0, d_proj, sums)
    proj = proj_ref[0].reshape(-1, 3 * D)
    d_proj[...] += dot_tn(in_ref[0].reshape(-1, D), proj)
    sums[...] += column_sum(proj.astype(F32))


def space_part(ins, projs):
    batch, frames, full, _ = ins.shape

    def clip(width):
        return pl.BlockSpec((1, frames, full, width), lambda i: (i, 0, 0, 0))

    return pl.pallas_call(
        space_part_kernel,
        grid=(batch - 1,),
        in_specs=[clip(D), clip(3 * D)],
        out_specs=[fixed((D, 3 * D)), fixed((1, 3 * D))],
        out_shape=[jax.ShapeDtypeStruct((D, 3 * D), F32), jax.ShapeDtypeStruct((1, 3 * D), F32)],
        compiler_params=PARAMS,
        cost_estimate=cost(18 * (batch - 1) * frames * full * D * D),
        name="space_part",
    )(ins, projs)


def space_weight_kernel(parts, in_ref, proj_ref, d_before, sums_before, w_ref, table, c_ref, b_ref, up_ref, square_ref, *refs):
    outs, biases, refs = refs[:parts], refs[parts : 2 * parts], refs[2 * parts + 1 :]
    d_ref, small_ref, d_proj, d_out, sums, rows, stage, sems = refs
    rows[...] = jnp.zeros_like(rows)
    proj = proj_ref[0].reshape(-1, 3 * D)
    d_proj[...] = d_before[...] + dot_tn(in_ref[0].reshape(-1, D), proj)
    sums[...] = sums_before[...] + column_sum(proj.astype(F32))

    @pl.when(pl.program_id(0) == 0)
    def _():
        d_out[...] = sum(ref[...] for ref in outs)
        moves = [(d_proj.at[:, pl.ds(c * D, D)], d_ref.at[:, pl.ds((4 + c) * D, D)]) for c in range(3)]
        flush(moves + [(d_out, d_ref.at[:, pl.ds(7 * D, D)])], stage, sems)
        many = up_ref.shape[0]
        rows[1:2, :], rows[2:3, :] = b_ref[0:1, :], c_ref[0:1, :]
        rows[4:5, :], rows[5:6, :] = b_ref[1:2, :], c_ref[1:2, :]
        rows[6:7, :], rows[7:8, :] = sums[:, :D], sums[:, 2 * D :]
        rows[8:9, :], rows[9:10, :] = b_ref[3:4, :], b_ref[2:3, :]
        rows[10:11, :] = sum(ref[...] for ref in biases)
        rows[11:12, :], rows[12:13, :] = b_ref[4:5, :], c_ref[2:3, :]
        rows[13 : 13 + many, :] = up_ref[...]
        square = jnp.sum(square_ref[...], -1, keepdims=True)
        rows[13 + many : 14 + many, :] = jnp.broadcast_to(square, square_ref.shape)
        rows[SMALL - 2 : SMALL - 1, :] = table[GAIN : GAIN + 1, :]
        rows[SMALL - 1 : SMALL, :] = table[SHIFT : SHIFT + 1, :]
        columns = jnp.swapaxes(rows[...], 0, 1)
        wide = w_ref[...].astype(F32)
        with_grad = jnp.sum(wide * d_proj[...], -1, keepdims=True)
        shift_grad = jnp.sum(wide * sums[...], -1, keepdims=True)
        gain, shift = columns[:, SMALL - 2 : SMALL - 1], columns[:, SMALL - 1 :]
        gain_grad = (with_grad - shift * shift_grad) / gain
        lane = lax.broadcasted_iota(jnp.int32, columns.shape, 1)
        small_ref[...] = jnp.where(lane == 0, gain_grad, jnp.where(lane == 3, shift_grad, columns))


def space_weights(ins, projs, before, weights, table, rows_c, rows_b, bias_up, squares, outs, biases, matrix):
    batch, frames, full, _ = ins.shape

    def clip(width):
        return pl.BlockSpec((1, frames, full, width), lambda i: (batch - 1, 0, 0, 0))

    smalls = [table, rows_c, rows_b, bias_up, squares]
    return pl.pallas_call(
        functools.partial(space_weight_kernel, batch),
        grid=(1,),
        in_specs=[clip(D), clip(3 * D), fixed((D, 3 * D)), fixed((1, 3 * D)), columns_of(3 * D, 0)]
        + [fixed(a.shape) for a in smalls]
        + [fixed((D, D))] * batch
        + [fixed((1, D))] * batch
        + [pl.BlockSpec(memory_space=pl.ANY)],
        out_specs=[pl.BlockSpec(memory_space=pl.ANY), fixed((D, SMALL))],
        out_shape=[jax.ShapeDtypeStruct(matrix.shape, BF16), jax.ShapeDtypeStruct((D, SMALL), F32)],
        input_output_aliases={10 + 2 * batch: 0},
        scratch_shapes=[
            pltpu.VMEM((D, 3 * D), F32),
            pltpu.VMEM((D, D), F32),
            pltpu.VMEM((1, 3 * D), F32),
            pltpu.VMEM((SMALL, D), F32),
            pltpu.VMEM((2, D, D), BF16),
            pltpu.SemaphoreType.DMA((2,)),
        ],
        compiler_params=PARAMS,
        cost_estimate=cost(18 * frames * full * D * D),
        name="space_weights",
    )(ins, projs, *before, weights, *smalls, *outs, *biases, matrix)


def place_kernel(order, *refs):
    blocks, out_ref = refs[:-1], refs[-1]
    for n, ref in enumerate(blocks):

        @pl.when(pl.program_id(0) == n)
        def _():
            out_ref[0] = ref[...]


def place_clips(order, blocks):
    shape = blocks[0].shape
    return pl.pallas_call(
        place_kernel,
        grid_spec=pltpu.PrefetchScalarGridSpec(
            num_scalar_prefetch=1,
            grid=(len(blocks),),
            in_specs=[fixed(shape)] * len(blocks),
            out_specs=pl.BlockSpec((1,) + shape, lambda i, order: (order[i], 0, 0, 0)),
        ),
        out_shape=jax.ShapeDtypeStruct((len(blocks),) + shape, BF16),
        compiler_params=PARAMS,
        name="place_clips",
    )(order, *blocks)


AXES = ("clip", "frame")
MESH = pl.DeviceIdType.MESH


def position():
    clip, frame = lax.axis_index("clip"), lax.axis_index("frame")
    return clip // 2, clip % 2, frame // 2, frame % 2


def device(z, x, y, core):
    return (2 * z + x, 2 * y + core)


def greet(partners):
    barrier = pltpu.get_barrier_semaphore()
    for partner in partners:
        pl.semaphore_signal(barrier, inc=1, device_id=partner, device_id_type=MESH)
    pl.semaphore_wait(barrier, len(partners))


def neighbours(depth, height):
    z, x, y, core = position()
    return (
        [device(lax.rem(z + d, depth), x, y, core) for d in range(1, depth)]
        + [device(z, x, lax.rem(y + d, height), core) for d in range(1, height)]
        + [device(z, 1 - x, y, core), device(z, x, y, 1 - core)]
    )


def gather_kernel(depth, height, in_ref, out_ref, local, y_send, y_recv, z_send, z_recv, x_send, x_recv, c_send, c_recv):
    z, x, y, core = position()
    greet(neighbours(depth, height))

    def send(source, target, sems, slot, index, to):
        copy = pltpu.make_async_remote_copy(
            src_ref=source, dst_ref=target, send_sem=sems[0].at[slot], recv_sem=sems[1].at[index],
            device_id=to, device_id_type=MESH,
        )
        copy.start()
        return copy

    def block(zz, xx, cc):
        return out_ref.at[2 * zz + xx, :, cc]

    def arrival(ref, sem):
        return pltpu.make_async_remote_copy(
            src_ref=ref, dst_ref=ref, send_sem=sem, recv_sem=sem, device_id=device(z, 1 - x, y, core), device_id_type=MESH
        )

    sent = []
    own = out_ref.at[2 * z + x, y, core]
    for d in range(1, height):
        sent.append(send(in_ref, own, (y_send, y_recv), d - 1, y, device(z, x, lax.rem(y + d, height), core)))
    mine = pltpu.make_async_copy(in_ref, own, local)
    mine.start()
    mine.wait()
    for d in range(1, height):
        other = lax.rem(y + height - d, height)
        arrival(out_ref.at[2 * z + x, other, core], y_recv.at[other]).wait_recv()
    here = block(z, x, core)
    for d in range(1, depth):
        sent.append(send(here, here, (z_send, z_recv), d - 1, z, device(lax.rem(z + d, depth), x, y, core)))

    def to_x(step, zz):
        sent.append(send(block(zz, x, core), block(zz, x, core), (x_send, x_recv), step, zz, device(z, 1 - x, y, core)))

    def to_core(step, zz, xx):
        sent.append(
            send(block(zz, xx, core), block(zz, xx, core), (c_send, c_recv), step, 2 * zz + xx, device(z, x, y, 1 - core))
        )

    to_x(0, z)
    to_core(0, z, x)
    for d in range(1, depth):
        zz = lax.rem(z + depth - d, depth)
        arrival(block(zz, x, core), z_recv.at[zz]).wait_recv()
        to_x(d, zz)
        to_core(d, zz, x)
    for d in range(depth):
        zz = lax.rem(z + depth - d, depth)
        arrival(block(zz, 1 - x, core), x_recv.at[zz]).wait_recv()
        to_core(depth + d, zz, 1 - x)
    for d in range(depth):
        zz = lax.rem(z + depth - d, depth)
        arrival(block(zz, x, 1 - core), c_recv.at[2 * zz + x]).wait_recv()
        arrival(block(zz, 1 - x, 1 - core), c_recv.at[2 * zz + 1 - x]).wait_recv()
    for copy in sent:
        copy.wait_send()


def gather_rows(block):
    clips, frames = lax.axis_size("clip"), lax.axis_size("frame")
    depth, height = clips // 2, frames // 2
    sems = pltpu.SemaphoreType.DMA
    out = pl.pallas_call(
        functools.partial(gather_kernel, depth, height),
        in_specs=[pl.BlockSpec(memory_space=pl.ANY)],
        out_specs=pl.BlockSpec(memory_space=pl.ANY),
        out_shape=jax.ShapeDtypeStruct((clips, height, 2) + block.shape, block.dtype),
        scratch_shapes=[
            sems,
            sems((max(height - 1, 1),)), sems((height,)),
            sems((depth - 1,)), sems((depth,)),
            sems((depth,)), sems((depth,)),
            sems((clips,)), sems((clips,)),
        ],
        compiler_params=pltpu.CompilerParams(collective_id=0, has_side_effects=True),
        name="gather_rows",
    )(block)
    return out.reshape(-1, block.shape[1])


def turned(number, flips, size):
    total, bit = 0, 1
    while bit < size:
        value = (number // bit) % 2
        total = total + bit * (1 - value if flips & bit else value)
        bit *= 2
    return total


def reduce_kernel(depth, height, many, batch, part_ref, small_ref, projs, x_ref, table, all_w, *refs):
    grads, outs, refs = refs[:batch], refs[batch : batch + many], refs[batch + many :]
    out_small, dx_ref, refs = refs[0], refs[1], refs[2:]
    refs, (p_buf, g_buf, x_buf, o_buf, i_sems, o_sems, w_ref, w_sem) = refs[:-8], refs[-8:]
    weights = pltpu.make_async_copy(all_w.at[:, pl.ds(0, 3 * D)], w_ref, w_sem)
    weights.start()
    frames, places = x_ref.shape[1], x_ref.shape[2]
    group = lax.axis_index("frame") // (lax.axis_size("frame") // batch)

    def input_grads(j):
        clip = turned(group, j, batch)

        def loads(f, slot):
            return [
                pltpu.make_async_copy(projs.at[j, f], p_buf.at[slot], i_sems.at[slot, 0]),
                pltpu.make_async_copy(grads[j].at[f], g_buf.at[slot], i_sems.at[slot, 1]),
                pltpu.make_async_copy(x_ref.at[clip, f], x_buf.at[slot], i_sems.at[slot, 2]),
            ]

        def store(f, slot):
            return pltpu.make_async_copy(o_buf.at[slot], dx_ref.at[clip, f], o_sems.at[slot])

        def one(f, carry):
            slot = lax.rem(f, 2)

            @pl.when(f + 1 < frames)
            def _():
                for copy in loads(f + 1, 1 - slot):
                    copy.start()

            for copy in loads(f, slot):
                copy.wait()

            @pl.when(f >= 2)
            def _():
                store(f - 2, slot).wait()

            back = dot_nt(p_buf[slot, :places, :], w_ref[...])
            hat, inverse = normalize(x_buf[slot].astype(F32))
            grad = g_buf[slot].astype(F32) + normalize_back(back, hat, inverse, table[GAIN : GAIN + 1, :])
            o_buf[slot] = grad.astype(BF16)
            store(f, slot).start()
            return carry

        for copy in loads(0, 0):
            copy.start()
        lax.fori_loop(0, frames, one, 0)
        for f in range(max(frames - 2, 0), frames):
            store(f, f % 2).wait()

    own, from_core, to_x, from_x, to_z, from_z, to_y, from_y = refs[:8]
    low_core, low_to_x, low_x, low_to_z, low_z, low_to_y, low_y = refs[8:15]
    c_send, c_recv, x_send, x_recv, z_send, z_recv, y_send, y_recv = refs[15:23]
    lc_send, lc_recv, lx_send, lx_recv, lz_send, lz_recv, ly_send, ly_recv, local = refs[23:]
    z, x, y, core = position()
    greet(neighbours(depth, height))

    def remote(source, target, send_sem, recv_sem, to):
        return pltpu.make_async_remote_copy(
            src_ref=source, dst_ref=target, send_sem=send_sem, recv_sem=recv_sem, device_id=to, device_id_type=MESH
        )

    def away(d):
        return lax.rem(z + d, depth)

    order = list(range(1, depth)) + [0]
    core_device, x_device = device(z, x, y, 1 - core), device(z, 1 - x, y, core)
    sent = []

    def start(copy):
        copy.start()
        sent.append(copy)
        return copy

    low_c = start(remote(small_ref.at[:, :, 1 - core], low_core, lc_send, lc_recv, core_device))
    c_copies, mine = [], []
    for side in range(2):
        xx = (1 - x) if side == 0 else x
        for d in order:
            slot, block = side * depth + d, 2 * away(d) + xx
            c_copies.append(
                start(
                    remote(
                        part_ref.at[block, :, 1 - core], from_core.at[slot],
                        c_send.at[slot], c_recv.at[slot], core_device,
                    )
                )
            )
            mine.append(pltpu.make_async_copy(part_ref.at[block, :, core], own.at[slot], local.at[slot]))
            mine[-1].start()

    def pair_sum(slot):
        return own[slot].astype(F32) + from_core[slot].astype(F32)

    x_copies = []
    for n, d in enumerate(order):
        mine[n].wait()
        c_copies[n].wait_recv()
        to_x[d] = pair_sum(d).astype(BF16)
        x_copies.append(start(remote(to_x.at[d], from_x.at[d], x_send.at[d], x_recv.at[d], x_device)))
    low_c.wait_recv()
    for zz in range(depth):
        low_to_x[zz] = small_ref[2 * zz + 1 - x, :, core] + low_core[2 * zz + 1 - x]
    low_xc = start(remote(low_to_x, low_x, lx_send, lx_recv, x_device))
    weights.wait()
    for n, d in enumerate(order):
        for j in range(n * batch // depth, (n + 1) * batch // depth):
            input_grads(j)
        mine[depth + n].wait()
        c_copies[depth + n].wait_recv()
        x_copies[n].wait_recv()
        total = pair_sum(depth + d) + from_x[d].astype(F32)
        if d:
            to_z[d] = total.astype(BF16)
            start(remote(to_z.at[d], from_z.at[z], z_send.at[d], z_recv.at[z], device(away(d), x, y, core)))
        else:
            from_z[z] = total.astype(BF16)
    low_xc.wait_recv()
    for d in order:
        block = 2 * away(d) + x
        total = small_ref[block, :, core] + low_core[block] + low_x[away(d)]
        if d:
            low_to_z[d] = total
            start(remote(low_to_z.at[d], low_z.at[z], lz_send.at[d], lz_recv.at[z], device(away(d), x, y, core)))
        else:
            low_z[z] = total
    for d in range(1, depth):
        zz, to = lax.rem(z + depth - d, depth), device(away(d), x, y, core)
        remote(to_z.at[d], from_z.at[zz], z_send.at[d], z_recv.at[zz], to).wait_recv()
        remote(low_to_z.at[d], low_z.at[zz], lz_send.at[d], lz_recv.at[zz], to).wait_recv()

    def over(ref, *row):
        total = ref[(0,) + row].astype(F32)
        for n in range(1, ref.shape[0]):
            total = total + ref[(n,) + row].astype(F32)
        return total

    for d in range(1, height):
        other = lax.rem(y + d, height)
        to = device(z, x, other, core)
        to_y[d] = over(from_z, other).astype(BF16)
        start(remote(to_y.at[d], from_y.at[y], y_send.at[d], y_recv.at[y], to))
        low_to_y[d] = over(low_z, other)
        start(remote(low_to_y.at[d], low_y.at[y], ly_send.at[d], ly_recv.at[y], to))
    from_y[y] = over(from_z, y).astype(BF16)
    low_y[y] = over(low_z, y)
    for d in range(1, height):
        yy, to = lax.rem(y + height - d, height), device(z, x, lax.rem(y + d, height), core)
        remote(to_y.at[d], from_y.at[yy], y_send.at[d], y_recv.at[yy], to).wait_recv()
        remote(low_to_y.at[d], low_y.at[yy], ly_send.at[d], ly_recv.at[yy], to).wait_recv()
    total, at = over(from_y), 0
    for ref in outs:
        ref[...] = total[:, at : at + ref.shape[1]]
        at += ref.shape[1]
    out_small[...] = over(low_y)
    for copy in sent:
        copy.wait_send()


def reduce_rows(block, small, widths, projs, grads, inputs, table, weights):
    clips, frames = lax.axis_size("clip"), lax.axis_size("frame")
    depth, height = clips // 2, frames // 2
    rows = block.shape[0] // (clips * frames)
    sems, tail, low = pltpu.SemaphoreType.DMA, (rows, block.shape[1]), (rows, small.shape[1])
    lead = (clips, height, 2)
    hbm, vmem = pl.BlockSpec(memory_space=pl.ANY), pl.BlockSpec(memory_space=pltpu.VMEM)
    frame = (2,) + inputs.shape[2:]
    return pl.pallas_call(
        functools.partial(reduce_kernel, depth, height, len(widths), len(grads)),
        in_specs=[hbm, vmem, hbm, hbm, vmem, hbm] + [hbm] * len(grads),
        out_specs=[vmem] * (len(widths) + 1) + [hbm],
        out_shape=[jax.ShapeDtypeStruct((rows, width), F32) for width in (*widths, small.shape[1])]
        + [jax.ShapeDtypeStruct(inputs.shape, BF16)],
        scratch_shapes=[
            pltpu.VMEM((2 * depth, height) + tail, BF16),
            pltpu.VMEM((2 * depth, height) + tail, BF16),
            pltpu.VMEM((depth, height) + tail, BF16),
            pltpu.VMEM((depth, height) + tail, BF16),
            pltpu.VMEM((depth, height) + tail, BF16),
            pltpu.VMEM((depth, height) + tail, BF16),
            pltpu.VMEM((height,) + tail, BF16),
            pltpu.VMEM((height,) + tail, BF16),
            pltpu.VMEM((clips, height) + low, F32),
            pltpu.VMEM((depth, height) + low, F32),
            pltpu.VMEM((depth, height) + low, F32),
            pltpu.VMEM((depth, height) + low, F32),
            pltpu.VMEM((depth, height) + low, F32),
            pltpu.VMEM((height,) + low, F32),
            pltpu.VMEM((height,) + low, F32),
            sems((2 * depth,)), sems((2 * depth,)),
            sems((depth,)), sems((depth,)),
            sems((depth,)), sems((depth,)),
            sems((height,)), sems((height,)),
            sems, sems,
            sems, sems,
            sems((depth,)), sems((depth,)),
            sems((height,)), sems((height,)),
            sems((2 * depth,)),
            pltpu.VMEM((2,) + projs.shape[2:], BF16),
            pltpu.VMEM(frame, BF16),
            pltpu.VMEM(frame, BF16),
            pltpu.VMEM(frame, BF16),
            sems((2, 3)), sems((2,)),
            pltpu.VMEM((D, 3 * D), BF16),
            sems,
        ],
        compiler_params=pltpu.CompilerParams(
            collective_id=1, has_side_effects=True, vmem_limit_bytes=60 << 20
        ),
        name="reduce_rows",
    )(block.reshape(lead + tail), small.reshape(lead + low), projs, inputs, table, weights, *grads)


def gather(block):
    return lax.all_gather(block, AXES, axis=0, tiled=True)


def scatter(block):
    return lax.psum_scatter(block, AXES, scatter_dimension=0, tiled=True)


def shards(
    clips_in, teacher, valid, norm_gain, norm_shift, w_space, qv_bias, w_space_out, mix_bias,
    w_time, w_time_out, w_up, up_bias, w_down,
):
    batch, frames, places, _ = clips_in.shape
    ring = lax.axis_size("frame")
    pieces = ring // batch
    chunk = places // pieces
    all_frames = ring * frames
    me = lax.axis_index("frame")
    depth = w_up.shape[0]

    def swap(block, step):
        if step == 0:
            return block
        return lax.ppermute(block, "frame", [(i, i ^ step) for i in range(ring)])

    def clip_of(step):
        return (me // pieces) ^ (step // pieces)

    def place_of(step):
        return ((me % pieces) ^ (step % pieces)) * chunk

    def cut(block, step):
        if pieces == 1:
            return block
        return lax.dynamic_slice_in_dim(block, place_of(step), chunk, 0)

    def spread(block):
        got = []
        for step in range(ring):
            mine = lax.dynamic_index_in_dim(block, clip_of(step), 0, keepdims=False)
            got.append(cut(jnp.swapaxes(mine, 0, 1), step))
        return got

    many = FF // D
    count = jnp.sum(valid)
    counts = jnp.stack([count // 256, count % 256]).astype(BF16)
    smalls = jnp.concatenate(
        [
            norm_gain, norm_shift, qv_bias, mix_bias, up_bias.reshape(depth, many),
            jnp.broadcast_to(counts[None], (depth, 2)),
        ],
        1,
    )
    smalls = jnp.pad(smalls, ((0, 0), (0, SMALL - smalls.shape[1])))
    first = gather_rows(jnp.concatenate([w_space, w_space_out, smalls], 1))
    up_turned = jnp.swapaxes(w_up.reshape(depth, D, many), 1, 2).reshape(depth, FF)
    time_weights = gather(jnp.concatenate([w_time, w_time_out], 1))
    to_feed = jnp.concatenate([up_turned, w_down.reshape(depth, FF)], 1)
    table = jnp.swapaxes(first[:, 4 * D : 4 * D + 24].astype(F32), 0, 1)
    up_row = table[UP : UP + many].reshape(1, FF)
    counted = table[UP + many : UP + many + 2, ::depth]
    total_count = jnp.sum(counted[0]) * 256.0 + jnp.sum(counted[1])
    scale = (2.0 / (total_count * D)).reshape(1, 1)
    table = table[:16]

    order = [((me // pieces) ^ j).astype(jnp.int32) for j in range(batch)]
    clip_ids = [jnp.reshape(c, (1,)) for c in order]
    valid_column = [swap(part, step) for step, part in enumerate(spread(valid))]
    valid_column = jnp.concatenate(valid_column, 1).reshape(-1, 1).astype(F32)
    saved, sent, ins = [None] * batch, [None] * ring, None
    near = min(1, batch - 1)
    turns = [j for j in range(batch - 1, -1, -1) if j != near] + [near]
    cuts = spread(teacher)
    for turn, j in enumerate(turns):
        if turn == 3:
            ins, sent[-1], cuts = lax.optimization_barrier((ins, sent[-1], cuts))
        ins, *kept_j, after = space_forward(clip_ids[j], j, clips_in, table, first, ins)
        saved[j] = kept_j
        after = jnp.swapaxes(after, 0, 1)
        if turn == 0:
            after, to_feed = lax.optimization_barrier((after, to_feed))
        if turn == 1:
            cuts, after = lax.optimization_barrier((cuts, after))
        for r in range(pieces):
            step = j * pieces + r
            sent[step] = swap(cut(after, step), step)
    feed_weights = gather(to_feed)
    teachers = [swap(part, step) for step, part in enumerate(cuts)]
    *saved_b, after_b = time_forward(sent, table, time_weights)
    tile, _ = time_tiles(chunk, all_frames)
    layer_parts, grad_b, d_feed, rows_c, bias_up, squares = feed_forward(
        after_b, teachers, valid_column, scale, table, up_row, feed_weights, tile
    )
    d_feed = scatter(d_feed)
    grad_parts, d_both, rows_b = time_back(grad_b, saved_b, sent, table, time_weights)
    grad_parts = [swap(part, step) for step, part in enumerate(grad_parts)]

    def join(parts, j):
        if pieces == 1:
            return parts[j]
        whole = jnp.zeros((places, frames, D), BF16)
        for r in range(pieces):
            step = j * pieces + r
            whole = lax.dynamic_update_slice_in_dim(whole, parts[step], place_of(step), 0)
        return whole

    outs, biases, projs = [], [], None
    grads = [jnp.swapaxes(join(grad_parts, 0), 0, 1)] + [None] * (batch - 1)
    for j in range(batch):
        if j == batch - 1:
            before = space_part(ins, projs)
            projs, *before = lax.optimization_barrier((projs, *before))
        projs, d_out, bias = space_back(grads[j], j, batch, saved[j], first, projs)
        outs.append(d_out)
        biases.append(bias)
        if j == batch - 1:
            projs, layer_parts = lax.optimization_barrier((projs, layer_parts))
            layer_parts = [swap(part, step) for step, part in enumerate(layer_parts)]
        if j + 1 < batch:
            following = join(grad_parts, j + 1)
            if j:
                projs, following = lax.optimization_barrier((projs, following))
            grads[j + 1] = jnp.swapaxes(following, 0, 1)
    d_both, small = space_weights(
        ins, projs, before, first, table, rows_c, rows_b, bias_up.reshape(many, D), squares, outs, biases, d_both
    )
    d_time, d_time_out, d_space, d_space_out, here, input_grad = reduce_rows(
        d_both, small, (3 * D, D, 3 * D, D), projs, grads, clips_in, table, first
    )
    layer_out = place_clips(jnp.stack(order), [join(layer_parts, j) for j in range(batch)])
    d_up = jnp.swapaxes(d_feed[:, :FF].reshape(depth, many, D), 1, 2).reshape(depth, FF)
    return (
        jnp.swapaxes(layer_out, 1, 2),
        here[0, 13 + many] / (total_count * D),
        input_grad,
        here[:, 0:3],
        here[:, 3:6],
        d_space,
        here[:, 6:9],
        here[:, 9],
        d_space_out,
        here[:, 10:13],
        d_time,
        d_time_out,
        d_up.astype(F32),
        here[:, 13 : 13 + many].reshape(-1),
        d_feed[:, FF:].reshape(-1, D).astype(F32),
    )


def solution(mesh):
    tokens, rows = P("clip", "frame", None, None), P(AXES, None)
    in_specs = (tokens, tokens, P("clip", "frame", None)) + (rows,) * 9 + (P(AXES), rows)
    out_specs = (
        (tokens, P(), tokens, rows, rows, rows, rows, P(AXES)) + (rows,) * 5 + (P(AXES), rows)
    )
    return jax.shard_map(shards, mesh=mesh, in_specs=in_specs, out_specs=out_specs, check_vma=False)
```
